32 devices in a mesh: dp: 4 (over y, x), row: 2 (over core), col: 4 (over z).
Axes of the slice: x: 2, y: 2, z: 4, core: 2. Of those that a mesh axis runs over, the one named last changes fastest.
Arguments:
- layer_in: float32 [16, 1024, 768], P(('dp', 'row'), 'col'), may hold values from -6 to 6
- w_qkv: bfloat16 [768, 3, 768], P('row', None, 'col'), may hold values from -0.21875 to 0.21875
- b_qv: float32 [2, 768], P(None, 'col'), may hold values from -1.8 to 1.8
- w_out: bfloat16 [768, 768], P('col', 'row'), may hold values from -0.875 to 0.875
- b_out: float32 [768], replicated, may hold values from -1.8 to 1.8
- ln1_g: float32 [768], replicated, may hold values from 0.1 to 1.9
- ln1_b: float32 [768], replicated, may hold values from -1.8 to 1.8
- ln2_g: float32 [768], replicated, may hold values from 0.1 to 1.9
- ln2_b: float32 [768], replicated, may hold values from -1.8 to 1.8
- w_fc: bfloat16 [768, 3072], P('row', 'col'), may hold values from -0.21875 to 0.21875
- b_fc: float32 [3072], P('col'), may hold values from -1.8 to 1.8
- w_proj: bfloat16 [3072, 768], P('col', 'row'), may hold values from -0.109375 to 0.109375
- b_proj: float32 [768], replicated, may hold values from -1.8 to 1.8
- lengths: int32 [16], P(('dp', 'row')), may hold values from 64 to 1024, as said below
- cotangent: float32 [16, 1024, 768], P(('dp', 'row'), 'col'), may hold values from -6 to 6
Outputs:
- layer_out: float32 [16, 1024, 768], P(('dp', 'row'), 'col')
- grad_input: float32 [16, 1024, 768], P(('dp', 'row'), 'col')
- sample_norms: float32 [16], P(('dp', 'row'))
- grad_w_qkv: float32 [768, 3, 768], P('row', None, 'col')
- grad_b_qv: float32 [2, 768], P(None, 'col')
- grad_w_out: float32 [768, 768], P('col', 'row')
- grad_b_out: float32 [768], replicated
- grad_ln1_g: float32 [768], replicated
- grad_ln1_b: float32 [768], replicated
- grad_ln2_g: float32 [768], replicated
- grad_ln2_b: float32 [768], replicated
- grad_w_fc: float32 [768, 3072], P('row', 'col')
- grad_b_fc: float32 [3072], P('col')
- grad_w_proj: float32 [3072, 768], P('col', 'row')
- grad_b_proj: float32 [768], replicated
The draws below stay inside these ranges and needn't reach their ends.
Inputs may be any that keep to these rules, and one draw needn't show every extreme that they name: `lengths`: among the 2 sequences of each index pair of dp and row (an aligned block of 2 entries), one has more than 768 real tokens; some sequence has all 1024 slots real.
All inputs are finite; a program needn't handle non-finite values.
Results may differ from the reference program's by a relative error of at most 0.015.
Values may be sent and summed in bfloat16 or wider, within the bound.
A program may use at most 192 MiB of HBM per device.

```python
import math
import jax
import jax.numpy as jnp
from jax import lax

D = 768
HEADS = 12
HEAD_DIM = 64
FF = 3072
LEN = 1024
MIN_LEN = 64
SEQ_DEV = 2
SEQS = 16
N_COL = 4


def draw_lengths(key, part):
    key = jax.random.fold_in(key, 7)
    first_key, second_key, third_key, fourth_key = jax.random.split(key, 4)
    groups = SEQS // SEQ_DEV
    raw = jax.random.randint(first_key, (groups, SEQ_DEV), MIN_LEN, LEN + 1)
    chosen = jax.random.randint(second_key, (groups, 1), 0, SEQ_DEV)
    reaching = jax.random.randint(third_key, (groups, 1), LEN - LEN // N_COL + 1, LEN + 1)
    filled = jnp.arange(SEQ_DEV, dtype=jnp.int32)[None, :] == chosen
    result = jnp.where(filled, reaching, raw).reshape(SEQS)
    longest = jax.random.randint(fourth_key, (), 0, SEQS)
    result = jnp.where(jnp.arange(SEQS, dtype=jnp.int32) == longest, LEN, result)
    return result.astype(jnp.int32)


def draw_cotangent(key, part):
    key = jax.random.fold_in(key, 11)
    base_key = jax.random.fold_in(key, 0)
    pick_key = jax.random.fold_in(key, 2)
    base = jnp.clip(jax.random.normal(base_key, (SEQS, LEN, D), jnp.float32), -6.0, 6.0)
    order = jax.random.permutation(pick_key, SEQS)
    quiet = order < max(1, SEQS // 4)
    seq_scale = jnp.where(quiet, 1e-06, 1.0).astype(jnp.float32)
    return base * seq_scale[:, None, None]


def steps_of(key, shape, shards, low, largest):
    factor_of = 1.0
    for dim, parts in shards:
        heights = jax.random.uniform(jax.random.fold_in(jax.random.fold_in(key, 6), dim), (parts,), jnp.float32, low / len(shards), largest / len(shards))
        factor_of = factor_of * jnp.repeat(jnp.exp(heights), shape[dim] // parts).reshape((-1,) + (1,) * (len(shape) - 1 - dim))
    return factor_of


def normal_values(rng, dims, scale, reach, cuts=(), kind=jnp.bfloat16):
    entries = scale * jax.random.normal(rng, dims, jnp.float32)
    if cuts:
        entries = entries * steps_of(rng, dims, cuts, -0.22, 0.18)
    return jnp.clip(entries, -reach, reach).astype(kind)


def setup_inputs(seed: int = 0) -> dict:
    streams_of = jax.random.split(jax.random.key(seed), 16)
    layer_in = normal_values(streams_of[0], (SEQS, LEN, D), 1.0, 6.0, ((0, 8), (1, 4)), jnp.float32)
    w_qkv = normal_values(streams_of[1], (D, 3, D), D ** -0.5, 0.21875, ((0, 2), (2, 4)))
    b_qv = normal_values(streams_of[2], (2, D), 0.3, 1.8, ((1, 4),), jnp.float32)
    w_out = normal_values(streams_of[3], (D, D), (D // 16) ** -0.5, 0.875, ((0, 4), (1, 2)))
    b_out = normal_values(streams_of[4], (D,), 0.3, 1.8, (), jnp.float32)
    ln1_g = jnp.clip(1.0 + 0.18 * jax.random.normal(streams_of[5], (D,), jnp.float32), 0.1, 1.9)
    ln1_b = normal_values(streams_of[6], (D,), 0.3, 1.8, (), jnp.float32)
    ln2_g = jnp.clip(1.0 + 0.18 * jax.random.normal(streams_of[7], (D,), jnp.float32), 0.1, 1.9)
    ln2_b = normal_values(streams_of[8], (D,), 0.3, 1.8, (), jnp.float32)
    w_fc = normal_values(streams_of[9], (D, FF), D ** -0.5, 0.21875, ((0, 2), (1, 4)))
    b_fc = normal_values(streams_of[10], (FF,), 0.3, 1.8, ((0, 4),), jnp.float32)
    w_proj = normal_values(streams_of[11], (FF, D), FF ** -0.5, 0.109375, ((0, 4), (1, 2)))
    b_proj = normal_values(streams_of[12], (D,), 0.3, 1.8, (), jnp.float32)
    lengths = draw_lengths(jax.random.fold_in(streams_of[15], 71), 0)
    cotangent = draw_cotangent(jax.random.fold_in(streams_of[15], 71), 0)
    return {"layer_in": layer_in, "w_qkv": w_qkv, "b_qv": b_qv, "w_out": w_out, "b_out": b_out, "ln1_g": ln1_g, "ln1_b": ln1_b, "ln2_g": ln2_g, "ln2_b": ln2_b, "w_fc": w_fc, "b_fc": b_fc, "w_proj": w_proj, "b_proj": b_proj, "lengths": lengths, "cotangent": cotangent}


HIGHEST = lax.Precision.HIGHEST
EPSILON = 1e-05
CLIP_BOUND = 1.0
GELU_C = 0.7978845608028654
GELU_A = 0.044715
MASKED = -1e+30

@jax.custom_vjp
def low(v):
    return lax.optimization_barrier(v.astype(jnp.bfloat16)).astype(jnp.float32)

@jax.custom_vjp
def low_back(v):
    return v

def low_keep(v):
    return (low(v), None)

def low_pass(kept, grad):
    return (grad,)

def back_keep(v):
    return (v, None)

def back_low(kept, grad):
    return (low(grad),)
low.defvjp(low_keep, low_pass)
low_back.defvjp(back_keep, back_low)

def layer_norm(values, gain, shift):
    center = values - lax.optimization_barrier(jnp.mean(values, axis=-1, keepdims=True))
    spread = lax.optimization_barrier(jnp.mean(center * center, axis=-1, keepdims=True))
    return center * lax.rsqrt(spread + EPSILON) * gain + shift

def gelu_tanh(values):
    return 0.5 * values * (1.0 + jnp.tanh(GELU_C * (values + GELU_A * values * values * values)))

def attend_block(offset, query_rows, key_rows, value_rows, length):
    block_rows = min(512, LEN)
    query_block = lax.dynamic_slice_in_dim(query_rows, offset, block_rows, 0)
    scores = jnp.einsum('qhd,khd->hqk', query_block, key_rows, precision=HIGHEST) * (1.0 / math.sqrt(HEAD_DIM))
    scores = low_back(scores)
    query_place = offset + jnp.arange(block_rows, dtype=jnp.int32)
    key_place = jnp.arange(LEN, dtype=jnp.int32)
    allowed = (key_place[None, :] <= query_place[:, None]) & (key_place[None, :] < length)
    scores = jnp.where(allowed[None], scores, MASKED)
    highest = lax.optimization_barrier(jnp.max(scores, axis=-1, keepdims=True))
    weights = jnp.exp(scores - highest)
    attn_prob = low(weights / lax.optimization_barrier(jnp.sum(weights, axis=-1, keepdims=True)))
    return jnp.einsum('hqk,khd->qhd', attn_prob, value_rows, precision=HIGHEST)

def layer(params, layer_in, length):
    w_qkv, b_qv, w_out, b_out, ln1_g, ln1_b, ln2_g, ln2_b, w_fc, b_fc, w_proj, b_proj = params
    first_in = low(layer_norm(layer_in, ln1_g, ln1_b))
    qkv_rows = jnp.einsum('td,dkf->tkf', first_in, w_qkv, precision=HIGHEST)
    qkv_bias = jnp.stack([b_qv[0], jnp.zeros_like(b_qv[0]), b_qv[1]])
    qkv_rows = low_back(low(qkv_rows + qkv_bias))
    query_rows = qkv_rows[:, 0].reshape(LEN, HEADS, HEAD_DIM)
    key_rows = qkv_rows[:, 1].reshape(LEN, HEADS, HEAD_DIM)
    value_rows = qkv_rows[:, 2].reshape(LEN, HEADS, HEAD_DIM)
    block_rows = min(512, LEN)
    offsets = jnp.arange(LEN // block_rows, dtype=jnp.int32) * block_rows
    blocked = jax.checkpoint(attend_block)
    context = lax.map(lambda offset: blocked(offset, query_rows, key_rows, value_rows, length), offsets)
    context = low_back(low(context.reshape(LEN, D)))
    hidden = layer_in + low_back(jnp.dot(context, w_out, precision=HIGHEST)) + b_out
    second_in = low(layer_norm(hidden, ln2_g, ln2_b))
    fc_pre = low_back(jnp.dot(second_in, w_fc, precision=HIGHEST) + b_fc)
    active = low(gelu_tanh(fc_pre))
    return hidden + low_back(jnp.dot(active, w_proj, precision=HIGHEST)) + b_proj

def reference(layer_in, w_qkv, b_qv, w_out, b_out, ln1_g, ln1_b, ln2_g, ln2_b, w_fc, b_fc, w_proj, b_proj, lengths, cotangent):
    params = tuple((member.astype(jnp.float32) for member in (w_qkv, b_qv, w_out, b_out, ln1_g, ln1_b, ln2_g, ln2_b, w_fc, b_fc, w_proj, b_proj)))

    def one_sequence(totals, element):
        sequence, upstream, length = element
        result, pullback = jax.vjp(lambda weights, inputs: layer(weights, inputs, length), params, sequence.astype(jnp.float32))
        is_real = (jnp.arange(LEN, dtype=jnp.int32) < length).astype(jnp.float32)[:, None]
        weight_grads, input_grad = pullback(upstream.astype(jnp.float32) * is_real)
        squares = sum((jnp.sum(member * member) for member in weight_grads))
        norm_value = jnp.sqrt(squares)
        factor = CLIP_BOUND / jnp.maximum(norm_value, CLIP_BOUND)
        totals = tuple((total + factor * member for total, member in zip(totals, weight_grads)))
        return (totals, (result, input_grad, norm_value))
    starting = tuple((jnp.zeros_like(member) for member in params))
    totals, outputs = lax.scan(one_sequence, starting, (layer_in, cotangent, lengths))
    layer_out, grad_input, sample_norms = outputs
    return (layer_out, grad_input, sample_norms, totals[0], totals[1], totals[2], totals[3], totals[4], totals[5], totals[6], totals[7], totals[8], totals[9], totals[10], totals[11])
```

```python
import functools

import jax
import jax.numpy as jnp
from jax import lax
from jax.experimental import pallas as pl
from jax.experimental.pallas import tpu as pltpu
from jax.sharding import PartitionSpec as P

MESH = pl.DeviceIdType.MESH
EPSILON = 1e-05
CLIP_BOUND = 1.0
GELU_C = 0.7978845608028654
GELU_A = 0.044715
MASKED = -1e30
HEAD_DIM = 64
QUAD = 4
BF = jnp.bfloat16
F32 = jnp.float32

V_BOUT, V_LN1G, V_LN1B, V_LN2G, V_LN2B, V_BPROJ, V_BQV, V_BFC, V_SQ = 0, 1, 2, 3, 4, 5, 6, 7, 9
V_FACTOR, V_NORM = 12, 13


def dot(a, b):
    return lax.dot_general(a, b, (((1,), (0,)), ((), ())), preferred_element_type=F32)


def dot_t(a, b):
    return lax.dot_general(a, b, (((1,), (1,)), ((), ())), preferred_element_type=F32)


def t_dot(a, b):
    return lax.dot_general(a, b, (((0,), (0,)), ((), ())), preferred_element_type=F32)


def fold8(v):
    return jnp.sum(v.reshape(v.shape[0] // 8, 8, v.shape[1]), axis=0)


def norm_stats(v):
    center = v - jnp.mean(v, axis=-1, keepdims=True)
    inverse = lax.rsqrt(jnp.mean(center * center, axis=-1, keepdims=True) + EPSILON)
    return center * inverse, inverse


def kernel(
    x_in, cot_in, wq_in, wo_in, wf_in, wp_in, misc_in, vec_in,
    lo_out, gi_out, gq_out, go_out, gf_out, gp_out, vec_out, norm_out,
    XR, H, A1, WQ, WO, WF, WP, MISC, QKV, CTX, LSE, KB, ACC,
    PS, PR, A2, M, SL, GF, GA, GCTX, GQKV, DK, DV, LO, GI,
    V8, SQ, VF, VK, VP, VZ,
    GWQ, GWO, GWF, GWP, RQ, RO, RF, RP, SQW, SOW, SFW, SPW, ZQ, ZO, ZF, ZP, EQ, EO, EF, EP,
    ss, rs,
):
    d, row, z = lax.axis_index("dp"), lax.axis_index("row"), lax.axis_index("col")
    k = lax.rem(row, 2)
    dq = d

    def at(plane, core, place):
        return (plane, row - k + core, place)

    zk, zs = z // 2, lax.rem(z, 2)
    L, D = A1.shape
    T = XR.shape[1]
    HC = CTX.shape[1]
    FH = M.shape[1]
    QR, OR_, FR, PR_ = wq_in.shape[1], wo_in.shape[0], wf_in.shape[0], wp_in.shape[0]
    DH = wo_in.shape[1]
    own, other = k * 2 * T, (1 - k) * 2 * T

    def mo(v, n):
        return pl.multiple_of(v, n)

    def when(cond, f):
        if cond is True:
            f()
        else:
            pl.when(cond)(f)

    n_send = [0]
    n_recv = [0]
    pending = []

    def new_send():
        n_send[0] += 1
        assert n_send[0] <= ss.shape[0]
        return ss.at[n_send[0] - 1]

    def new_recv(n):
        n_recv[0] += n
        assert n_recv[0] <= rs.shape[0]
        return n_recv[0] - n

    def send(src, dst, rsem, dev, cond=True):
        sem = new_send()

        def make():
            return pltpu.make_async_remote_copy(
                src(), dst(), sem, rs.at[rsem], device_id=dev, device_id_type=MESH
            )

        when(cond, lambda: make().start())
        pending.append((cond, make))

    def local(src, dst, rsem, cond=True):
        when(cond, lambda: pltpu.make_async_copy(src(), dst(), rs.at[rsem]).start())

    def arrive(dst, rsem, cond=True):
        def f():
            pltpu.make_async_remote_copy(
                dst(), dst(), ss.at[0], rs.at[rsem], device_id=at(d, k, z), device_id_type=MESH
            ).wait_recv()

        when(cond, f)

    def arrive_local(dst, rsem, cond=True):
        when(cond, lambda: pltpu.make_async_copy(dst(), dst(), rs.at[rsem]).wait())

    mate = at(d, 1 - k, z)
    quad = [at(d ^ j, k, z) for j in (1, 2, 3)]

    barrier = pltpu.get_barrier_semaphore()
    line = [at(d, k, z ^ j) for j in (1, 2, 3)] + [at(d, 1 - k, z ^ j) for j in (0, 1, 2, 3)]
    for dev in quad + line:
        pl.semaphore_signal(barrier, inc=1, device_id=dev, device_id_type=MESH)
    pl.semaphore_wait(barrier, len(quad) + len(line))

    def line_send(src, dst):
        base = new_recv(2)
        for i in range(2):
            mine = (zk == k) & (2 * k + i == z)
            send(lambda i=i: src(i), lambda: dst(zs), base + zs, at(d, zk, 2 * k + i), jnp.logical_not(mine))
            local(lambda i=i: src(i), lambda: dst(zs), base + zs, mine)
        return base

    def line_wait(dst, base, i):
        mine = (zk == k) & (2 * k + i == z)
        arrive(lambda: dst(i), base + i, jnp.logical_not(mine))
        arrive_local(lambda: dst(i), base + i, mine)

    class Weight:
        def __init__(self, src, src_quarter, piece, full, slab):
            self.src, self.src_quarter, self.piece, self.full, self.slab = src, src_quarter, piece, full, slab
            self.zsem, self.xsem = new_recv(4), new_recv(6)

        def push(self):
            sem = self.zsem + zs * 2 + k
            for j in (1, 2, 3):
                send(self.src_quarter, lambda: self.piece(zs, k, dq), sem, at(d, zk, z ^ j))
            send(lambda: self.src, lambda: self.full(zs, k), sem, mate, zk != k)
            local(lambda: self.src, lambda: self.full(zs, k), sem, zk == k)

        def forward(self):
            for cs in range(2):
                c = 2 * k + cs
                for r in range(2):
                    sem = self.zsem + cs * 2 + r
                    arrive(lambda: self.piece(cs, r, dq), sem, c != z)
                    arrive(lambda: self.full(cs, r), sem, (c == z) & (k != r))
                    arrive_local(lambda: self.full(cs, r), sem, (c == z) & (k == r))
                for j in (1, 2, 3):
                    send(
                        lambda cs=cs: self.slab(cs, dq),
                        lambda cs=cs: self.slab(cs, dq),
                        self.xsem + cs * 3 + j - 1,
                        quad[j - 1],
                        c != z,
                    )

        def ready(self):
            for cs in range(2):
                for j in (1, 2, 3):
                    arrive(lambda: self.slab(cs, dq ^ j), self.xsem + cs * 3 + j - 1, 2 * k + cs != z)

    q48, o48, f96, p192 = QR // QUAD, OR_ // QUAD, FR // QUAD, PR_ // QUAD

    def cols(r):
        return pl.ds(mo(r * DH, 128), DH)

    w_qkv = Weight(
        wq_in,
        lambda: wq_in.at[:, pl.ds(mo(dq * q48, 16), q48), :],
        lambda cs, r, q: WQ.at[:, pl.ds(mo(cs * QR + q * q48, 16), q48), cols(r)],
        lambda cs, r: WQ.at[:, pl.ds(mo(cs * QR, 16), QR), cols(r)],
        lambda cs, q: WQ.at[:, pl.ds(mo(cs * QR + q * q48, 16), q48), :],
    )
    w_out = Weight(
        wo_in,
        lambda: wo_in.at[pl.ds(mo(dq * o48, 16), o48), :],
        lambda cs, r, q: WO.at[pl.ds(mo(cs * OR_ + q * o48, 16), o48), cols(r)],
        lambda cs, r: WO.at[pl.ds(mo(cs * OR_, 16), OR_), cols(r)],
        lambda cs, q: WO.at[pl.ds(mo(cs * OR_ + q * o48, 16), o48), :],
    )
    FC = wf_in.shape[1]
    w_fc = Weight(
        wf_in,
        lambda: wf_in.at[pl.ds(mo(dq * f96, 16), f96), :],
        lambda cs, r, q: WF.at[r, pl.ds(mo(q * f96, 16), f96), pl.ds(mo(cs * FC, 128), FC)],
        lambda cs, r: WF.at[r, :, pl.ds(mo(cs * FC, 128), FC)],
        lambda cs, q: WF.at[:, pl.ds(mo(q * f96, 16), f96), pl.ds(mo(cs * FC, 128), FC)],
    )
    w_proj = Weight(
        wp_in,
        lambda: wp_in.at[pl.ds(mo(dq * p192, 16), p192), :],
        lambda cs, r, q: WP.at[pl.ds(mo(cs * PR_ + q * p192, 16), p192), cols(r)],
        lambda cs, r: WP.at[pl.ds(mo(cs * PR_, 16), PR_), cols(r)],
        lambda cs, q: WP.at[pl.ds(mo(cs * PR_ + q * p192, 16), p192), :],
    )

    misc_sem = new_recv(8)
    for dev in line:
        send(lambda: misc_in, lambda: MISC.at[k, z], misc_sem + k * 4 + z, dev)
    local(lambda: misc_in, lambda: MISC.at[k, z], misc_sem + k * 4 + z)
    w_qkv.push()
    x_sem = line_send(lambda i: x_in.at[i], lambda i: XR.at[i])

    V8[...] = jnp.zeros_like(V8)
    SQ[...] = jnp.zeros_like(SQ)

    vec = lambda i: vec_in[i : i + 1, :]
    b_out, ln1_g, ln1_b, ln2_g, ln2_b, b_proj = (vec(i) for i in range(6))

    w_qkv.forward()

    RB = 32
    a1_sem = new_recv(2)

    def rows_of(base, i, n):
        return pl.ds(mo(base + i * n, 16), n)

    for s in range(2):
        line_wait(lambda i: XR.at[i], x_sem, s)

        def first_norm(i, c):
            scaled, _ = norm_stats(XR[s, rows_of(0, i, RB), :].astype(F32))
            A1[rows_of(own + s * T, i, RB), :] = (scaled * ln1_g + ln1_b).astype(BF)
            return c

        lax.fori_loop(0, T // RB, first_norm, 0)
        mine = lambda s=s: A1.at[pl.ds(mo(own + s * T, 16), T), :]
        send(mine, mine, a1_sem + s, mate)

    w_out.push()
    w_fc.push()
    w_proj.push()

    for r in range(2):
        for c in range(4):
            here = (k == r) & (z == c)
            arrive(lambda: MISC.at[r, c], misc_sem + r * 4 + c, jnp.logical_not(here))
            arrive_local(lambda: MISC.at[r, c], misc_sem + r * 4 + c, here)
    pair_misc = MISC[0, 2 * k] + MISC[0, 2 * k + 1]
    bias_q, bias_v = pair_misc[1:2, :HC], pair_misc[1:2, HC:]
    length = MISC[zk, 0, pl.ds(2 + zs, 1), :][:, 0:1]

    w_qkv.ready()

    def project(i, c):
        rows = rows_of(0, lax.rem(2 * k + i, 4), T)
        a = A1[rows, :]
        QKV[0, rows, :] = ((dot_t(a, WQ[0]) + bias_q).astype(BF).astype(F32) * (HEAD_DIM**-0.5)).astype(BF)
        QKV[1, rows, :] = dot_t(a, WQ[1]).astype(BF)
        QKV[2, rows, :] = (dot_t(a, WQ[2]) + bias_v).astype(BF)
        return c

    lax.fori_loop(0, 2, project, 0)
    for s in range(2):
        arrive(lambda: A1.at[pl.ds(mo(other + s * T, 16), T), :], a1_sem + s)
    lax.fori_loop(2, 4, project, 0)

    key_place = lax.broadcasted_iota(jnp.int32, (L, 128), 0).astype(F32)
    KB[...] = jnp.where(key_place < length, 0.0, MASKED)

    QB = T
    NQ = L // QB
    low_lane = lax.broadcasted_iota(jnp.int32, (1, 128), 1) < HEAD_DIM
    low_row = lax.broadcasted_iota(jnp.int32, (128, 1), 0) < HEAD_DIM
    diag = lax.broadcasted_iota(jnp.int32, (QB, QB), 0) <= lax.broadcasted_iota(jnp.int32, (QB, QB), 1)

    def keep_lane(v, h):
        return jnp.where(low_lane if h == 0 else jnp.logical_not(low_lane), v, jnp.zeros_like(v))

    def scores_t(kp, qm, qb):
        kv = (qb + 1) * QB
        s = dot_t(kp[:kv], qm)
        kb = KB[0:kv, :]
        s = s + jnp.concatenate([kb] * (QB // 128), axis=1)
        last = jnp.where(diag, s[kv - QB :], MASKED)
        if qb == 0:
            return last
        return jnp.concatenate([s[: kv - QB], last], axis=0)

    def attend(p):
        lanes = pl.ds(p * 128, 128)
        kp, vp = QKV[1, :, lanes], QKV[2, :, lanes]
        vt = vp.T
        for qb in range(NQ):
            kv = (qb + 1) * QB
            qp = QKV[0, qb * QB : kv, lanes]
            parts = []
            for h in range(2):
                s = scores_t(kp, keep_lane(qp, h), qb)
                top = jnp.max(s, axis=0, keepdims=True)
                e = jnp.exp(s - top)
                total = jnp.sum(e, axis=0, keepdims=True)
                LSE[pl.ds(2 * p + h, 1), qb * QB : kv] = top + jnp.log(total)
                parts.append(dot(vt[:, :kv], e.astype(BF)) / total)
            CTX[qb * QB : kv, lanes] = jnp.where(low_row, parts[0], parts[1]).T.astype(BF)

    attend(0)
    w_out.forward()
    w_fc.forward()
    attend(1)
    w_proj.forward()
    cot_sem = line_send(lambda i: cot_in.at[i], lambda i: GF.at[pl.ds(mo(z * T, 16), T), :])
    attend(2)

    def split_sum(n, product, sums=None):
        base = new_recv(2)
        for s in range(2):
            PS[n, s] = product(pl.ds(mo(other + s * T, 16), T)).astype(BF)
            send(lambda s=s: PS.at[n, s], lambda s=s: PR.at[n, s], base + s, mate)

        def keep(s, c):
            ACC[s] = product(pl.ds(mo(own + s * T, 16), T))
            return c

        lax.fori_loop(0, 2, keep, 0)
        return base

    def split_wait(n, base, s):
        arrive(lambda: PR.at[n, s], base + s)

    w_out.ready()
    ex = split_sum(0, lambda rows: dot(CTX[rows, :], WO[...]))
    a2_sem = new_recv(2)
    for s in range(2):
        split_wait(0, ex, s)

        def second_norm(i, c):
            rows = rows_of(0, i, RB)
            h = XR[s, rows, :].astype(F32) + ACC[s, rows, :] + PR[0, s, rows, :].astype(F32) + b_out
            H[s, rows, :] = h
            scaled, _ = norm_stats(h)
            A2[rows_of(own + s * T, i, RB), :] = (scaled * ln2_g + ln2_b).astype(BF)
            return c

        lax.fori_loop(0, T // RB, second_norm, 0)
        mine = lambda s=s: A2.at[pl.ds(mo(own + s * T, 16), T), :]
        send(mine, mine, a2_sem + s, mate)

    NB = 512
    NN = FH // NB
    w_fc.ready()
    WFv = lambda cs: WF[:, :, cs].reshape(D, NB)

    def hidden(i, c):
        rows = rows_of(0, lax.rem(2 * k + i // NN, 4), T)
        n = lax.rem(i, NN)
        cs = pl.ds(mo(n * NB, 128), NB)
        bias = jnp.concatenate([MISC[0, 2 * k, 0:1, :], MISC[0, 2 * k + 1, 0:1, :]], axis=1)
        VF[...] = bias
        u = dot(A2[rows, :], WFv(cs)) + VF[:, cs]
        t = jnp.tanh(GELU_C * (u + GELU_A * u * u * u))
        M[rows, cs] = (0.5 * u * (1.0 + t)).astype(BF)
        SL[rows, cs] = (
            0.5 * (1.0 + t) + 0.5 * u * (1.0 - t * t) * GELU_C * (1.0 + 3.0 * GELU_A * u * u)
        ).astype(BF)
        return c

    lax.fori_loop(0, 2 * NN, hidden, 0)
    for s in range(2):
        arrive(lambda: A2.at[pl.ds(mo(other + s * T, 16), T), :], a2_sem + s)
    lax.fori_loop(2 * NN, 4 * NN, hidden, 0)
    w_proj.ready()
    ex = split_sum(1, lambda rows: dot(M[rows, :], WP[...]))

    gf_sem = new_recv(2)
    for s in range(2):
        line_wait(lambda i: GF.at[pl.ds(mo(own + i * T, 16), T), :], cot_sem, s)

        def mask_rows(i, c):
            rows = rows_of(own + s * T, i, RB)
            place = (lax.broadcasted_iota(jnp.int32, (RB, 1), 0) + (own + s * T + i * RB)).astype(F32)
            g = jnp.where(place < length, GF[rows, :].astype(F32), 0.0)
            GF[rows, :] = g.astype(BF)
            V8[V_BPROJ] += fold8(g)
            return c

        lax.fori_loop(0, T // RB, mask_rows, 0)
        mine = lambda s=s: GF.at[pl.ds(mo(own + s * T, 16), T), :]
        send(mine, mine, gf_sem + s, mate)

    for s in range(2):
        split_wait(1, ex, s)

        def output_rows(i, c):
            rows = rows_of(0, i, RB)
            LO[s, rows, :] = (H[s, rows, :] + ACC[s, rows, :] + PR[1, s, rows, :].astype(F32) + b_proj).astype(BF)
            return c

        lax.fori_loop(0, T // RB, output_rows, 0)
    lo_sem = line_send(lambda i: LO.at[i], lambda i: lo_out.at[i])

    for s in range(2):
        arrive(lambda: GF.at[pl.ds(mo(other + s * T, 16), T), :], gf_sem + s)

    def spread(quarter, land):
        base = new_recv(3)
        for j in (1, 2, 3):
            send(lambda j=j: quarter(dq ^ j), lambda j=j: land(j - 1), base + j - 1, quad[j - 1])
        return base

    def grad_proj(i, c):
        cs = pl.ds(mo(i * 256, 128), 256)
        g = t_dot(M[:, cs], GF[...])
        SQ[...] += fold8(g * g)
        GWP[i // 3, pl.ds(mo(lax.rem(i, 3) * 256, 16), 256), :] = g.astype(BF)
        return c

    lax.fori_loop(0, FH // 256, grad_proj, 0)
    p_quarter = lambda q: GWP.at[:, pl.ds(mo(q * p192, 16), p192), :]
    p_sem = spread(p_quarter, lambda j: RP.at[j])

    def grad_hidden(i, c):
        rows = rows_of(0, i // NN, T)
        cs = pl.ds(mo(lax.rem(i, NN) * NB, 128), NB)
        g = dot_t(GF[rows, :], WP[cs, :]) * SL[rows, cs].astype(F32)
        low = g.astype(BF)
        SL[rows, cs] = low
        VF[:, cs] = jnp.where(i < NN, 0.0, VF[:, cs]) + jnp.sum(low.astype(F32), axis=0, keepdims=True)
        return c

    lax.fori_loop(0, 4 * NN, grad_hidden, 0)
    ex = split_sum(2, lambda rows: dot_t(SL[rows, :], WF[...].reshape(D, FH)))

    def grad_fc(i, c):
        cs = pl.ds(mo(i * 128, 128), 128)
        g = t_dot(A2[:, cs], SL[...])
        q = fold8(g * g)
        SQ[...] += q[:, :D] + q[:, D:]
        GWF[i // 3, pl.ds(mo(lax.rem(i, 3) * 128, 16), 128), :] = g.astype(BF)
        return c

    lax.fori_loop(0, D // 128, grad_fc, 0)
    f_quarter = lambda q: GWF.at[:, pl.ds(mo(q * f96, 16), f96), :]
    f_sem = spread(f_quarter, lambda j: RF.at[j])

    ga_sem = new_recv(2)
    for s in range(2):
        split_wait(2, ex, s)

        def second_back(i, c):
            rows = rows_of(0, i, RB)
            full = rows_of(own + s * T, i, RB)
            up = ACC[s, rows, :] + PR[2, s, rows, :].astype(F32)
            scaled, inverse = norm_stats(H[s, rows, :])
            through = up * ln2_g
            V8[V_LN2G] += fold8(up * scaled)
            V8[V_LN2B] += fold8(up)
            g = GF[full, :].astype(F32) + inverse * (
                through
                - jnp.mean(through, axis=-1, keepdims=True)
                - scaled * jnp.mean(through * scaled, axis=-1, keepdims=True)
            )
            V8[V_BOUT] += fold8(g)
            H[s, rows, :] = g
            GA[full, :] = g.astype(BF)
            return c

        lax.fori_loop(0, T // RB, second_back, 0)
        mine = lambda s=s: GA.at[pl.ds(mo(own + s * T, 16), T), :]
        send(mine, mine, ga_sem + s, mate)
    for s in range(2):
        arrive(lambda: GA.at[pl.ds(mo(other + s * T, 16), T), :], ga_sem + s)

    def grad_context(i, c):
        rows = rows_of(0, i, T)
        GCTX[rows, :] = dot_t(GA[rows, :], WO[...]).astype(BF)
        return c

    lax.fori_loop(0, 4, grad_context, 0)
    half = HC // 2
    for cs in range(HC // 128):
        g = t_dot(CTX[:, cs * 128 : (cs + 1) * 128], GA[...])
        SQ[...] += fold8(g * g)
        low = g.astype(BF)
        lo_row = cs * 128
        if lo_row + 128 <= half:
            GWO[0, lo_row : lo_row + 128, :] = low
        elif lo_row >= half:
            GWO[1, lo_row - half : lo_row - half + 128, :] = low
        else:
            GWO[0, lo_row:half, :] = low[: half - lo_row]
            GWO[1, : lo_row + 128 - half, :] = low[half - lo_row :]
    o_quarter = lambda q: GWO.at[:, pl.ds(mo(q * o48, 16), o48), :]
    o_sem = spread(o_quarter, lambda j: RO.at[j])

    def attend_back(p):
        lanes = pl.ds(p * 128, 128)
        kp, vp = QKV[1, :, lanes], QKV[2, :, lanes]
        kt = kp.T
        DK[...] = jnp.zeros_like(DK)
        DV[...] = jnp.zeros_like(DV)
        for qb in range(NQ):
            kv = (qb + 1) * QB
            qp = QKV[0, qb * QB : kv, lanes]
            do = GCTX[qb * QB : kv, lanes]
            dqt = []
            for h in range(2):
                qm, dm = keep_lane(qp, h), keep_lane(do, h)
                pt = jnp.exp(scores_t(kp, qm, qb) - LSE[pl.ds(2 * p + h, 1), qb * QB : kv])
                gp = dot_t(vp[:kv], dm)
                both = pt * gp
                gs = (both - pt * jnp.sum(both, axis=0, keepdims=True)).astype(BF)
                DV[0:kv, :] += dot(pt.astype(BF), dm)
                DK[0:kv, :] += dot(gs, qm)
                dqt.append(dot(kt[:, :kv], gs))
            GQKV[0, qb * QB : kv, lanes] = (
                jnp.where(low_row, dqt[0], dqt[1]).T * (HEAD_DIM**-0.5)
            ).astype(BF)
        GQKV[1, :, lanes] = DK[...].astype(BF)
        GQKV[2, :, lanes] = DV[...].astype(BF)

    for p in range(HC // 128):
        attend_back(p)

    def grad_norm_in(rows):
        return dot(GQKV[0, rows, :], WQ[0]) + dot(GQKV[1, rows, :], WQ[1]) + dot(GQKV[2, rows, :], WQ[2])

    ex = split_sum(3, grad_norm_in)
    for i in range(3):
        g = t_dot(GQKV[i], A1[...])
        SQ[...] += fold8(g * g)
        low = g.astype(BF)
        GWQ[i, 0] = low[:half]
        GWQ[i, 1] = low[half:]
    q_quarter = lambda q: GWQ.at[:, :, pl.ds(mo(q * q48, 16), q48), :]
    q_sem = spread(q_quarter, lambda j: RQ.at[j])

    for s in range(2):
        split_wait(3, ex, s)

        def first_back(i, c):
            rows = rows_of(0, i, RB)
            up = ACC[s, rows, :] + PR[3, s, rows, :].astype(F32)
            scaled, inverse = norm_stats(XR[s, rows, :].astype(F32))
            through = up * ln1_g
            V8[V_LN1G] += fold8(up * scaled)
            V8[V_LN1B] += fold8(up)
            g = H[s, rows, :] + inverse * (
                through
                - jnp.mean(through, axis=-1, keepdims=True)
                - scaled * jnp.mean(through * scaled, axis=-1, keepdims=True)
            )
            GI[s, rows, :] = g.astype(BF)
            return c

        lax.fori_loop(0, T // RB, first_back, 0)

    VK[k] = jnp.zeros(VK.shape[1:], F32)
    for i in range(6):
        VK[k, i : i + 1, :] = jnp.sum(V8[i], axis=0, keepdims=True)
    VK[k, V_BQV : V_BQV + 1, :] = jnp.concatenate(
        [jnp.sum(GQKV[i].astype(F32), axis=0, keepdims=True) for i in (0, 2)], axis=1
    )
    VK[k, V_BFC : V_BFC + 1, :] = VF[:, :D]
    VK[k, V_BFC + 1 : V_BFC + 2, :] = VF[:, D:]
    VK[k, V_SQ : V_SQ + 1, :] = jnp.sum(SQ[...], axis=0, keepdims=True)
    vk_sem = new_recv(1)
    send(lambda: VK.at[k], lambda: VK.at[k], vk_sem, mate)
    arrive(lambda: VK.at[1 - k], vk_sem)
    va, vb = VK[0], VK[1]
    pack = jnp.concatenate([va[0:6] + vb[0:6], va[6:9], vb[6:9]], axis=0)
    squares = jnp.sum(jnp.sum(pack * pack, axis=0, keepdims=True) + va[9:10] + vb[9:10], axis=1, keepdims=True)
    norm = jnp.sqrt(squares)
    factor = CLIP_BOUND / jnp.maximum(norm, CLIP_BOUND)
    wide = lambda v: jnp.broadcast_to(v, (1, D))
    VP[dq] = jnp.concatenate([pack, wide(factor), wide(norm), jnp.zeros((2, D), F32)], axis=0)
    vp_sem = new_recv(3)
    for j in (1, 2, 3):
        send(lambda: VP.at[dq], lambda: VP.at[dq], vp_sem + j - 1, quad[j - 1])

    gi_sem = line_send(lambda i: GI.at[i], lambda i: gi_out.at[i])
    for j in (1, 2, 3):
        arrive(lambda: VP.at[dq ^ j], vp_sem + j - 1)

    total = jnp.zeros((12, D), F32)
    for q in range(QUAD):
        total = total + VP[q, 0:12, :] * VP[q, V_FACTOR : V_FACTOR + 1, :]
    VZ[z] = jnp.concatenate([total, VP[dq, V_FACTOR:, :]], axis=0)
    vz_sem = new_recv(3)
    for j in (1, 2, 3):
        send(lambda: VZ.at[z], lambda: VZ.at[z], vz_sem + j - 1, at(d, k, z ^ j))

    def reduce_plane(base, quarter, land, S, to, ZR, piece):
        for j in (1, 2, 3):
            arrive(lambda: land(j - 1), base + j - 1)
        to()
        zsem = new_recv(4)
        for cs in range(2):
            for r in range(2):
                mine = (r == k) & (2 * k + cs == z)
                send(
                    lambda cs=cs, r=r: piece(cs, r), lambda: ZR.at[z], zsem + z,
                    at(d, r, 2 * k + cs), jnp.logical_not(mine),
                )
                local(lambda cs=cs, r=r: piece(cs, r), lambda: ZR.at[z], zsem + z, mine)
        return zsem

    def fac(q):
        return VP[q, V_FACTOR : V_FACTOR + 1, :]

    def wide_fac(q, width):
        f = fac(q)
        return f[:, :width] if width <= D else jnp.concatenate([f] * (width // D), axis=1)

    def combine2(G, quarter_rows, n, R, S):
        def to():
            for a in range(2):
                v = G[a, pl.ds(mo(dq * n, 16), n), :].astype(F32) * wide_fac(dq, S.shape[-1])
                for j in (1, 2, 3):
                    v = v + R[j - 1, a].astype(F32) * wide_fac(dq ^ j, S.shape[-1])
                S[a] = v.astype(BF)

        return to

    def combine_q():
        for i in range(3):
            for a in range(2):
                v = GWQ[i, a, pl.ds(mo(dq * q48, 16), q48), :].astype(F32) * fac(dq)
                for j in (1, 2, 3):
                    v = v + RQ[j - 1, i, a].astype(F32) * fac(dq ^ j)
                SQW[i, a] = v.astype(BF)

    zp = reduce_plane(
        p_sem, None, lambda j: RP.at[j], SPW, combine2(GWP, None, p192, RP, SPW), ZP,
        lambda cs, r: SPW.at[cs, :, cols(r)],
    )
    zf = reduce_plane(
        f_sem, None, lambda j: RF.at[j], SFW, combine2(GWF, None, f96, RF, SFW), ZF,
        lambda cs, r: SFW.at[r, :, pl.ds(mo(cs * FC, 128), FC)],
    )
    zo = reduce_plane(
        o_sem, None, lambda j: RO.at[j], SOW, combine2(GWO, None, o48, RO, SOW), ZO,
        lambda cs, r: SOW.at[cs, :, cols(r)],
    )
    zq = reduce_plane(
        q_sem, None, lambda j: RQ.at[j], SQW, combine_q, ZQ,
        lambda cs, r: SQW.at[:, cs, :, cols(r)],
    )

    def finish(zsem, ZR, E, place):
        for c in range(4):
            here = (zk == k) & (z == c)
            arrive(lambda: ZR.at[c], zsem + c, jnp.logical_not(here))
            arrive_local(lambda: ZR.at[c], zsem + c, here)
        E[...] = (
            ZR[0].astype(F32) + ZR[1].astype(F32) + ZR[2].astype(F32) + ZR[3].astype(F32)
        ).astype(BF)
        base = new_recv(4)
        for j in (1, 2, 3):
            send(lambda: E, lambda: place(dq), base + j, quad[j - 1])
        local(lambda: E, lambda: place(dq), base)
        return base, E, place

    ends = [
        finish(zp, ZP, EP, lambda q: gp_out.at[pl.ds(mo(q * p192, 16), p192), :]),
        finish(zf, ZF, EF, lambda q: gf_out.at[pl.ds(mo(q * f96, 16), f96), :]),
        finish(zo, ZO, EO, lambda q: go_out.at[pl.ds(mo(q * o48, 16), o48), :]),
        finish(zq, ZQ, EQ, lambda q: gq_out.at[:, pl.ds(mo(q * q48, 16), q48), :]),
    ]

    for j in (1, 2, 3):
        arrive(lambda: VZ.at[z ^ j], vz_sem + j - 1)
    vec_out[...] = (VZ[0] + VZ[1] + VZ[2] + VZ[3])[0:12]
    for c in range(4):
        norm_out[c : c + 1, :] = VZ[c, V_NORM : V_NORM + 1, 0:128]

    for base, E, place in ends:
        arrive_local(lambda: place(dq), base)
        for j in (1, 2, 3):
            arrive(lambda: place(dq ^ j), base + j)
    for i in range(2):
        line_wait(lambda i: lo_out.at[i], lo_sem, i)
        line_wait(lambda i: gi_out.at[i], gi_sem, i)
    for cond, make in pending:
        when(cond, lambda: make().wait_send())


def shards(
    layer_in, w_qkv, b_qv, w_out, b_out, ln1_g, ln1_b, ln2_g, ln2_b, w_fc, b_fc, w_proj, b_proj, lengths, cotangent
):
    E, T, D = layer_in.shape
    n_col, n_row = lax.axis_size("col"), lax.axis_size("row")
    assert lax.axis_size("dp") == QUAD and n_col == 4 and n_row % 2 == 0
    pairs = n_row // 2
    r = lax.axis_index("row")
    core = lax.rem(r, 2)
    half_rows = w_fc.shape[0] * pairs

    def halves(w, axis):
        if pairs == 1:
            return w
        whole = lax.all_gather(w, "row", axis=axis, tiled=True)
        return lax.dynamic_slice_in_dim(whole, core * half_rows, half_rows, axis)

    w_qkv, w_out, w_fc, w_proj = halves(w_qkv, 0), halves(w_out, 1), halves(w_fc, 0), halves(w_proj, 1)
    L = T * n_col
    HQ = w_qkv.shape[2]
    HC = HQ * n_col // 2
    FQ = w_fc.shape[1]
    FH = FQ * n_col // 2
    DH = w_fc.shape[0]
    c = lax.axis_index("col")

    zero = jnp.zeros_like(b_qv)
    even = lax.rem(c, 2) == 0
    both = jnp.where(
        even, jnp.concatenate([b_qv, zero], axis=1), jnp.concatenate([zero, b_qv], axis=1)
    ).reshape(1, 2 * HC)
    misc = jnp.concatenate(
        [
            b_fc[None, :],
            both,
            jnp.broadcast_to(lengths.astype(F32)[:, None], (E, D)),
            jnp.zeros((4, D), F32),
        ],
        axis=0,
    )
    vecs = jnp.stack([b_out, ln1_g, ln1_b, ln2_g, ln2_b, b_proj, b_proj, b_proj])
    wq_t = jnp.transpose(w_qkv, (1, 2, 0))
    q48, o48, f96, p192 = HQ // QUAD, HQ // QUAD, DH // QUAD, FQ // QUAD

    anyspec = pl.BlockSpec(memory_space=pl.ANY)
    vm = pl.BlockSpec(memory_space=pltpu.VMEM)
    V = pltpu.VMEM
    outs = pl.pallas_call(
        kernel,
        name="layer",
        out_shape=(
            jax.ShapeDtypeStruct((E, T, D), BF),
            jax.ShapeDtypeStruct((E, T, D), BF),
            jax.ShapeDtypeStruct((3, HQ, DH), BF),
            jax.ShapeDtypeStruct((HQ, DH), BF),
            jax.ShapeDtypeStruct((DH, FQ), BF),
            jax.ShapeDtypeStruct((FQ, DH), BF),
            jax.ShapeDtypeStruct((12, D), F32),
            jax.ShapeDtypeStruct((8, 128), F32),
        ),
        in_specs=[anyspec] * 7 + [vm],
        out_specs=(anyspec,) * 6 + (vm, vm),
        scratch_shapes=[
            V((2, T, D), BF),
            V((2, T, D), F32),
            V((L, D), BF),
            V((3, HC, D), BF),
            V((HC, D), BF),
            V((2, DH, FH), BF),
            V((FH, D), BF),
            V((2, n_col, 8, D), F32),
            V((3, L, HC), BF),
            V((L, HC), BF),
            V((8, L), F32),
            V((L, 128), F32),
            V((2, T, D), F32),
            V((4, 2, T, D), BF),
            V((4, 2, T, D), BF),
            V((L, D), BF),
            V((L, FH), BF),
            V((L, FH), BF),
            V((L, D), BF),
            V((L, D), BF),
            V((L, HC), BF),
            V((3, L, HC), BF),
            V((L, 128), F32),
            V((L, 128), F32),
            V((2, T, D), BF),
            V((2, T, D), BF),
            V((6, 8, D), F32),
            V((8, D), F32),
            V((1, FH), F32),
            V((2, 16, D), F32),
            V((QUAD, 16, D), F32),
            V((n_col, 16, D), F32),
            V((3, 2, HQ, D), BF),
            V((2, HQ, D), BF),
            V((2, DH, FH), BF),
            V((2, FQ, D), BF),
            V((3, 3, 2, q48, D), BF),
            V((3, 2, o48, D), BF),
            V((3, 2, f96, FH), BF),
            V((3, 2, p192, D), BF),
            V((3, 2, q48, D), BF),
            V((2, o48, D), BF),
            V((2, f96, FH), BF),
            V((2, p192, D), BF),
            V((4, 3, q48, DH), BF),
            V((4, o48, DH), BF),
            V((4, f96, FQ), BF),
            V((4, p192, DH), BF),
            V((3, q48, DH), BF),
            V((o48, DH), BF),
            V((f96, FQ), BF),
            V((p192, DH), BF),
            pltpu.SemaphoreType.DMA((160,)),
            pltpu.SemaphoreType.DMA((160,)),
        ],
        compiler_params=pltpu.CompilerParams(
            collective_id=0, has_side_effects=True, vmem_limit_bytes=63 * 2**20
        ),
    )(layer_in.astype(BF), cotangent.astype(BF), wq_t, w_out, w_fc, w_proj, misc, vecs)
    lo, gi, gq, go, gf, gp, vec, norms = outs
    lo, gi, gq, go, gf, gp = (v.astype(F32) for v in (lo, gi, gq, go, gf, gp))
    gq = jnp.transpose(gq, (2, 0, 1))
    if pairs > 1:
        groups = [[2 * p + q for p in range(pairs)] for q in range(2)]
        cores = [[2 * p, 2 * p + 1] for p in range(pairs)]
        gq, go, gf, gp, vec = (
            lax.psum(v, "row", axis_index_groups=groups) for v in (gq, go, gf, gp, vec)
        )

        def share(v, axis):
            whole = lax.all_gather(v, "row", axis=axis, tiled=True, axis_index_groups=cores)
            part = whole.shape[axis] // n_row
            return lax.dynamic_slice_in_dim(whole, r * part, part, axis)

        gq, go, gf, gp = share(gq, 0), share(go, 1), share(gf, 0), share(gp, 1)
    sample_norms = lax.dynamic_slice_in_dim(norms[:, 0], 2 * core, 2, 0)
    row = 6 + 3 * (c // 2)
    part = lax.rem(c, 2)
    bqv = lax.dynamic_slice(vec, (row, 0), (1, D)).reshape(2, HC)
    grad_bqv = lax.dynamic_slice(bqv, (0, part * HQ), (2, HQ))
    grad_bfc = lax.dynamic_slice(vec, (row + 1 + part, 0), (1, D))[0]
    return (
        lo, gi, sample_norms, gq, grad_bqv, go,
        vec[V_BOUT], vec[V_LN1G], vec[V_LN1B], vec[V_LN2G], vec[V_LN2B],
        gf, grad_bfc, gp, vec[V_BPROJ],
    )


def solution(mesh):
    in_specs = (
        P(("dp", "row"), "col", None),
        P("row", None, "col"),
        P(None, "col"),
        P("col", "row"),
        P(),
        P(),
        P(),
        P(),
        P(),
        P("row", "col"),
        P("col"),
        P("col", "row"),
        P(),
        P(("dp", "row")),
        P(("dp", "row"), "col", None),
    )
    out_specs = (
        P(("dp", "row"), "col", None),
        P(("dp", "row"), "col", None),
        P(("dp", "row")),
        P("row", None, "col"),
        P(None, "col"),
        P("col", "row"),
        P(),
        P(),
        P(),
        P(),
        P(),
        P("row", "col"),
        P("col"),
        P("col", "row"),
        P(),
    )
    return jax.shard_map(shards, mesh=mesh, in_specs=in_specs, out_specs=out_specs, check_vma=False)
```

```python
import functools

import jax
import jax.numpy as jnp
from jax import lax
from jax.experimental import pallas as pl
from jax.experimental.pallas import tpu as pltpu
from jax.sharding import PartitionSpec as P

MESH = pl.DeviceIdType.MESH
EPSILON = 1e-05
CLIP_BOUND = 1.0
GELU_C = 0.7978845608028654
GELU_A = 0.044715
MASKED = -1e30
HEAD_DIM = 64
QUAD = 4
BF = jnp.bfloat16
F32 = jnp.float32

V_BOUT, V_LN1G, V_LN1B, V_LN2G, V_LN2B, V_BPROJ, V_BQV, V_BFC, V_SQ = 0, 1, 2, 3, 4, 5, 6, 7, 9
V_FACTOR, V_NORM = 12, 13


def dot(a, b):
    return lax.dot_general(a, b, (((1,), (0,)), ((), ())), preferred_element_type=F32)


def dot_t(a, b):
    return lax.dot_general(a, b, (((1,), (1,)), ((), ())), preferred_element_type=F32)


def t_dot(a, b):
    return lax.dot_general(a, b, (((0,), (0,)), ((), ())), preferred_element_type=F32)


def fold8(v):
    return jnp.sum(v.reshape(v.shape[0] // 8, 8, v.shape[1]), axis=0)


def norm_stats(v):
    center = v - jnp.mean(v, axis=-1, keepdims=True)
    inverse = lax.rsqrt(jnp.mean(center * center, axis=-1, keepdims=True) + EPSILON)
    return center * inverse, inverse


def kernel(
    x_in, cot_in, wq_in, wo_in, wf_in, wp_in, misc_in, vec_in,
    lo_out, gi_out, gq_out, go_out, gf_out, gp_out, vec_out, norm_out,
    XR, H, A1, WQ, WO, WF, WP, MISC, QKV, CTX, LSE, KB, ACC,
    PS, PR, A2, M, SL, GF, GA, GCTX, GQKV, DK, DV, LO, GI,
    V8, SQ, VF, VK, VP, VZ,
    GWQ, GWO, GWF, GWP, RQ, RO, RF, RF2, RP, SQW, SOW, SFW, SFW2, SPW, ZQ, ZO, ZF, ZF2, ZP, EQ, EO, EF, EF2, EP,
    ss, rs,
):
    d, row, z = lax.axis_index("dp"), lax.axis_index("row"), lax.axis_index("col")
    k = lax.rem(row, 2)
    dq = d

    def at(plane, core, place):
        return (plane, row - k + core, place)

    zk, zs = z // 2, lax.rem(z, 2)
    L, D = A1.shape
    T = XR.shape[1]
    HC = CTX.shape[1]
    FH = M.shape[1]
    QR, OR_, FR, PR_ = wq_in.shape[1], wo_in.shape[0], wf_in.shape[0], wp_in.shape[0]
    DH = wo_in.shape[1]
    own, other = k * 2 * T, (1 - k) * 2 * T

    def mo(v, n):
        return pl.multiple_of(v, n)

    def when(cond, f):
        if cond is True:
            f()
        else:
            pl.when(cond)(f)

    n_send = [0]
    n_recv = [0]
    pending = []

    def new_send():
        n_send[0] += 1
        assert n_send[0] <= ss.shape[0]
        return n_send[0] - 1

    def new_recv(n):
        n_recv[0] += n
        assert n_recv[0] <= rs.shape[0]
        return n_recv[0] - n

    def send(src, dst, rsem, dev, cond=True):
        sem = new_send()

        def make():
            return pltpu.make_async_remote_copy(
                src(), dst(), ss.at[sem], rs.at[rsem], device_id=dev, device_id_type=MESH
            )

        when(cond, lambda: make().start())
        pending.append((cond, make))

    def local(src, dst, rsem, cond=True):
        when(cond, lambda: pltpu.make_async_copy(src(), dst(), rs.at[rsem]).start())

    def arrive(dst, rsem, cond=True):
        def f():
            pltpu.make_async_remote_copy(
                dst(), dst(), ss.at[0], rs.at[rsem], device_id=at(d, k, z), device_id_type=MESH
            ).wait_recv()

        when(cond, f)

    def arrive_local(dst, rsem, cond=True):
        when(cond, lambda: pltpu.make_async_copy(dst(), dst(), rs.at[rsem]).wait())

    mate = at(d, 1 - k, z)
    quad = [at(d ^ j, k, z) for j in (1, 2, 3)]

    barrier = pltpu.get_barrier_semaphore()
    line = [at(d, k, z ^ j) for j in (1, 2, 3)] + [at(d, 1 - k, z ^ j) for j in (0, 1, 2, 3)]
    for dev in quad + line:
        pl.semaphore_signal(barrier, inc=1, device_id=dev, device_id_type=MESH)
    pl.semaphore_wait(barrier, len(quad) + len(line))

    def line_send(src, dst):
        base = new_recv(2)
        for i in range(2):
            mine = (zk == k) & (2 * k + i == z)
            send(lambda i=i: src(i), lambda: dst(zs), base + zs, at(d, zk, 2 * k + i), jnp.logical_not(mine))
            local(lambda i=i: src(i), lambda: dst(zs), base + zs, mine)
        return base

    def line_wait(dst, base, i):
        mine = (zk == k) & (2 * k + i == z)
        arrive(lambda: dst(i), base + i, jnp.logical_not(mine))
        arrive_local(lambda: dst(i), base + i, mine)

    away = [2 * k + cs != z for cs in range(2)]
    near_mate = [[(2 * k + cs == z) & (k != r) for r in range(2)] for cs in range(2)]
    near_self = [[(2 * k + cs == z) & (k == r) for r in range(2)] for cs in range(2)]

    class Weight:
        def __init__(self, src, src_quarter, piece, full, slab):
            self.src, self.src_quarter, self.piece, self.full, self.slab = src, src_quarter, piece, full, slab
            self.zsem, self.xsem = new_recv(4), new_recv(8)

        def push(self):
            sem = self.zsem + zs * 2 + k
            for j in (1, 2, 3):
                send(self.src_quarter, lambda: self.piece(zs, k, dq), sem, at(d, zk, z ^ j))
            send(self.src, lambda: self.full(zs, k), sem, mate, zk != k)
            local(self.src, lambda: self.full(zs, k), sem, zk == k)

        def forward(self):
            for cs in range(2):
                for r in range(2):
                    sem = self.zsem + cs * 2 + r
                    arrive(lambda: self.piece(cs, r, dq), sem, away[cs])
                    arrive(lambda: self.full(cs, r), sem, near_mate[cs][r])
                    arrive_local(lambda: self.full(cs, r), sem, near_self[cs][r])
                mine = lambda cs=cs: self.slab(cs, dq)
                for j in (1, 2):
                    send(mine, mine, self.xsem + cs * 4 + j - 1, quad[j - 1], away[cs])

        def relay(self):
            for cs in range(2):
                for j in (1, 2):
                    arrive(lambda: self.slab(cs, dq ^ j), self.xsem + cs * 4 + j - 1, away[cs])
                    half = lambda cs=cs, j=j: self.piece(cs, j - 1, dq ^ j)
                    send(half, half, self.xsem + cs * 4 + 1 + j, quad[2 - j], away[cs])

        def ready(self):
            for cs in range(2):
                for j in (1, 2):
                    arrive(lambda: self.piece(cs, j - 1, dq ^ 3), self.xsem + cs * 4 + 1 + j, away[cs])

    q48, o48, f96, p192 = QR // QUAD, OR_ // QUAD, FR // QUAD, PR_ // QUAD

    def cols(r):
        return pl.ds(mo(r * DH, 128), DH)

    w_qkv = Weight(
        lambda: wq_in,
        lambda: wq_in.at[:, pl.ds(mo(dq * q48, 16), q48), :],
        lambda cs, r, q: WQ.at[:, pl.ds(mo(cs * QR + q * q48, 16), q48), cols(r)],
        lambda cs, r: WQ.at[:, pl.ds(mo(cs * QR, 16), QR), cols(r)],
        lambda cs, q: WQ.at[:, pl.ds(mo(cs * QR + q * q48, 16), q48), :],
    )
    w_out = Weight(
        lambda: wo_in,
        lambda: wo_in.at[pl.ds(mo(dq * o48, 16), o48), :],
        lambda cs, r, q: WO.at[pl.ds(mo(cs * OR_ + q * o48, 16), o48), cols(r)],
        lambda cs, r: WO.at[pl.ds(mo(cs * OR_, 16), OR_), cols(r)],
        lambda cs, q: WO.at[pl.ds(mo(cs * OR_ + q * o48, 16), o48), :],
    )
    FC = wf_in.shape[1]

    def fc_part(at0, n):
        return Weight(
            lambda: wf_in.at[:, pl.ds(at0, n)],
            lambda: wf_in.at[pl.ds(mo(dq * f96, 16), f96), pl.ds(at0, n)],
            lambda cs, r, q: WF.at[r, pl.ds(mo(q * f96, 16), f96), pl.ds(mo(cs * FC + at0, 128), n)],
            lambda cs, r: WF.at[r, :, pl.ds(mo(cs * FC + at0, 128), n)],
            lambda cs, q: WF.at[:, pl.ds(mo(q * f96, 16), f96), pl.ds(mo(cs * FC + at0, 128), n)],
        )

    def proj_part(at0, n):
        n4 = n // QUAD
        return Weight(
            lambda: wp_in.at[pl.ds(at0, n), :],
            lambda: wp_in.at[pl.ds(mo(at0 + dq * n4, 16), n4), :],
            lambda cs, r, q: WP.at[pl.ds(mo(cs * PR_ + at0 + q * n4, 16), n4), cols(r)],
            lambda cs, r: WP.at[pl.ds(mo(cs * PR_ + at0, 16), n), cols(r)],
            lambda cs, q: WP.at[pl.ds(mo(cs * PR_ + at0 + q * n4, 16), n4), :],
        )

    first = FC // 3
    w_fc, w_fc2 = fc_part(0, first), fc_part(first, FC - first)
    w_proj, w_proj2 = proj_part(0, first), proj_part(first, FC - first)

    misc_sem = new_recv(8)
    for dev in line:
        send(lambda: misc_in, lambda: MISC.at[k, z], misc_sem + k * 4 + z, dev)
    local(lambda: misc_in, lambda: MISC.at[k, z], misc_sem + k * 4 + z)
    w_qkv.push()
    x_sem = line_send(lambda i: x_in.at[i], lambda i: XR.at[i])

    V8[...] = jnp.zeros_like(V8)
    SQ[...] = jnp.zeros_like(SQ)

    vec = lambda i: vec_in[i : i + 1, :]
    b_out, ln1_g, ln1_b, ln2_g, ln2_b, b_proj = (vec(i) for i in range(6))

    w_qkv.forward()
    w_qkv.relay()

    RB = 32
    a1_sem = new_recv(2)

    def rows_of(base, i, n):
        return pl.ds(mo(base + i * n, 16), n)

    for s in range(2):
        line_wait(lambda i: XR.at[i], x_sem, s)

        def first_norm(i, c):
            scaled, _ = norm_stats(XR[s, rows_of(0, i, RB), :].astype(F32))
            A1[rows_of(own + s * T, i, RB), :] = (scaled * ln1_g + ln1_b).astype(BF)
            return c

        lax.fori_loop(0, T // RB, first_norm, 0)
        mine = lambda s=s: A1.at[pl.ds(mo(own + s * T, 16), T), :]
        send(mine, mine, a1_sem + s, mate)

    for r in range(2):
        for c in range(4):
            here = (k == r) & (z == c)
            arrive(lambda: MISC.at[r, c], misc_sem + r * 4 + c, jnp.logical_not(here))
            arrive_local(lambda: MISC.at[r, c], misc_sem + r * 4 + c, here)
    pair_misc = MISC[0, 2 * k] + MISC[0, 2 * k + 1]
    bias_q, bias_v = pair_misc[1:2, :HC], pair_misc[1:2, HC:]
    length = MISC[zk, 0, pl.ds(2 + zs, 1), :][:, 0:1]

    w_qkv.ready()

    def project(i, c):
        rows = rows_of(0, lax.rem(2 * k + i, 4), T)
        a = A1[rows, :]
        QKV[0, rows, :] = ((dot_t(a, WQ[0]) + bias_q).astype(BF).astype(F32) * (HEAD_DIM**-0.5)).astype(BF)
        QKV[1, rows, :] = dot_t(a, WQ[1]).astype(BF)
        QKV[2, rows, :] = (dot_t(a, WQ[2]) + bias_v).astype(BF)
        return c

    lax.fori_loop(0, 2, project, 0)
    for s in range(2):
        arrive(lambda: A1.at[pl.ds(mo(other + s * T, 16), T), :], a1_sem + s)
    for w in (w_out, w_fc, w_fc2, w_proj, w_proj2):
        w.push()
    cot_sem = line_send(lambda i: cot_in.at[i], lambda i: GF.at[pl.ds(mo(z * T, 16), T), :])
    lax.fori_loop(2, 4, project, 0)

    key_place = lax.broadcasted_iota(jnp.int32, (L, 128), 0).astype(F32)
    KB[...] = jnp.where(key_place < length, 0.0, MASKED)

    QB = T
    NQ = L // QB
    low_lane = lax.broadcasted_iota(jnp.int32, (1, 128), 1) < HEAD_DIM
    low_row = lax.broadcasted_iota(jnp.int32, (128, 1), 0) < HEAD_DIM
    diag = lax.broadcasted_iota(jnp.int32, (QB, QB), 0) <= lax.broadcasted_iota(jnp.int32, (QB, QB), 1)

    def keep_lane(v, h):
        return jnp.where(low_lane if h == 0 else jnp.logical_not(low_lane), v, jnp.zeros_like(v))

    def scores_t(kp, qm, qb):
        kv = (qb + 1) * QB
        s = dot_t(kp[:kv], qm)
        kb = KB[0:kv, :]
        s = s + jnp.concatenate([kb] * (QB // 128), axis=1)
        last = jnp.where(diag, s[kv - QB :], MASKED)
        if qb == 0:
            return last
        return jnp.concatenate([s[: kv - QB], last], axis=0)

    def attend(p):
        lanes = pl.ds(mo(p * 128, 128), 128)
        kp, vp = QKV[1, :, lanes], QKV[2, :, lanes]
        vt = vp.T
        for qb in range(NQ):
            kv = (qb + 1) * QB
            qp = QKV[0, qb * QB : kv, lanes]
            parts = []
            for h in range(2):
                s = scores_t(kp, keep_lane(qp, h), qb)
                top = jnp.max(s, axis=0, keepdims=True)
                e = jnp.exp(s - top)
                total = jnp.sum(e, axis=0, keepdims=True)
                LSE[pl.ds(2 * p + h, 1), qb * QB : kv] = top + jnp.log(total)
                parts.append(dot(vt[:, :kv], e.astype(BF)) / total)
            CTX[qb * QB : kv, lanes] = jnp.where(low_row, parts[0], parts[1]).T.astype(BF)

    def attend_step(p, c):
        @pl.when(p == 1)
        def _():
            w_out.forward()
            w_fc.forward()

        @pl.when(p == 2)
        def _():
            w_out.relay()
            w_fc.relay()

        attend(p)
        return c

    lax.fori_loop(0, HC // 128, attend_step, 0)
    w_fc2.forward()

    def split_sum(n, product, sums=None):
        base = new_recv(2)
        for s in range(2):
            PS[n, s] = product(pl.ds(mo(other + s * T, 16), T)).astype(BF)
            send(lambda s=s: PS.at[n, s], lambda s=s: PR.at[n, s], base + s, mate)

        def keep(s, c):
            ACC[s] = product(pl.ds(mo(own + s * T, 16), T))
            return c

        lax.fori_loop(0, 2, keep, 0)
        return base

    def split_wait(n, base, s):
        arrive(lambda: PR.at[n, s], base + s)

    w_out.ready()
    ex = split_sum(0, lambda rows: dot(CTX[rows, :], WO[...]))
    w_fc2.relay()
    w_proj.forward()
    a2_sem = new_recv(2)
    for s in range(2):
        split_wait(0, ex, s)

        def second_norm(i, c):
            rows = rows_of(0, i, RB)
            h = XR[s, rows, :].astype(F32) + ACC[s, rows, :] + PR[0, s, rows, :].astype(F32) + b_out
            H[s, rows, :] = h
            scaled, _ = norm_stats(h)
            A2[rows_of(own + s * T, i, RB), :] = (scaled * ln2_g + ln2_b).astype(BF)
            return c

        lax.fori_loop(0, T // RB, second_norm, 0)
        mine = lambda s=s: A2.at[pl.ds(mo(own + s * T, 16), T), :]
        send(mine, mine, a2_sem + s, mate)

    VF[...] = jnp.concatenate([MISC[0, 2 * k, 0:1, :], MISC[0, 2 * k + 1, 0:1, :]], axis=1)

    def hidden(start, width):
        def body(i, c):
            rows = rows_of(0, lax.rem(2 * k + i // 2, 4), T)
            cs = pl.ds(mo(lax.rem(i, 2) * FC + start, 128), width)
            u = dot(A2[rows, :], WF[:, :, cs].reshape(D, width)) + VF[:, cs]
            t = jnp.tanh(GELU_C * (u + GELU_A * u * u * u))
            M[rows, cs] = (0.5 * u * (1.0 + t)).astype(BF)
            SL[rows, cs] = (
                0.5 * (1.0 + t) + 0.5 * u * (1.0 - t * t) * GELU_C * (1.0 + 3.0 * GELU_A * u * u)
            ).astype(BF)
            return c

        return body

    w_fc.ready()
    lax.fori_loop(0, 4, hidden(0, first), 0)
    for s in range(2):
        arrive(lambda: A2.at[pl.ds(mo(other + s * T, 16), T), :], a2_sem + s)
    lax.fori_loop(4, 8, hidden(0, first), 0)
    w_proj2.forward()
    w_proj.relay()
    w_fc2.ready()
    lax.fori_loop(0, 8, hidden(first, FC - first), 0)
    w_proj2.relay()
    w_proj.ready()
    w_proj2.ready()
    ex = split_sum(1, lambda rows: dot(M[rows, :], WP[...]))

    gf_sem = new_recv(2)
    for s in range(2):
        line_wait(lambda i: GF.at[pl.ds(mo(own + i * T, 16), T), :], cot_sem, s)

        def mask_rows(i, c):
            rows = rows_of(own + s * T, i, RB)
            place = (lax.broadcasted_iota(jnp.int32, (RB, 1), 0) + (own + s * T + i * RB)).astype(F32)
            g = jnp.where(place < length, GF[rows, :].astype(F32), 0.0)
            GF[rows, :] = g.astype(BF)
            V8[V_BPROJ] += fold8(g)
            return c

        lax.fori_loop(0, T // RB, mask_rows, 0)
        mine = lambda s=s: GF.at[pl.ds(mo(own + s * T, 16), T), :]
        send(mine, mine, gf_sem + s, mate)

    for s in range(2):
        split_wait(1, ex, s)

        def output_rows(i, c):
            rows = rows_of(0, i, RB)
            LO[s, rows, :] = (H[s, rows, :] + ACC[s, rows, :] + PR[1, s, rows, :].astype(F32) + b_proj).astype(BF)
            return c

        lax.fori_loop(0, T // RB, output_rows, 0)
    lo_sem = line_send(lambda i: LO.at[i], lambda i: lo_out.at[i])

    for s in range(2):
        arrive(lambda: GF.at[pl.ds(mo(other + s * T, 16), T), :], gf_sem + s)

    class Part:
        def __init__(self, quarter, R, S, Z, E, pieces, place):
            self.quarter, self.R, self.S, self.Z, self.E = quarter, R, S, Z, E
            self.pieces, self.place = pieces, place
            self.raw, self.zsem, self.end = new_recv(3), new_recv(4), new_recv(4)

        def spread(self):
            for j in (1, 2, 3):
                send(lambda j=j: self.quarter(dq ^ j), lambda j=j: self.R.at[j - 1], self.raw + j - 1, quad[j - 1])

        def reduce(self):
            for j in (1, 2, 3):
                arrive(lambda: self.R.at[j - 1], self.raw + j - 1)
            G, (_, n, width) = self.quarter(dq), self.S.shape
            wide = lambda f: f if width <= D else jnp.concatenate([f] * (width // D), axis=1)
            factors = [wide(VP[dq ^ j, V_FACTOR : V_FACTOR + 1, :]) for j in range(QUAD)]
            steps = n // 16

            def add(i, c):
                a, rows = i // steps, pl.ds(mo(lax.rem(i, steps) * 16, 16), 16)
                v = G[a, rows, :].astype(F32) * factors[0]
                for j in (1, 2, 3):
                    v = v + self.R[j - 1, a, rows, :].astype(F32) * factors[j]
                self.S[a, rows, :] = v.astype(BF)
                return c

            lax.fori_loop(0, 2 * steps, add, 0)
            for cs in range(2):
                for r in range(2):
                    mine = (r == k) & (2 * k + cs == z)
                    piece = lambda cs=cs, r=r: self.pieces(cs, r)
                    send(piece, lambda: self.Z.at[z], self.zsem + z, at(d, r, 2 * k + cs), jnp.logical_not(mine))
                    local(piece, lambda: self.Z.at[z], self.zsem + z, mine)

        def finish(self):
            for c in range(4):
                here = (zk == k) & (z == c)
                arrive(lambda: self.Z.at[c], self.zsem + c, jnp.logical_not(here))
                arrive_local(lambda: self.Z.at[c], self.zsem + c, here)
            Z = self.Z
            self.E[...] = (
                Z[0].astype(F32) + Z[1].astype(F32) + Z[2].astype(F32) + Z[3].astype(F32)
            ).astype(BF)
            for j in (1, 2, 3):
                send(lambda: self.E, lambda: self.place(dq), self.end + j, quad[j - 1])
            local(lambda: self.E, lambda: self.place(dq), self.end)

        def done(self):
            arrive_local(lambda: self.place(dq), self.end)
            for j in (1, 2, 3):
                arrive(lambda: self.place(dq ^ j), self.end + j)

    g_proj = Part(
        lambda q: GWP.at[:, pl.ds(mo(q * p192, 16), p192), :], RP, SPW, ZP, EP,
        lambda cs, r: SPW.at[cs, :, cols(r)],
        lambda q: gp_out.at[pl.ds(mo(q * p192, 16), p192), :],
    )
    g_out = Part(
        lambda q: GWO.at[:, pl.ds(mo(q * o48, 16), o48), :], RO, SOW, ZO, EO,
        lambda cs, r: SOW.at[cs, :, cols(r)],
        lambda q: go_out.at[pl.ds(mo(q * o48, 16), o48), :],
    )

    def fc_grad(R, S, Z, E, start, n):
        return Part(
            lambda q: GWF.at[:, pl.ds(mo(start + q * n, 16), n), :], R, S, Z, E,
            lambda cs, r: S.at[r, :, pl.ds(mo(cs * FC, 128), FC)],
            lambda q: gf_out.at[pl.ds(mo(start + q * n, 16), n), :],
        )

    g_fc = fc_grad(RF, SFW, ZF, EF, 0, 128 // QUAD)
    g_fc2 = fc_grad(RF2, SFW2, ZF2, EF2, 128, (FR - 128) // QUAD)

    def qkv_grad(i):
        return Part(
            lambda q: GWQ.at[i, :, pl.ds(mo(q * q48, 16), q48), :], RQ.at[i], SQW.at[i], ZQ.at[i], EQ.at[i],
            lambda cs, r: SQW.at[i, cs, :, cols(r)],
            lambda q: gq_out.at[i, pl.ds(mo(q * q48, 16), q48), :],
        )

    g_qkv = [qkv_grad(i) for i in range(3)]

    def grad_proj(i, c):
        cs = pl.ds(mo(i * 256, 128), 256)
        g = t_dot(M[:, cs], GF[...])
        SQ[...] += fold8(g * g)
        GWP[i // 3, pl.ds(mo(lax.rem(i, 3) * 256, 16), 256), :] = g.astype(BF)
        return c

    lax.fori_loop(0, FH // 256, grad_proj, 0)
    g_proj.spread()

    NB = 512
    NN = FH // NB

    def grad_hidden(i, c):
        rows = rows_of(0, i // NN, T)
        cs = pl.ds(mo(lax.rem(i, NN) * NB, 128), NB)
        g = dot_t(GF[rows, :], WP[cs, :]) * SL[rows, cs].astype(F32)
        low = g.astype(BF)
        SL[rows, cs] = low
        VF[:, cs] = jnp.where(i < NN, 0.0, VF[:, cs]) + jnp.sum(low.astype(F32), axis=0, keepdims=True)
        return c

    lax.fori_loop(0, 4 * NN, grad_hidden, 0)
    ex = split_sum(2, lambda rows: dot_t(SL[rows, :], WF[...].reshape(D, FH)))

    ga_sem = new_recv(2)
    for s in range(2):
        split_wait(2, ex, s)

        def second_back(i, c):
            rows = rows_of(0, i, RB)
            full = rows_of(own + s * T, i, RB)
            up = ACC[s, rows, :] + PR[2, s, rows, :].astype(F32)
            scaled, inverse = norm_stats(H[s, rows, :])
            through = up * ln2_g
            V8[V_LN2G] += fold8(up * scaled)
            V8[V_LN2B] += fold8(up)
            g = GF[full, :].astype(F32) + inverse * (
                through
                - jnp.mean(through, axis=-1, keepdims=True)
                - scaled * jnp.mean(through * scaled, axis=-1, keepdims=True)
            )
            V8[V_BOUT] += fold8(g)
            H[s, rows, :] = g
            GA[full, :] = g.astype(BF)
            return c

        lax.fori_loop(0, T // RB, second_back, 0)
        mine = lambda s=s: GA.at[pl.ds(mo(own + s * T, 16), T), :]
        send(mine, mine, ga_sem + s, mate)
    for s in range(2):
        arrive(lambda: GA.at[pl.ds(mo(other + s * T, 16), T), :], ga_sem + s)

    def grad_context(i, c):
        rows = rows_of(0, i, T)
        GCTX[rows, :] = dot_t(GA[rows, :], WO[...]).astype(BF)
        return c

    lax.fori_loop(0, 4, grad_context, 0)
    half = HC // 2
    for cs in range(HC // 128):
        g = t_dot(CTX[:, cs * 128 : (cs + 1) * 128], GA[...])
        SQ[...] += fold8(g * g)
        low = g.astype(BF)
        lo_row = cs * 128
        if lo_row + 128 <= half:
            GWO[0, lo_row : lo_row + 128, :] = low
        elif lo_row >= half:
            GWO[1, lo_row - half : lo_row - half + 128, :] = low
        else:
            GWO[0, lo_row:half, :] = low[: half - lo_row]
            GWO[1, : lo_row + 128 - half, :] = low[half - lo_row :]
    g_out.spread()

    def grad_fc(i, c):
        block = lax.rem(i, 2) * 3 + i // 2
        cs = pl.ds(mo(block * 128, 128), 128)
        g = t_dot(A2[:, cs], SL[...])
        q = fold8(g * g)
        SQ[...] += q[:, :D] + q[:, D:]
        GWF[lax.rem(i, 2), pl.ds(mo(i // 2 * 128, 16), 128), :] = g.astype(BF)
        return c

    lax.fori_loop(0, 2, grad_fc, 0)
    g_fc.spread()

    def attend_back(p):
        lanes = pl.ds(mo(p * 128, 128), 128)
        kp, vp = QKV[1, :, lanes], QKV[2, :, lanes]
        kt = kp.T
        DK[...] = jnp.zeros_like(DK)
        DV[...] = jnp.zeros_like(DV)
        for qb in range(NQ):
            kv = (qb + 1) * QB
            qp = QKV[0, qb * QB : kv, lanes]
            do = GCTX[qb * QB : kv, lanes]
            dqt = []
            for h in range(2):
                qm, dm = keep_lane(qp, h), keep_lane(do, h)
                pt = jnp.exp(scores_t(kp, qm, qb) - LSE[pl.ds(2 * p + h, 1), qb * QB : kv])
                gp = dot_t(vp[:kv], dm)
                both = pt * gp
                gs = (both - pt * jnp.sum(both, axis=0, keepdims=True)).astype(BF)
                DV[0:kv, :] += dot(pt.astype(BF), dm)
                DK[0:kv, :] += dot(gs, qm)
                dqt.append(dot(kt[:, :kv], gs))
            GQKV[0, qb * QB : kv, lanes] = (
                jnp.where(low_row, dqt[0], dqt[1]).T * (HEAD_DIM**-0.5)
            ).astype(BF)
        GQKV[1, :, lanes] = DK[...].astype(BF)
        GQKV[2, :, lanes] = DV[...].astype(BF)

    def attend_back_step(p, c):
        attend_back(p)
        return c

    lax.fori_loop(0, HC // 128, attend_back_step, 0)

    def grad_norm_in(rows):
        return dot(GQKV[0, rows, :], WQ[0]) + dot(GQKV[1, rows, :], WQ[1]) + dot(GQKV[2, rows, :], WQ[2])

    ex = split_sum(3, grad_norm_in)
    lax.fori_loop(2, D // 128, grad_fc, 0)
    for s in range(2):
        split_wait(3, ex, s)

        def first_back(i, c):
            rows = rows_of(0, i, RB)
            up = ACC[s, rows, :] + PR[3, s, rows, :].astype(F32)
            scaled, inverse = norm_stats(XR[s, rows, :].astype(F32))
            through = up * ln1_g
            V8[V_LN1G] += fold8(up * scaled)
            V8[V_LN1B] += fold8(up)
            g = H[s, rows, :] + inverse * (
                through
                - jnp.mean(through, axis=-1, keepdims=True)
                - scaled * jnp.mean(through * scaled, axis=-1, keepdims=True)
            )
            GI[s, rows, :] = g.astype(BF)
            return c

        lax.fori_loop(0, T // RB, first_back, 0)

    gi_sem = line_send(lambda i: GI.at[i], lambda i: gi_out.at[i])

    def grad_qkv(i, c):
        g = t_dot(GQKV[i], A1[...])
        SQ[...] += fold8(g * g)
        low = g.astype(BF)
        GWQ[i, 0] = low[:half]
        GWQ[i, 1] = low[half:]
        return c

    lax.fori_loop(0, 3, grad_qkv, 0)
    VK[k] = jnp.zeros(VK.shape[1:], F32)
    for i in range(6):
        VK[k, i : i + 1, :] = jnp.sum(V8[i], axis=0, keepdims=True)
    VK[k, V_BQV : V_BQV + 1, :] = jnp.concatenate(
        [jnp.sum(GQKV[i].astype(F32), axis=0, keepdims=True) for i in (0, 2)], axis=1
    )
    VK[k, V_BFC : V_BFC + 1, :] = VF[:, :D]
    VK[k, V_BFC + 1 : V_BFC + 2, :] = VF[:, D:]
    VK[k, V_SQ : V_SQ + 1, :] = jnp.sum(SQ[...], axis=0, keepdims=True)
    vk_sem = new_recv(1)
    send(lambda: VK.at[k], lambda: VK.at[k], vk_sem, mate)
    arrive(lambda: VK.at[1 - k], vk_sem)
    va, vb = VK[0], VK[1]
    pack = jnp.concatenate([va[0:6] + vb[0:6], va[6:9], vb[6:9]], axis=0)
    squares = jnp.sum(jnp.sum(pack * pack, axis=0, keepdims=True) + va[9:10] + vb[9:10], axis=1, keepdims=True)
    norm = jnp.sqrt(squares)
    factor = CLIP_BOUND / jnp.maximum(norm, CLIP_BOUND)
    wide = lambda v: jnp.broadcast_to(v, (1, D))
    VP[dq] = jnp.concatenate([pack, wide(factor), wide(norm), jnp.zeros((2, D), F32)], axis=0)
    vp_sem = new_recv(3)
    for j in (1, 2, 3):
        send(lambda: VP.at[dq], lambda: VP.at[dq], vp_sem + j - 1, quad[j - 1])
    for part in (g_fc2, *g_qkv):
        part.spread()

    for j in (1, 2, 3):
        arrive(lambda: VP.at[dq ^ j], vp_sem + j - 1)

    total = jnp.zeros((12, D), F32)
    for q in range(QUAD):
        total = total + VP[q, 0:12, :] * VP[q, V_FACTOR : V_FACTOR + 1, :]
    VZ[z] = jnp.concatenate([total, VP[dq, V_FACTOR:, :]], axis=0)
    vz_sem = new_recv(3)
    for j in (1, 2, 3):
        send(lambda: VZ.at[z], lambda: VZ.at[z], vz_sem + j - 1, at(d, k, z ^ j))

    order = [g_proj, g_out, g_fc, g_fc2, *g_qkv]
    for i, part in enumerate(order):
        part.reduce()
        if i >= 2:
            order[i - 2].finish()
    for part in order[-2:]:
        part.finish()

    for j in (1, 2, 3):
        arrive(lambda: VZ.at[z ^ j], vz_sem + j - 1)
    vec_out[...] = (VZ[0] + VZ[1] + VZ[2] + VZ[3])[0:12]
    for c in range(4):
        norm_out[c : c + 1, :] = VZ[c, V_NORM : V_NORM + 1, 0:128]

    for part in order:
        part.done()
    for i in range(2):
        line_wait(lambda i: lo_out.at[i], lo_sem, i)
        line_wait(lambda i: gi_out.at[i], gi_sem, i)
    for cond, make in pending:
        when(cond, lambda: make().wait_send())


def shards(
    layer_in, w_qkv, b_qv, w_out, b_out, ln1_g, ln1_b, ln2_g, ln2_b, w_fc, b_fc, w_proj, b_proj, lengths, cotangent
):
    E, T, D = layer_in.shape
    n_col, n_row = lax.axis_size("col"), lax.axis_size("row")
    assert lax.axis_size("dp") == QUAD and n_col == 4 and n_row % 2 == 0
    pairs = n_row // 2
    r = lax.axis_index("row")
    core = lax.rem(r, 2)
    half_rows = w_fc.shape[0] * pairs

    def halves(w, axis):
        if pairs == 1:
            return w
        whole = lax.all_gather(w, "row", axis=axis, tiled=True)
        return lax.dynamic_slice_in_dim(whole, core * half_rows, half_rows, axis)

    w_qkv, w_out, w_fc, w_proj = halves(w_qkv, 0), halves(w_out, 1), halves(w_fc, 0), halves(w_proj, 1)
    L = T * n_col
    HQ = w_qkv.shape[2]
    HC = HQ * n_col // 2
    FQ = w_fc.shape[1]
    FH = FQ * n_col // 2
    DH = w_fc.shape[0]
    c = lax.axis_index("col")

    zero = jnp.zeros_like(b_qv)
    even = lax.rem(c, 2) == 0
    both = jnp.where(
        even, jnp.concatenate([b_qv, zero], axis=1), jnp.concatenate([zero, b_qv], axis=1)
    ).reshape(1, 2 * HC)
    misc = jnp.concatenate(
        [
            b_fc[None, :],
            both,
            jnp.broadcast_to(lengths.astype(F32)[:, None], (E, D)),
            jnp.zeros((4, D), F32),
        ],
        axis=0,
    )
    vecs = jnp.stack([b_out, ln1_g, ln1_b, ln2_g, ln2_b, b_proj, b_proj, b_proj])
    wq_t = jnp.transpose(w_qkv, (1, 2, 0))
    q48, o48, p192 = HQ // QUAD, HQ // QUAD, FQ // QUAD
    fa, fb = 128 // QUAD, (DH - 128) // QUAD

    anyspec = pl.BlockSpec(memory_space=pl.ANY)
    vm = pl.BlockSpec(memory_space=pltpu.VMEM)
    V = pltpu.VMEM
    outs = pl.pallas_call(
        kernel,
        name="layer",
        out_shape=(
            jax.ShapeDtypeStruct((E, T, D), BF),
            jax.ShapeDtypeStruct((E, T, D), BF),
            jax.ShapeDtypeStruct((3, HQ, DH), BF),
            jax.ShapeDtypeStruct((HQ, DH), BF),
            jax.ShapeDtypeStruct((DH, FQ), BF),
            jax.ShapeDtypeStruct((FQ, DH), BF),
            jax.ShapeDtypeStruct((12, D), F32),
            jax.ShapeDtypeStruct((8, 128), F32),
        ),
        in_specs=[anyspec] * 7 + [vm],
        out_specs=(anyspec,) * 6 + (vm, vm),
        scratch_shapes=[
            V((2, T, D), BF),
            V((2, T, D), F32),
            V((L, D), BF),
            V((3, HC, D), BF),
            V((HC, D), BF),
            V((2, DH, FH), BF),
            V((FH, D), BF),
            V((2, n_col, 8, D), F32),
            V((3, L, HC), BF),
            V((L, HC), BF),
            V((8, L), F32),
            V((L, 128), F32),
            V((2, T, D), F32),
            V((4, 2, T, D), BF),
            V((4, 2, T, D), BF),
            V((L, D), BF),
            V((L, FH), BF),
            V((L, FH), BF),
            V((L, D), BF),
            V((L, D), BF),
            V((L, HC), BF),
            V((3, L, HC), BF),
            V((L, 128), F32),
            V((L, 128), F32),
            V((2, T, D), BF),
            V((2, T, D), BF),
            V((6, 8, D), F32),
            V((8, D), F32),
            V((1, FH), F32),
            V((2, 16, D), F32),
            V((QUAD, 16, D), F32),
            V((n_col, 16, D), F32),
            V((3, 2, HQ, D), BF),
            V((2, HQ, D), BF),
            V((2, DH, FH), BF),
            V((2, FQ, D), BF),
            V((3, 3, 2, q48, D), BF),
            V((3, 2, o48, D), BF),
            V((3, 2, fa, FH), BF),
            V((3, 2, fb, FH), BF),
            V((3, 2, p192, D), BF),
            V((3, 2, q48, D), BF),
            V((2, o48, D), BF),
            V((2, fa, FH), BF),
            V((2, fb, FH), BF),
            V((2, p192, D), BF),
            V((3, 4, q48, DH), BF),
            V((4, o48, DH), BF),
            V((4, fa, FQ), BF),
            V((4, fb, FQ), BF),
            V((4, p192, DH), BF),
            V((3, q48, DH), BF),
            V((o48, DH), BF),
            V((fa, FQ), BF),
            V((fb, FQ), BF),
            V((p192, DH), BF),
            pltpu.SemaphoreType.DMA((200,)),
            pltpu.SemaphoreType.DMA((200,)),
        ],
        compiler_params=pltpu.CompilerParams(
            collective_id=0, has_side_effects=True, vmem_limit_bytes=63 * 2**20
        ),
    )(layer_in.astype(BF), cotangent.astype(BF), wq_t, w_out, w_fc, w_proj, misc, vecs)
    lo, gi, gq, go, gf, gp, vec, norms = outs
    lo, gi, gq, go, gf, gp = (v.astype(F32) for v in (lo, gi, gq, go, gf, gp))
    gq = jnp.transpose(gq, (2, 0, 1))
    if pairs > 1:
        groups = [[2 * p + q for p in range(pairs)] for q in range(2)]
        cores = [[2 * p, 2 * p + 1] for p in range(pairs)]
        gq, go, gf, gp, vec = (
            lax.psum(v, "row", axis_index_groups=groups) for v in (gq, go, gf, gp, vec)
        )

        def share(v, axis):
            whole = lax.all_gather(v, "row", axis=axis, tiled=True, axis_index_groups=cores)
            part = whole.shape[axis] // n_row
            return lax.dynamic_slice_in_dim(whole, r * part, part, axis)

        gq, go, gf, gp = share(gq, 0), share(go, 1), share(gf, 0), share(gp, 1)
    sample_norms = lax.dynamic_slice_in_dim(norms[:, 0], 2 * core, 2, 0)
    row = 6 + 3 * (c // 2)
    part = lax.rem(c, 2)
    bqv = lax.dynamic_slice(vec, (row, 0), (1, D)).reshape(2, HC)
    grad_bqv = lax.dynamic_slice(bqv, (0, part * HQ), (2, HQ))
    grad_bfc = lax.dynamic_slice(vec, (row + 1 + part, 0), (1, D))[0]
    return (
        lo, gi, sample_norms, gq, grad_bqv, go,
        vec[V_BOUT], vec[V_LN1G], vec[V_LN1B], vec[V_LN2G], vec[V_LN2B],
        gf, grad_bfc, gp, vec[V_BPROJ],
    )


def solution(mesh):
    in_specs = (
        P(("dp", "row"), "col", None),
        P("row", None, "col"),
        P(None, "col"),
        P("col", "row"),
        P(),
        P(),
        P(),
        P(),
        P(),
        P("row", "col"),
        P("col"),
        P("col", "row"),
        P(),
        P(("dp", "row")),
        P(("dp", "row"), "col", None),
    )
    out_specs = (
        P(("dp", "row"), "col", None),
        P(("dp", "row"), "col", None),
        P(("dp", "row")),
        P("row", None, "col"),
        P(None, "col"),
        P("col", "row"),
        P(),
        P(),
        P(),
        P(),
        P(),
        P("row", "col"),
        P("col"),
        P("col", "row"),
        P(),
    )
    return jax.shard_map(shards, mesh=mesh, in_specs=in_specs, out_specs=out_specs, check_vma=False)
```

```python
import functools

import jax
import jax.numpy as jnp
from jax import lax
from jax.experimental import pallas as pl
from jax.experimental.pallas import tpu as pltpu
from jax.sharding import PartitionSpec as P

MESH = pl.DeviceIdType.MESH
EPSILON = 1e-05
CLIP_BOUND = 1.0
GELU_C = 0.7978845608028654
GELU_A = 0.044715
MASKED = -1e30
HEAD_DIM = 64
QUAD = 4
BF = jnp.bfloat16
F32 = jnp.float32

V_BOUT, V_LN1G, V_LN1B, V_LN2G, V_LN2B, V_BPROJ, V_BQV, V_BFC, V_SQ = 0, 1, 2, 3, 4, 5, 6, 7, 9
V_FACTOR, V_NORM = 12, 13


def dot(a, b):
    return lax.dot_general(a, b, (((1,), (0,)), ((), ())), preferred_element_type=F32)


def dot_t(a, b):
    return lax.dot_general(a, b, (((1,), (1,)), ((), ())), preferred_element_type=F32)


def t_dot(a, b):
    return lax.dot_general(a, b, (((0,), (0,)), ((), ())), preferred_element_type=F32)


def fold8(v):
    return jnp.sum(v.reshape(v.shape[0] // 8, 8, v.shape[1]), axis=0)


def norm_stats(v):
    center = v - jnp.mean(v, axis=-1, keepdims=True)
    inverse = lax.rsqrt(jnp.mean(center * center, axis=-1, keepdims=True) + EPSILON)
    return center * inverse, inverse


def kernel(
    x_in, cot_in, wq_in, wo_in, wf_in, wp_in, bfc_in, bqv_in, len_in, b_out, ln1_g, ln1_b, ln2_g, ln2_b, b_proj,
    lo_out, gi_out, gq_out, go_out, gf_out, gp_out, vec_out,
    XS, XH, CS, misc_in, XR, H, A1, WQ, WO, WF, WP, MISC, QKV, CTX, LSE, KB, ACC,
    PS, PR, A2, M, SL, GF, GA, GCTX, GQKV, DK, DV, LO, GI,
    V8, SQ, VF, VK, VP, VZ,
    GWQ, GWO, GWF, GWP, RQ, RO, RF, RF2, RP, SQW, SOW, SFW, SFW2, SPW, BQ, BO, BF1, BF2, BP, UQ, UO, UF, UF2, UP, ZQ, ZO, ZF, ZF2, ZP, EQ, EO, EF, EF2, EP,
    ss, rs,
):
    d, row, z = lax.axis_index("dp"), lax.axis_index("row"), lax.axis_index("col")
    k = lax.rem(row, 2)
    dq = d

    def at(plane, core, place):
        return (plane, row - k + core, place)

    zk, zs = z // 2, lax.rem(z, 2)
    L, D = A1.shape
    T = XR.shape[1]
    HC = CTX.shape[1]
    FH = M.shape[1]
    QR, OR_, FR, PR_ = wq_in.shape[1], wo_in.shape[0], wf_in.shape[0], wp_in.shape[0]
    DH = wo_in.shape[1]
    own, other = k * 2 * T, (1 - k) * 2 * T

    def mo(v, n):
        return pl.multiple_of(v, n)

    def when(cond, f):
        if cond is True:
            f()
        else:
            pl.when(cond)(f)

    n_send = [0]
    n_recv = [0]
    pending = []

    def new_send():
        n_send[0] += 1
        assert n_send[0] <= ss.shape[0]
        return n_send[0] - 1

    def new_recv(n):
        n_recv[0] += n
        assert n_recv[0] <= rs.shape[0]
        return n_recv[0] - n

    def send(src, dst, rsem, dev, cond=True):
        sem = new_send()

        def make():
            return pltpu.make_async_remote_copy(
                src(),
                dst(),
                ss.at[sem],
                rs.at[rsem() if callable(rsem) else rsem],
                device_id=dev() if callable(dev) else dev,
                device_id_type=MESH,
            )

        when(cond, lambda: make().start())
        pending.append((cond, make))

    def local(src, dst, rsem, cond=True):
        when(cond, lambda: pltpu.make_async_copy(src(), dst(), rs.at[rsem]).start())

    def arrive(dst, rsem, cond=True):
        def f():
            pltpu.make_async_remote_copy(
                dst(), dst(), ss.at[0], rs.at[rsem], device_id=at(d, k, z), device_id_type=MESH
            ).wait_recv()

        when(cond, f)

    def arrive_local(dst, rsem, cond=True):
        when(cond, lambda: pltpu.make_async_copy(dst(), dst(), rs.at[rsem]).wait())

    mate = at(d, 1 - k, z)
    quad = [at(d ^ j, k, z) for j in (1, 2, 3)]

    barrier = pltpu.get_barrier_semaphore()
    line = [at(d, k, z ^ j) for j in (1, 2, 3)] + [at(d, 1 - k, z ^ j) for j in (0, 1, 2, 3)]
    for dev in quad + line:
        pl.semaphore_signal(barrier, inc=1, device_id=dev, device_id_type=MESH)
    pl.semaphore_wait(barrier, len(quad) + len(line))

    def line_send(src, dst):
        base = new_recv(2)
        for i in range(2):
            mine = (zk == k) & (2 * k + i == z)
            send(lambda i=i: src(i), lambda: dst(zs), base + zs, at(d, zk, 2 * k + i), jnp.logical_not(mine))
            local(lambda i=i: src(i), lambda: dst(zs), base + zs, mine)
        return base

    def line_wait(dst, base, i):
        mine = (zk == k) & (2 * k + i == z)
        arrive(lambda: dst(i), base + i, jnp.logical_not(mine))
        arrive_local(lambda: dst(i), base + i, mine)

    far = lax.rem(k + zk, 2)
    target = z ^ (2 * far)
    is_near, is_far = far == 0, far == 1
    zo = 1 - zs

    class Weight:
        def __init__(self, src, src_quarter, piece, full, slab):
            self.src, self.src_quarter, self.piece, self.full, self.slab = src, src_quarter, piece, full, slab
            self.zsem, self.xsem = new_recv(4), new_recv(8)

        def push(self):
            sem = lambda: self.zsem + zs * 2 + k
            for j in (2, 1):
                send(self.src_quarter, lambda: self.piece(zs, k, dq), sem, lambda j=j: at(d, zk, z ^ j))
            send(self.src, lambda: self.full(zs, k), sem, mate, is_far)
            local(self.src, lambda: self.full(zs, k), self.zsem + zs * 2 + k, is_near)

        def spread(self, cs, cond):
            mine = lambda: self.slab(cs, dq)
            for j in (1, 2):
                send(mine, mine, lambda j=j: self.xsem + cs * 4 + j - 1, quad[j - 1], cond)

        def hop(self):
            for r in range(2):
                arrive(lambda: self.piece(zo, r, dq), self.zsem + zo * 2 + r, is_near)
                arrive(lambda: self.piece(zs, r, dq), self.zsem + zs * 2 + r, is_far)
                mine = lambda r=r: self.piece(zs, r, dq)
                send(mine, mine, lambda r=r: self.zsem + zs * 2 + r, lambda: at(d, k, z ^ 1), is_far)
            self.spread(zo, is_near)
            self.spread(zs, is_far)

        def forward(self):
            for r in range(2):
                arrive(lambda: self.piece(zo, r, dq), self.zsem + zo * 2 + r, is_far)
            self.spread(zo, is_far)

        def relay(self):
            for cs, cond in ((zs, is_far), (zo, True)):
                for j in (1, 2):
                    arrive(lambda: self.slab(cs, dq ^ j), self.xsem + cs * 4 + j - 1, cond)
                    half = lambda cs=cs, j=j: self.piece(cs, j - 1, dq ^ j)
                    send(half, half, lambda cs=cs, j=j: self.xsem + cs * 4 + 1 + j, quad[2 - j], cond)

        def ready(self):
            for r in range(2):
                arrive(lambda: self.full(zs, r), self.zsem + zs * 2 + r, is_near & (k != r))
                arrive_local(lambda: self.full(zs, r), self.zsem + zs * 2 + r, is_near & (k == r))
            for cs, cond in ((zs, is_far), (zo, True)):
                for j in (1, 2):
                    arrive(lambda: self.piece(cs, j - 1, dq ^ 3), self.xsem + cs * 4 + 1 + j, cond)

    q48, o48, f96, p192 = QR // QUAD, OR_ // QUAD, FR // QUAD, PR_ // QUAD

    def cols(r):
        return pl.ds(mo(r * DH, 128), DH)

    w_qkv = Weight(
        lambda: wq_in,
        lambda: wq_in.at[:, pl.ds(mo(dq * q48, 16), q48), :],
        lambda cs, r, q: WQ.at[:, pl.ds(mo(cs * QR + q * q48, 16), q48), cols(r)],
        lambda cs, r: WQ.at[:, pl.ds(mo(cs * QR, 16), QR), cols(r)],
        lambda cs, q: WQ.at[:, pl.ds(mo(cs * QR + q * q48, 16), q48), :],
    )
    w_out = Weight(
        lambda: wo_in,
        lambda: wo_in.at[pl.ds(mo(dq * o48, 16), o48), :],
        lambda cs, r, q: WO.at[pl.ds(mo(cs * OR_ + q * o48, 16), o48), cols(r)],
        lambda cs, r: WO.at[pl.ds(mo(cs * OR_, 16), OR_), cols(r)],
        lambda cs, q: WO.at[pl.ds(mo(cs * OR_ + q * o48, 16), o48), :],
    )
    FC = wf_in.shape[1]

    def fc_part(at0, n):
        return Weight(
            lambda: wf_in.at[:, pl.ds(at0, n)],
            lambda: wf_in.at[pl.ds(mo(dq * f96, 16), f96), pl.ds(at0, n)],
            lambda cs, r, q: WF.at[r, pl.ds(mo(q * f96, 16), f96), pl.ds(mo(cs * FC + at0, 128), n)],
            lambda cs, r: WF.at[r, :, pl.ds(mo(cs * FC + at0, 128), n)],
            lambda cs, q: WF.at[:, pl.ds(mo(q * f96, 16), f96), pl.ds(mo(cs * FC + at0, 128), n)],
        )

    def proj_part(at0, n):
        n4 = n // QUAD
        return Weight(
            lambda: wp_in.at[pl.ds(at0, n), :],
            lambda: wp_in.at[pl.ds(mo(at0 + dq * n4, 16), n4), :],
            lambda cs, r, q: WP.at[pl.ds(mo(cs * PR_ + at0 + q * n4, 16), n4), cols(r)],
            lambda cs, r: WP.at[pl.ds(mo(cs * PR_ + at0, 16), n), cols(r)],
            lambda cs, q: WP.at[pl.ds(mo(cs * PR_ + at0 + q * n4, 16), n4), :],
        )

    first = FC // 3
    w_fc, w_fc2 = fc_part(0, first), fc_part(first, FC - first)
    w_proj, w_proj2 = proj_part(0, first), proj_part(first, FC - first)

    stage = new_recv(2)
    pltpu.make_async_copy(x_in, H, rs.at[stage]).start()
    pltpu.make_async_copy(cot_in, ACC, rs.at[stage + 1]).start()
    bq, bv = bqv_in[0:1, :], bqv_in[1:2, :]
    gap = jnp.zeros_like(bq)
    misc_in[...] = jnp.concatenate(
        [
            bfc_in[...].reshape(1, D),
            jnp.where(zs == 0, jnp.concatenate([bq, gap, bv, gap], axis=1), jnp.concatenate([gap, bq, gap, bv], axis=1)),
            jnp.full((1, D), len_in[0].astype(F32)),
            jnp.full((1, D), len_in[1].astype(F32)),
            jnp.zeros((4, D), F32),
        ],
        axis=0,
    )
    misc_sem = new_recv(8)
    for dev in line:
        send(lambda: misc_in, lambda: MISC.at[k, z], misc_sem + k * 4 + z, dev)
    local(lambda: misc_in, lambda: MISC.at[k, z], misc_sem + k * 4 + z)
    w_qkv.push()
    pltpu.make_async_copy(x_in, H, rs.at[stage]).wait()
    XS[...] = H[...].astype(BF)
    half_rows = T // 2
    xh_sem, x_sem = new_recv(1), new_recv(4)
    part_of = lambda core: pl.ds(mo(core * half_rows, 16), half_rows)
    send(lambda: XS.at[:, part_of(1 - k)], lambda: XH, xh_sem, mate)
    for i in range(2):
        mine = is_near & (zs == i)
        src, dst = lambda i=i: XS.at[i, part_of(k)], lambda: XR.at[zs, part_of(k)]
        send(src, dst, x_sem + zs * 2 + k, at(d, zk, 2 * k + i), jnp.logical_not(mine))
        local(src, dst, x_sem + zs * 2 + k, mine)
    pltpu.make_async_copy(cot_in, ACC, rs.at[stage + 1]).wait()
    CS[...] = ACC[...].astype(BF)

    V8[...] = jnp.zeros_like(V8)
    SQ[...] = jnp.zeros_like(SQ)

    b_out, ln1_g, ln1_b, ln2_g, ln2_b, b_proj = (
        v[...].reshape(1, D) for v in (b_out, ln1_g, ln1_b, ln2_g, ln2_b, b_proj)
    )

    w_qkv.hop()
    arrive(lambda: XH, xh_sem)
    for i in range(2):
        send(lambda i=i: XH.at[i], dst, x_sem + zs * 2 + k, at(d, zk, 2 * (1 - k) + i))
    w_qkv.forward()
    w_qkv.relay()

    RB = 128
    a1_sem = new_recv(2)

    def rows_of(base, i, n):
        return pl.ds(mo(base + i * n, 16), n)

    for s in range(2):
        for core in range(2):
            here = is_near & (zs == s) & (k == core)
            arrive(lambda: XR.at[s, part_of(core)], x_sem + s * 2 + core, jnp.logical_not(here))
            arrive_local(lambda: XR.at[s, part_of(core)], x_sem + s * 2 + core, here)

        def first_norm(i, c):
            scaled, _ = norm_stats(XR[s, rows_of(0, i, RB), :].astype(F32))
            A1[rows_of(own + s * T, i, RB), :] = (scaled * ln1_g + ln1_b).astype(BF)
            return c

        lax.fori_loop(0, T // RB, first_norm, 0)
        mine = lambda s=s: A1.at[pl.ds(mo(own + s * T, 16), T), :]
        send(mine, mine, a1_sem + s, mate)

    for r in range(2):
        for c in range(4):
            here = (k == r) & (z == c)
            arrive(lambda: MISC.at[r, c], misc_sem + r * 4 + c, jnp.logical_not(here))
            arrive_local(lambda: MISC.at[r, c], misc_sem + r * 4 + c, here)
    pair_misc = MISC[0, 2 * k] + MISC[0, 2 * k + 1]
    bias_q, bias_v = pair_misc[1:2, :HC], pair_misc[1:2, HC:]
    length = MISC[zk, 0, pl.ds(2 + zs, 1), :][:, 0:1]

    w_qkv.ready()

    def project(base):
        rows = pl.ds(mo(base, 16), 2 * T)
        a = A1[rows, :]
        QKV[0, rows, :] = ((dot_t(a, WQ[0]) + bias_q).astype(BF).astype(F32) * (HEAD_DIM**-0.5)).astype(BF)
        QKV[1, rows, :] = dot_t(a, WQ[1]).astype(BF)
        QKV[2, rows, :] = (dot_t(a, WQ[2]) + bias_v).astype(BF)

    project(own)
    for s in range(2):
        arrive(lambda: A1.at[pl.ds(mo(other + s * T, 16), T), :], a1_sem + s)
    w_out.push()
    w_fc.push()
    project(other)

    key_place = lax.broadcasted_iota(jnp.int32, (L, 128), 0).astype(F32)
    KB[...] = jnp.where(key_place < length, 0.0, MASKED)

    QB = T
    NQ = L // QB
    low_lane = lax.broadcasted_iota(jnp.int32, (1, 128), 1) < HEAD_DIM
    low_row = lax.broadcasted_iota(jnp.int32, (128, 1), 0) < HEAD_DIM
    diag = lax.broadcasted_iota(jnp.int32, (QB, QB), 0) <= lax.broadcasted_iota(jnp.int32, (QB, QB), 1)

    def keep_lane(v, h):
        return jnp.where(low_lane if h == 0 else jnp.logical_not(low_lane), v, jnp.zeros_like(v))

    def scores_t(kp, qm, qb):
        kv = (qb + 1) * QB
        s = dot_t(kp[:kv], qm)
        kb = KB[0:kv, :]
        s = s + jnp.concatenate([kb] * (QB // 128), axis=1)
        last = jnp.where(diag, s[kv - QB :], MASKED)
        if qb == 0:
            return last
        return jnp.concatenate([s[: kv - QB], last], axis=0)

    def send_cot():
        return line_send(lambda i: CS.at[i], lambda i: GF.at[pl.ds(mo(z * T, 16), T), :])

    between = {
        (0, 3): (w_out.hop, w_fc2.push),
        (1, 0): (w_fc.hop,),
        (1, 2): (w_out.forward, w_proj.push),
        (1, 3): (w_fc.forward, w_fc2.hop),
        (2, 0): (w_out.relay, w_proj2.push),
        (2, 2): (w_fc.relay, w_proj.hop),
        (2, 3): (w_fc2.forward,),
    }

    def attend(p, c):
        lanes = pl.ds(mo(p * 128, 128), 128)
        kp, vp = QKV[1, :, lanes], QKV[2, :, lanes]
        vt = vp.T
        for qb in range(NQ):
            for (step, at_qb), work in between.items():
                if at_qb == qb:

                    @pl.when(p == step)
                    def _():
                        for do in work:
                            do()

            kv = (qb + 1) * QB
            qp = QKV[0, qb * QB : kv, lanes]
            parts = []
            for h in range(2):
                s = scores_t(kp, keep_lane(qp, h), qb)
                top = jnp.max(s, axis=0, keepdims=True)
                e = jnp.exp(s - top)
                total = jnp.sum(e, axis=0, keepdims=True)
                LSE[pl.ds(2 * p + h, 1), qb * QB : kv] = top + jnp.log(total)
                parts.append(dot(vt[:, :kv], e.astype(BF)) / total)
            CTX[qb * QB : kv, lanes] = jnp.where(low_row, parts[0], parts[1]).T.astype(BF)
        return c

    lax.fori_loop(0, HC // 128, attend, 0)
    w_proj2.hop()

    def split_sum(n, product):
        base = new_recv(2)
        PS[n] = product(pl.ds(mo(other, 16), 2 * T)).astype(BF).reshape(2, T, D)
        for s in range(2):
            send(lambda s=s: PS.at[n, s], lambda s=s: PR.at[n, s], base + s, mate)
        ACC[...] = product(pl.ds(mo(own, 16), 2 * T)).reshape(2, T, D)
        return base

    def split_wait(n, base, s):
        arrive(lambda: PR.at[n, s], base + s)

    w_out.ready()
    ex = split_sum(0, lambda rows: dot(CTX[rows, :], WO[...]))
    w_proj.forward()
    cot_sem = send_cot()
    a2_sem = new_recv(2)
    for s in range(2):
        split_wait(0, ex, s)

        def second_norm(i, c):
            rows = rows_of(0, i, RB)
            h = XR[s, rows, :].astype(F32) + ACC[s, rows, :] + PR[0, s, rows, :].astype(F32) + b_out
            H[s, rows, :] = h
            scaled, _ = norm_stats(h)
            A2[rows_of(own + s * T, i, RB), :] = (scaled * ln2_g + ln2_b).astype(BF)
            return c

        lax.fori_loop(0, T // RB, second_norm, 0)
        mine = lambda s=s: A2.at[pl.ds(mo(own + s * T, 16), T), :]
        send(mine, mine, a2_sem + s, mate)

    VF[...] = jnp.concatenate([MISC[0, 2 * k, 0:1, :], MISC[0, 2 * k + 1, 0:1, :]], axis=1)

    def hidden(base, start, width):
        rows = pl.ds(mo(base, 16), 2 * T)

        def body(i, c):
            cs = pl.ds(mo(i * FC + start, 128), width)
            u = dot(A2[rows, :], WF[:, :, cs].reshape(D, width)) + VF[:, cs]
            t = jnp.tanh(GELU_C * (u + GELU_A * u * u * u))
            M[rows, cs] = (0.5 * u * (1.0 + t)).astype(BF)
            SL[rows, cs] = (
                0.5 * (1.0 + t) + 0.5 * u * (1.0 - t * t) * GELU_C * (1.0 + 3.0 * GELU_A * u * u)
            ).astype(BF)
            return c

        lax.fori_loop(0, 2, body, 0)

    w_fc.ready()
    hidden(own, 0, first)
    w_fc2.relay()
    for s in range(2):
        arrive(lambda: A2.at[pl.ds(mo(other + s * T, 16), T), :], a2_sem + s)
    hidden(other, 0, first)
    w_proj2.forward()
    w_proj.relay()
    w_fc2.ready()
    hidden(own, first, FC - first)
    w_proj2.relay()
    hidden(other, first, FC - first)
    w_proj.ready()
    w_proj2.ready()
    ex = split_sum(1, lambda rows: dot(M[rows, :], WP[...]))

    gf_sem = new_recv(2)
    for s in range(2):
        line_wait(lambda i: GF.at[pl.ds(mo(own + i * T, 16), T), :], cot_sem, s)

        def mask_rows(i, c):
            rows = rows_of(own + s * T, i, RB)
            place = (lax.broadcasted_iota(jnp.int32, (RB, 1), 0) + (own + s * T + i * RB)).astype(F32)
            g = jnp.where(place < length, GF[rows, :].astype(F32), 0.0)
            GF[rows, :] = g.astype(BF)
            V8[V_BPROJ] += fold8(g)
            return c

        lax.fori_loop(0, T // RB, mask_rows, 0)
        mine = lambda s=s: GF.at[pl.ds(mo(own + s * T, 16), T), :]
        send(mine, mine, gf_sem + s, mate)

    for s in range(2):
        split_wait(1, ex, s)

        def output_rows(i, c):
            rows = rows_of(0, i, RB)
            LO[s, rows, :] = (H[s, rows, :] + ACC[s, rows, :] + PR[1, s, rows, :].astype(F32) + b_proj).astype(BF)
            return c

        lax.fori_loop(0, T // RB, output_rows, 0)
    lo_sem = line_send(lambda i: LO.at[i], lambda i: lo_out.at[i])

    for s in range(2):
        arrive(lambda: GF.at[pl.ds(mo(other + s * T, 16), T), :], gf_sem + s)


    class Part:
        def __init__(self, quarter, R, S, B, U, Z, E, slab, piece, place):
            self.quarter, self.R, self.S, self.B, self.U, self.Z, self.E = quarter, R, S, B, U, Z, E
            self.slab, self.piece, self.place = slab, piece, place
            self.raw, self.pair, self.zsem, self.end = new_recv(3), new_recv(1), new_recv(2), new_recv(4)

        def spread(self):
            for j in (1, 2, 3):
                send(lambda j=j: self.quarter(dq ^ j), lambda j=j: self.R.at[j - 1], self.raw + j - 1, quad[j - 1])

        def reduce(self):
            for j in (1, 2, 3):
                arrive(lambda: self.R.at[j - 1], self.raw + j - 1)
            G, (_, n, width) = self.quarter(dq), self.S.shape
            wide = lambda f: f if width <= D else jnp.concatenate([f] * (width // D), axis=1)
            factors = [wide(VP[dq ^ j, V_FACTOR : V_FACTOR + 1, :]) for j in range(QUAD)]
            steps = n // 16

            def add(i, c):
                a, rows = i // steps, pl.ds(mo(lax.rem(i, steps) * 16, 16), 16)
                v = G[a, rows, :].astype(F32) * factors[0]
                for j in (1, 2, 3):
                    v = v + self.R[j - 1, a, rows, :].astype(F32) * factors[j]
                self.S[a, rows, :] = v.astype(BF)
                return c

            lax.fori_loop(0, 2 * steps, add, 0)
            send(lambda: self.slab(1 - zs), lambda: self.B, self.pair, at(d, k, z ^ 1))

        def middle(self):
            arrive(lambda: self.B, self.pair)
            self.U[...] = (self.slab(zs)[...].astype(F32) + self.B[...].astype(F32)).astype(BF)
            for r in range(2):
                mine = (far == 0) & (r == k)
                piece = lambda r=r: self.piece(r)
                send(piece, lambda: self.Z.at[far], self.zsem + far, at(d, r, target), jnp.logical_not(mine))
                local(piece, lambda: self.Z.at[far], self.zsem + far, mine)

        def finish(self):
            arrive(lambda: self.Z.at[0], self.zsem, is_far)
            arrive_local(lambda: self.Z.at[0], self.zsem, is_near)
            arrive(lambda: self.Z.at[1], self.zsem + 1)
            self.E[...] = (self.Z[0].astype(F32) + self.Z[1].astype(F32)).astype(BF)
            for j in (1, 2, 3):
                send(lambda: self.E, lambda: self.place(dq), self.end + j, quad[j - 1])
            local(lambda: self.E, lambda: self.place(dq), self.end)

        def done(self):
            arrive_local(lambda: self.place(dq), self.end)
            for j in (1, 2, 3):
                arrive(lambda: self.place(dq ^ j), self.end + j)

    g_proj = Part(
        lambda q: GWP.at[:, pl.ds(mo(q * p192, 16), p192), :], RP, SPW, BP, UP, ZP, EP,
        lambda cs: SPW.at[cs],
        lambda r: UP.at[:, cols(r)],
        lambda q: gp_out.at[pl.ds(mo(q * p192, 16), p192), :],
    )
    g_out = Part(
        lambda q: GWO.at[:, pl.ds(mo(q * o48, 16), o48), :], RO, SOW, BO, UO, ZO, EO,
        lambda cs: SOW.at[cs],
        lambda r: UO.at[:, cols(r)],
        lambda q: go_out.at[pl.ds(mo(q * o48, 16), o48), :],
    )

    def fc_grad(R, S, B, U, Z, E, start, n):
        return Part(
            lambda q: GWF.at[:, pl.ds(mo(start + q * n, 16), n), :], R, S, B, U, Z, E,
            lambda cs: S.at[:, :, pl.ds(mo(cs * FC, 128), FC)],
            lambda r: U.at[r],
            lambda q: gf_out.at[pl.ds(mo(start + q * n, 16), n), :],
        )

    g_fc = fc_grad(RF, SFW, BF1, UF, ZF, EF, 0, 128 // QUAD)
    g_fc2 = fc_grad(RF2, SFW2, BF2, UF2, ZF2, EF2, 128, (FR - 128) // QUAD)

    def qkv_grad(i):
        return Part(
            lambda q: GWQ.at[i, :, pl.ds(mo(q * q48, 16), q48), :],
            RQ.at[i], SQW.at[i], BQ.at[i], UQ.at[i], ZQ.at[i], EQ.at[i],
            lambda cs: SQW.at[i, cs],
            lambda r: UQ.at[i, :, cols(r)],
            lambda q: gq_out.at[i, pl.ds(mo(q * q48, 16), q48), :],
        )

    g_qkv = [qkv_grad(i) for i in range(3)]

    def grad_proj(i, c):
        cs = pl.ds(mo(i * (FC // 2), 128), FC // 2)
        g = t_dot(M[:, cs], GF[...])
        SQ[...] += fold8(g * g)
        GWP[i // 2, pl.ds(mo(lax.rem(i, 2) * (FC // 2), 16), FC // 2), :] = g.astype(BF)
        return c

    lax.fori_loop(0, 4, grad_proj, 0)
    g_proj.spread()

    NB = 512
    NN = FH // NB

    def grad_hidden(i, c):
        rows = pl.ds(mo(i // NN * 2 * T, 16), 2 * T)
        cs = pl.ds(mo(lax.rem(i, NN) * NB, 128), NB)
        g = dot_t(GF[rows, :], WP[cs, :]) * SL[rows, cs].astype(F32)
        low = g.astype(BF)
        SL[rows, cs] = low
        VF[:, cs] = jnp.where(i < NN, 0.0, VF[:, cs]) + jnp.sum(low.astype(F32), axis=0, keepdims=True)
        return c

    lax.fori_loop(0, 2 * NN, grad_hidden, 0)
    ex = split_sum(2, lambda rows: dot_t(SL[rows, :], WF[...].reshape(D, FH)))

    ga_sem = new_recv(2)
    for s in range(2):
        split_wait(2, ex, s)

        def second_back(i, c):
            rows = rows_of(0, i, RB)
            full = rows_of(own + s * T, i, RB)
            up = ACC[s, rows, :] + PR[2, s, rows, :].astype(F32)
            scaled, inverse = norm_stats(H[s, rows, :])
            through = up * ln2_g
            V8[V_LN2G] += fold8(up * scaled)
            V8[V_LN2B] += fold8(up)
            g = GF[full, :].astype(F32) + inverse * (
                through
                - jnp.mean(through, axis=-1, keepdims=True)
                - scaled * jnp.mean(through * scaled, axis=-1, keepdims=True)
            )
            V8[V_BOUT] += fold8(g)
            H[s, rows, :] = g
            GA[full, :] = g.astype(BF)
            return c

        lax.fori_loop(0, T // RB, second_back, 0)
        mine = lambda s=s: GA.at[pl.ds(mo(own + s * T, 16), T), :]
        send(mine, mine, ga_sem + s, mate)
    for s in range(2):
        arrive(lambda: GA.at[pl.ds(mo(other + s * T, 16), T), :], ga_sem + s)

    GCTX[...] = dot_t(GA[...], WO[...]).astype(BF)
    half = HC // 2
    g = t_dot(CTX[...], GA[...])
    SQ[...] += fold8(g * g)
    GWO[0] = g[:half].astype(BF)
    GWO[1] = g[half:].astype(BF)
    g_out.spread()

    def grad_fc(start, n):
        g = t_dot(jnp.concatenate([A2[:, start : start + n], A2[:, FR + start : FR + start + n]], axis=1), SL[...])
        q = fold8(g * g)
        SQ[...] += q[:, :D] + q[:, D:]
        GWF[:, start : start + n, :] = g.astype(BF).reshape(2, n, FH)

    grad_fc(0, 128)
    g_fc.spread()

    def attend_back(p):
        lanes = pl.ds(mo(p * 128, 128), 128)
        kp, vp = QKV[1, :, lanes], QKV[2, :, lanes]
        kt = kp.T
        DK[...] = jnp.zeros_like(DK)
        DV[...] = jnp.zeros_like(DV)
        for qb in range(NQ):
            kv = (qb + 1) * QB
            qp = QKV[0, qb * QB : kv, lanes]
            do = GCTX[qb * QB : kv, lanes]
            dqt = []
            for h in range(2):
                qm, dm = keep_lane(qp, h), keep_lane(do, h)
                pt = jnp.exp(scores_t(kp, qm, qb) - LSE[pl.ds(2 * p + h, 1), qb * QB : kv])
                gp = dot_t(vp[:kv], dm)
                both = pt * gp
                gs = (both - pt * jnp.sum(both, axis=0, keepdims=True)).astype(BF)
                DV[0:kv, :] += dot(pt.astype(BF), dm)
                DK[0:kv, :] += dot(gs, qm)
                dqt.append(dot(kt[:, :kv], gs))
            GQKV[0, qb * QB : kv, lanes] = (
                jnp.where(low_row, dqt[0], dqt[1]).T * (HEAD_DIM**-0.5)
            ).astype(BF)
        GQKV[1, :, lanes] = DK[...].astype(BF)
        GQKV[2, :, lanes] = DV[...].astype(BF)

    def attend_back_step(p, c):
        attend_back(p)
        return c

    lax.fori_loop(0, HC // 128, attend_back_step, 0)

    def grad_norm_in(rows):
        return dot(GQKV[0, rows, :], WQ[0]) + dot(GQKV[1, rows, :], WQ[1]) + dot(GQKV[2, rows, :], WQ[2])

    ex = split_sum(3, grad_norm_in)
    grad_fc(128, FR - 128)
    for s in range(2):
        split_wait(3, ex, s)

        def first_back(i, c):
            rows = rows_of(0, i, RB)
            up = ACC[s, rows, :] + PR[3, s, rows, :].astype(F32)
            scaled, inverse = norm_stats(XR[s, rows, :].astype(F32))
            through = up * ln1_g
            V8[V_LN1G] += fold8(up * scaled)
            V8[V_LN1B] += fold8(up)
            g = H[s, rows, :] + inverse * (
                through
                - jnp.mean(through, axis=-1, keepdims=True)
                - scaled * jnp.mean(through * scaled, axis=-1, keepdims=True)
            )
            GI[s, rows, :] = g.astype(BF)
            return c

        lax.fori_loop(0, T // RB, first_back, 0)

    gi_sem = line_send(lambda i: GI.at[i], lambda i: gi_out.at[i])

    def grad_qkv(i, c):
        g = t_dot(GQKV[i], A1[...])
        SQ[...] += fold8(g * g)
        low = g.astype(BF)
        GWQ[i, 0] = low[:half]
        GWQ[i, 1] = low[half:]
        return c

    lax.fori_loop(0, 3, grad_qkv, 0)
    VK[k] = jnp.zeros(VK.shape[1:], F32)
    for i in range(6):
        VK[k, i : i + 1, :] = jnp.sum(V8[i], axis=0, keepdims=True)
    VK[k, V_BQV : V_BQV + 1, :] = jnp.concatenate(
        [jnp.sum(GQKV[i].astype(F32), axis=0, keepdims=True) for i in (0, 2)], axis=1
    )
    VK[k, V_BFC : V_BFC + 1, :] = VF[:, :D]
    VK[k, V_BFC + 1 : V_BFC + 2, :] = VF[:, D:]
    VK[k, V_SQ : V_SQ + 1, :] = jnp.sum(SQ[...], axis=0, keepdims=True)
    vk_sem = new_recv(1)
    send(lambda: VK.at[k], lambda: VK.at[k], vk_sem, mate)
    arrive(lambda: VK.at[1 - k], vk_sem)
    va, vb = VK[0], VK[1]
    pack = jnp.concatenate([va[0:6] + vb[0:6], va[6:9], vb[6:9]], axis=0)
    squares = jnp.sum(jnp.sum(pack * pack, axis=0, keepdims=True) + va[9:10] + vb[9:10], axis=1, keepdims=True)
    norm = jnp.sqrt(squares)
    factor = CLIP_BOUND / jnp.maximum(norm, CLIP_BOUND)
    wide = lambda v: jnp.broadcast_to(v, (1, D))
    VP[dq] = jnp.concatenate([pack, wide(factor), wide(norm), jnp.zeros((2, D), F32)], axis=0)
    vp_sem = new_recv(3)
    for j in (1, 2, 3):
        send(lambda: VP.at[dq], lambda: VP.at[dq], vp_sem + j - 1, quad[j - 1])
    for part in (g_fc2, *g_qkv):
        part.spread()

    for j in (1, 2, 3):
        arrive(lambda: VP.at[dq ^ j], vp_sem + j - 1)

    total = jnp.zeros((12, D), F32)
    for q in range(QUAD):
        total = total + VP[q, 0:12, :] * VP[q, V_FACTOR : V_FACTOR + 1, :]
    VZ[z] = jnp.concatenate([total, VP[dq, V_FACTOR:, :]], axis=0)
    vz_sem = new_recv(3)
    for j in (1, 2, 3):
        send(lambda: VZ.at[z], lambda: VZ.at[z], vz_sem + j - 1, at(d, k, z ^ j))

    order = [g_proj, g_out, g_fc, g_fc2, *g_qkv]
    for i, part in enumerate(order):
        part.reduce()
        if i >= 1:
            order[i - 1].middle()
        if i >= 2:
            order[i - 2].finish()
    order[-1].middle()
    for part in order[-2:]:
        part.finish()

    for j in (1, 2, 3):
        arrive(lambda: VZ.at[z ^ j], vz_sem + j - 1)
    total = VZ[0] + VZ[1] + VZ[2] + VZ[3]
    vec_out[0:6, :] = total[0:6]
    V8[0, 0:6, :] = total[6:12]
    vec_out[6:7, :] = V8[0, pl.ds(V_BFC - V_BQV + 3 * zk + zs, 1), :]
    pair = V8[0, pl.ds(3 * zk, 1), :]
    spare = jnp.zeros((1, D - QR), F32)
    for i in range(2):
        a, b = pair[:, i * HC : i * HC + QR], pair[:, i * HC + QR : (i + 1) * HC]
        vec_out[7 + i : 8 + i, :] = jnp.concatenate([jnp.where(zs == 0, a, b), spare], axis=1)
    vec_out[9:10, :] = VZ[2 * k, V_NORM : V_NORM + 1, :]
    vec_out[10:11, :] = VZ[2 * k + 1, V_NORM : V_NORM + 1, :]
    vec_out[11:12, :] = jnp.zeros((1, D), F32)

    for part in order:
        part.done()
    for i in range(2):
        line_wait(lambda i: lo_out.at[i], lo_sem, i)
        line_wait(lambda i: gi_out.at[i], gi_sem, i)
    for cond, make in pending:
        when(cond, lambda: make().wait_send())


def shards(
    layer_in, w_qkv, b_qv, w_out, b_out, ln1_g, ln1_b, ln2_g, ln2_b, w_fc, b_fc, w_proj, b_proj, lengths, cotangent
):
    E, T, D = layer_in.shape
    n_col, n_row = lax.axis_size("col"), lax.axis_size("row")
    assert lax.axis_size("dp") == QUAD and n_col == 4 and n_row % 2 == 0
    pairs = n_row // 2
    r = lax.axis_index("row")
    core = lax.rem(r, 2)
    half_rows = w_fc.shape[0] * pairs

    def halves(w, axis):
        if pairs == 1:
            return w
        whole = lax.all_gather(w, "row", axis=axis, tiled=True)
        return lax.dynamic_slice_in_dim(whole, core * half_rows, half_rows, axis)

    w_qkv, w_out, w_fc, w_proj = halves(w_qkv, 0), halves(w_out, 1), halves(w_fc, 0), halves(w_proj, 1)
    L = T * n_col
    HQ = w_qkv.shape[2]
    HC = HQ * n_col // 2
    FQ = w_fc.shape[1]
    FH = FQ * n_col // 2
    DH = w_fc.shape[0]
    wq_t = jnp.transpose(w_qkv, (1, 2, 0))
    q48, o48, p192 = HQ // QUAD, HQ // QUAD, FQ // QUAD
    fa, fb = 128 // QUAD, (DH - 128) // QUAD

    anyspec = pl.BlockSpec(memory_space=pl.ANY)
    vm = pl.BlockSpec(memory_space=pltpu.VMEM)
    V = pltpu.VMEM
    outs = pl.pallas_call(
        kernel,
        name="layer",
        out_shape=(
            jax.ShapeDtypeStruct((E, T, D), BF),
            jax.ShapeDtypeStruct((E, T, D), BF),
            jax.ShapeDtypeStruct((3, HQ, DH), BF),
            jax.ShapeDtypeStruct((HQ, DH), BF),
            jax.ShapeDtypeStruct((DH, FQ), BF),
            jax.ShapeDtypeStruct((FQ, DH), BF),
            jax.ShapeDtypeStruct((12, D), F32),
        ),
        in_specs=[anyspec] * 6 + [vm, vm, pl.BlockSpec(memory_space=pltpu.SMEM)] + [vm] * 6,
        out_specs=(anyspec,) * 6 + (vm,),
        scratch_shapes=[
            V((2, T, D), BF),
            V((2, T // 2, D), BF),
            V((2, T, D), BF),
            V((8, D), F32),
            V((2, T, D), BF),
            V((2, T, D), F32),
            V((L, D), BF),
            V((3, HC, D), BF),
            V((HC, D), BF),
            V((2, DH, FH), BF),
            V((FH, D), BF),
            V((2, n_col, 8, D), F32),
            V((3, L, HC), BF),
            V((L, HC), BF),
            V((8, L), F32),
            V((L, 128), F32),
            V((2, T, D), F32),
            V((4, 2, T, D), BF),
            V((4, 2, T, D), BF),
            V((L, D), BF),
            V((L, FH), BF),
            V((L, FH), BF),
            V((L, D), BF),
            V((L, D), BF),
            V((L, HC), BF),
            V((3, L, HC), BF),
            V((L, 128), F32),
            V((L, 128), F32),
            V((2, T, D), BF),
            V((2, T, D), BF),
            V((6, 8, D), F32),
            V((8, D), F32),
            V((1, FH), F32),
            V((2, 16, D), F32),
            V((QUAD, 16, D), F32),
            V((n_col, 16, D), F32),
            V((3, 2, HQ, D), BF),
            V((2, HQ, D), BF),
            V((2, DH, FH), BF),
            V((2, FQ, D), BF),
            V((3, 3, 2, q48, D), BF),
            V((3, 2, o48, D), BF),
            V((3, 2, fa, FH), BF),
            V((3, 2, fb, FH), BF),
            V((3, 2, p192, D), BF),
            V((3, 2, q48, D), BF),
            V((2, o48, D), BF),
            V((2, fa, FH), BF),
            V((2, fb, FH), BF),
            V((2, p192, D), BF),
            *[
                V(shape, BF)
                for _ in "BU"
                for shape in ((3, q48, D), (o48, D), (2, fa, FQ), (2, fb, FQ), (p192, D))
            ],
            V((3, 2, q48, DH), BF),
            V((2, o48, DH), BF),
            V((2, fa, FQ), BF),
            V((2, fb, FQ), BF),
            V((2, p192, DH), BF),
            V((3, q48, DH), BF),
            V((o48, DH), BF),
            V((fa, FQ), BF),
            V((fb, FQ), BF),
            V((p192, DH), BF),
            pltpu.SemaphoreType.DMA((200,)),
            pltpu.SemaphoreType.DMA((200,)),
        ],
        compiler_params=pltpu.CompilerParams(
            collective_id=0, has_side_effects=True, vmem_limit_bytes=63 * 2**20
        ),
    )(
        layer_in, cotangent, wq_t, w_out, w_fc, w_proj, b_fc, b_qv, lengths,
        b_out, ln1_g, ln1_b, ln2_g, ln2_b, b_proj,
    )
    lo, gi, gq, go, gf, gp, vec = outs
    norms = vec[9:11, 0]
    lo, gi, gq, go, gf, gp = (v.astype(F32) for v in (lo, gi, gq, go, gf, gp))
    gq = jnp.transpose(gq, (2, 0, 1))
    if pairs > 1:
        groups = [[2 * p + q for p in range(pairs)] for q in range(2)]
        cores = [[2 * p, 2 * p + 1] for p in range(pairs)]
        gq, go, gf, gp, vec = (
            lax.psum(v, "row", axis_index_groups=groups) for v in (gq, go, gf, gp, vec)
        )

        def share(v, axis):
            whole = lax.all_gather(v, "row", axis=axis, tiled=True, axis_index_groups=cores)
            part = whole.shape[axis] // n_row
            return lax.dynamic_slice_in_dim(whole, r * part, part, axis)

        gq, go, gf, gp = share(gq, 0), share(go, 1), share(gf, 0), share(gp, 1)
    return (
        lo, gi, norms, gq, vec[7:9, :HQ], go,
        vec[V_BOUT], vec[V_LN1G], vec[V_LN1B], vec[V_LN2G], vec[V_LN2B],
        gf, vec[6], gp, vec[V_BPROJ],
    )


def solution(mesh):
    in_specs = (
        P(("dp", "row"), "col", None),
        P("row", None, "col"),
        P(None, "col"),
        P("col", "row"),
        P(),
        P(),
        P(),
        P(),
        P(),
        P("row", "col"),
        P("col"),
        P("col", "row"),
        P(),
        P(("dp", "row")),
        P(("dp", "row"), "col", None),
    )
    out_specs = (
        P(("dp", "row"), "col", None),
        P(("dp", "row"), "col", None),
        P(("dp", "row")),
        P("row", None, "col"),
        P(None, "col"),
        P("col", "row"),
        P(),
        P(),
        P(),
        P(),
        P(),
        P("row", "col"),
        P("col"),
        P("col", "row"),
        P(),
    )
    return jax.shard_map(shards, mesh=mesh, in_specs=in_specs, out_specs=out_specs, check_vma=False)
```

```python
import functools

import jax
import jax.numpy as jnp
from jax import lax
from jax.experimental import pallas as pl
from jax.experimental.pallas import tpu as pltpu
from jax.sharding import PartitionSpec as P

MESH = pl.DeviceIdType.MESH
EPSILON = 1e-05
CLIP_BOUND = 1.0
GELU_C = 0.7978845608028654
GELU_A = 0.044715
MASKED = -1e30
HEAD_DIM = 64
QUAD = 4
BF = jnp.bfloat16
F32 = jnp.float32

V_BOUT, V_LN1G, V_LN1B, V_LN2G, V_LN2B, V_BPROJ, V_BQV, V_BFC, V_SQ = 0, 1, 2, 3, 4, 5, 6, 7, 9
V_NORM = 12


def dot(a, b):
    return lax.dot_general(a, b, (((1,), (0,)), ((), ())), preferred_element_type=F32)


def dot_t(a, b):
    return lax.dot_general(a, b, (((1,), (1,)), ((), ())), preferred_element_type=F32)


def t_dot(a, b):
    return lax.dot_general(a, b, (((0,), (0,)), ((), ())), preferred_element_type=F32)


def fold8(v):
    return jnp.sum(v.reshape(v.shape[0] // 8, 8, v.shape[1]), axis=0)


def norm_stats(v):
    center = v - jnp.mean(v, axis=-1, keepdims=True)
    inverse = lax.rsqrt(jnp.mean(center * center, axis=-1, keepdims=True) + EPSILON)
    return center * inverse, inverse


def kernel(
    x_in, cot_in, wq_in, wo_in, wf_in, wp_in, bfc_in, bqv_in, len_in, b_out, ln1_g, ln1_b, ln2_g, ln2_b, b_proj,
    lo_out, gi_out, gq_out, go_out, gf_out, gp_out, vec_out,
    XS, XH, CS, misc_in, XR, H, A1, WQ, WO, WF, WP, MISC, QKV, CTX, LSE, KB, ACC,
    PS, PR, A2, M, SL, GF, GA, GCTX, GQKV, DK, DV, LO, GI,
    V8, SQ, VF, VK, FAC, VP, VZ,
    GWQ, GWO, GWF, GWF2, GWP, RP, XQ, XO, XF, XF2, OQ, OO, OF, OF2, YQ, YO, YF, YF2, SQW, SOW, SFW, SFW2, SPW, BQ, BO, BF1, BF2, BP, UQ, UO, UF, UF2, UP, ZQ, ZO, ZF, ZF2, ZP, EQ, EO, EF, EF2, EP,
    ss, rs,
):
    d, row, z = lax.axis_index("dp"), lax.axis_index("row"), lax.axis_index("col")
    k = lax.rem(row, 2)
    dq = d

    def at(plane, core, place):
        return (plane, row - k + core, place)

    zk, zs = z // 2, lax.rem(z, 2)
    L, D = A1.shape
    T = XR.shape[1]
    HC = CTX.shape[1]
    FH = M.shape[1]
    QR, OR_, FR, PR_ = wq_in.shape[1], wo_in.shape[0], wf_in.shape[0], wp_in.shape[0]
    DH = wo_in.shape[1]
    own, other = k * 2 * T, (1 - k) * 2 * T

    def mo(v, n):
        return pl.multiple_of(v, n)

    def when(cond, f):
        if cond is True:
            f()
        else:
            pl.when(cond)(f)

    n_send = [0]
    n_recv = [0]
    pending = []

    def new_send():
        n_send[0] += 1
        assert n_send[0] <= ss.shape[0]
        return n_send[0] - 1

    def new_recv(n):
        n_recv[0] += n
        assert n_recv[0] <= rs.shape[0]
        return n_recv[0] - n

    def send(src, dst, rsem, dev, cond=True):
        sem = new_send()

        def make():
            return pltpu.make_async_remote_copy(
                src(),
                dst(),
                ss.at[sem],
                rs.at[rsem() if callable(rsem) else rsem],
                device_id=dev() if callable(dev) else dev,
                device_id_type=MESH,
            )

        when(cond, lambda: make().start())
        pending.append((cond, make))

    def local(src, dst, rsem, cond=True):
        when(cond, lambda: pltpu.make_async_copy(src(), dst(), rs.at[rsem]).start())

    def arrive(dst, rsem, cond=True):
        def f():
            pltpu.make_async_remote_copy(
                dst(), dst(), ss.at[0], rs.at[rsem], device_id=at(d, k, z), device_id_type=MESH
            ).wait_recv()

        when(cond, f)

    def arrive_local(dst, rsem, cond=True):
        when(cond, lambda: pltpu.make_async_copy(dst(), dst(), rs.at[rsem]).wait())

    mate = at(d, 1 - k, z)
    quad = [at(d ^ j, k, z) for j in (1, 2, 3)]

    barrier = pltpu.get_barrier_semaphore()
    line = [at(d, k, z ^ j) for j in (1, 2, 3)] + [at(d, 1 - k, z ^ j) for j in (0, 1, 2, 3)]
    for dev in quad + line:
        pl.semaphore_signal(barrier, inc=1, device_id=dev, device_id_type=MESH)
    pl.semaphore_wait(barrier, len(quad) + len(line))

    def line_send(src, dst, parts=(0, 1), base=None):
        base = new_recv(2) if base is None else base
        for i in parts:
            mine = (zk == k) & (2 * k + i == z)
            send(lambda i=i: src(i), lambda: dst(zs), base + zs, at(d, zk, 2 * k + i), jnp.logical_not(mine))
            local(lambda i=i: src(i), lambda: dst(zs), base + zs, mine)
        return base

    def line_wait(dst, base, i):
        mine = (zk == k) & (2 * k + i == z)
        arrive(lambda: dst(i), base + i, jnp.logical_not(mine))
        arrive_local(lambda: dst(i), base + i, mine)

    far = lax.rem(k + zk, 2)
    target = z ^ (2 * far)
    is_near, is_far = far == 0, far == 1
    zo = 1 - zs

    class Weight:
        def __init__(self, src, src_quarter, piece, full, slab):
            self.src, self.src_quarter, self.piece, self.full, self.slab = src, src_quarter, piece, full, slab
            self.zsem, self.xsem = new_recv(4), new_recv(8)

        def push(self):
            sem = lambda: self.zsem + zs * 2 + k
            for j in (2, 1):
                send(self.src_quarter, lambda: self.piece(zs, k, dq), sem, lambda j=j: at(d, zk, z ^ j))
            send(self.src, lambda: self.full(zs, k), sem, mate, is_far)
            local(self.src, lambda: self.full(zs, k), self.zsem + zs * 2 + k, is_near)

        def spread(self, cs, cond):
            mine = lambda: self.slab(cs, dq)
            for j in (1, 2):
                send(mine, mine, lambda j=j: self.xsem + cs * 4 + j - 1, quad[j - 1], cond)

        def hop(self):
            for r in range(2):
                arrive(lambda: self.piece(zo, r, dq), self.zsem + zo * 2 + r, is_near)
                arrive(lambda: self.piece(zs, r, dq), self.zsem + zs * 2 + r, is_far)
                mine = lambda r=r: self.piece(zs, r, dq)
                send(mine, mine, lambda r=r: self.zsem + zs * 2 + r, lambda: at(d, k, z ^ 1), is_far)
            self.spread(zo, is_near)
            self.spread(zs, is_far)

        def forward(self):
            for r in range(2):
                arrive(lambda: self.piece(zo, r, dq), self.zsem + zo * 2 + r, is_far)
            self.spread(zo, is_far)

        def relay(self):
            for cs, cond in ((zs, is_far), (zo, True)):
                for j in (1, 2):
                    arrive(lambda: self.slab(cs, dq ^ j), self.xsem + cs * 4 + j - 1, cond)
                    half = lambda cs=cs, j=j: self.piece(cs, j - 1, dq ^ j)
                    send(half, half, lambda cs=cs, j=j: self.xsem + cs * 4 + 1 + j, quad[2 - j], cond)

        def ready(self):
            for r in range(2):
                arrive(lambda: self.full(zs, r), self.zsem + zs * 2 + r, is_near & (k != r))
                arrive_local(lambda: self.full(zs, r), self.zsem + zs * 2 + r, is_near & (k == r))
            for cs, cond in ((zs, is_far), (zo, True)):
                for j in (1, 2):
                    arrive(lambda: self.piece(cs, j - 1, dq ^ 3), self.xsem + cs * 4 + 1 + j, cond)

    q48, o48, f96, p192 = QR // QUAD, OR_ // QUAD, FR // QUAD, PR_ // QUAD

    def cols(r):
        return pl.ds(mo(r * DH, 128), DH)

    w_qkv = Weight(
        lambda: wq_in,
        lambda: wq_in.at[:, pl.ds(mo(dq * q48, 16), q48), :],
        lambda cs, r, q: WQ.at[:, pl.ds(mo(cs * QR + q * q48, 16), q48), cols(r)],
        lambda cs, r: WQ.at[:, pl.ds(mo(cs * QR, 16), QR), cols(r)],
        lambda cs, q: WQ.at[:, pl.ds(mo(cs * QR + q * q48, 16), q48), :],
    )
    w_out = Weight(
        lambda: wo_in,
        lambda: wo_in.at[pl.ds(mo(dq * o48, 16), o48), :],
        lambda cs, r, q: WO.at[pl.ds(mo(cs * OR_ + q * o48, 16), o48), cols(r)],
        lambda cs, r: WO.at[pl.ds(mo(cs * OR_, 16), OR_), cols(r)],
        lambda cs, q: WO.at[pl.ds(mo(cs * OR_ + q * o48, 16), o48), :],
    )
    FC = wf_in.shape[1]

    def fc_part(at0, n):
        return Weight(
            lambda: wf_in.at[:, pl.ds(at0, n)],
            lambda: wf_in.at[pl.ds(mo(dq * f96, 16), f96), pl.ds(at0, n)],
            lambda cs, r, q: WF.at[r, pl.ds(mo(q * f96, 16), f96), pl.ds(mo(cs * FC + at0, 128), n)],
            lambda cs, r: WF.at[r, :, pl.ds(mo(cs * FC + at0, 128), n)],
            lambda cs, q: WF.at[:, pl.ds(mo(q * f96, 16), f96), pl.ds(mo(cs * FC + at0, 128), n)],
        )

    def proj_part(at0, n):
        n4 = n // QUAD
        return Weight(
            lambda: wp_in.at[pl.ds(at0, n), :],
            lambda: wp_in.at[pl.ds(mo(at0 + dq * n4, 16), n4), :],
            lambda cs, r, q: WP.at[pl.ds(mo(cs * PR_ + at0 + q * n4, 16), n4), cols(r)],
            lambda cs, r: WP.at[pl.ds(mo(cs * PR_ + at0, 16), n), cols(r)],
            lambda cs, q: WP.at[pl.ds(mo(cs * PR_ + at0 + q * n4, 16), n4), :],
        )

    first = FC // 3
    w_fc, w_fc2 = fc_part(0, first), fc_part(first, FC - first)
    w_proj, w_proj2 = proj_part(0, first), proj_part(first, FC - first)

    stage = new_recv(2)
    pltpu.make_async_copy(x_in, H, rs.at[stage]).start()
    pltpu.make_async_copy(cot_in, ACC, rs.at[stage + 1]).start()
    bq, bv = bqv_in[0:1, :], bqv_in[1:2, :]
    gap = jnp.zeros_like(bq)
    misc_in[...] = jnp.concatenate(
        [
            bfc_in[...].reshape(1, D),
            jnp.where(zs == 0, jnp.concatenate([bq, gap, bv, gap], axis=1), jnp.concatenate([gap, bq, gap, bv], axis=1)),
            jnp.full((1, D), len_in[0].astype(F32)),
            jnp.full((1, D), len_in[1].astype(F32)),
            jnp.zeros((4, D), F32),
        ],
        axis=0,
    )
    misc_sem = new_recv(8)
    for dev in line:
        send(lambda: misc_in, lambda: MISC.at[k, z], misc_sem + k * 4 + z, dev)
    local(lambda: misc_in, lambda: MISC.at[k, z], misc_sem + k * 4 + z)
    w_qkv.push()
    pltpu.make_async_copy(x_in, H, rs.at[stage]).wait()
    XS[...] = H[...].astype(BF)
    half_rows = T // 2
    xh_sem, x_sem = new_recv(1), new_recv(4)
    part_of = lambda core: pl.ds(mo(core * half_rows, 16), half_rows)
    send(lambda: XS.at[:, part_of(1 - k)], lambda: XH, xh_sem, mate)
    for i in range(2):
        mine = is_near & (zs == i)
        src, dst = lambda i=i: XS.at[i, part_of(k)], lambda: XR.at[zs, part_of(k)]
        send(src, dst, x_sem + zs * 2 + k, at(d, zk, 2 * k + i), jnp.logical_not(mine))
        local(src, dst, x_sem + zs * 2 + k, mine)
    pltpu.make_async_copy(cot_in, ACC, rs.at[stage + 1]).wait()
    CS[...] = ACC[...].astype(BF)

    V8[...] = jnp.zeros_like(V8)
    SQ[...] = jnp.zeros_like(SQ)

    b_out, ln1_g, ln1_b, ln2_g, ln2_b, b_proj = (
        v[...].reshape(1, D) for v in (b_out, ln1_g, ln1_b, ln2_g, ln2_b, b_proj)
    )

    w_qkv.hop()
    arrive(lambda: XH, xh_sem)
    for i in range(2):
        send(lambda i=i: XH.at[i], dst, x_sem + zs * 2 + k, at(d, zk, 2 * (1 - k) + i))
    w_qkv.forward()
    w_qkv.relay()

    RB = 128
    a1_sem = new_recv(2)

    def rows_of(base, i, n):
        return pl.ds(mo(base + i * n, 16), n)

    for s in range(2):
        for core in range(2):
            here = is_near & (zs == s) & (k == core)
            arrive(lambda: XR.at[s, part_of(core)], x_sem + s * 2 + core, jnp.logical_not(here))
            arrive_local(lambda: XR.at[s, part_of(core)], x_sem + s * 2 + core, here)

        def first_norm(i, c):
            scaled, _ = norm_stats(XR[s, rows_of(0, i, RB), :].astype(F32))
            A1[rows_of(own + s * T, i, RB), :] = (scaled * ln1_g + ln1_b).astype(BF)
            return c

        lax.fori_loop(0, T // RB, first_norm, 0)
        mine = lambda s=s: A1.at[pl.ds(mo(own + s * T, 16), T), :]
        send(mine, mine, a1_sem + s, mate)

    for r in range(2):
        for c in range(4):
            here = (k == r) & (z == c)
            arrive(lambda: MISC.at[r, c], misc_sem + r * 4 + c, jnp.logical_not(here))
            arrive_local(lambda: MISC.at[r, c], misc_sem + r * 4 + c, here)
    pair_misc = MISC[0, 2 * k] + MISC[0, 2 * k + 1]
    bias_q, bias_v = pair_misc[1:2, :HC], pair_misc[1:2, HC:]
    length = MISC[zk, 0, pl.ds(2 + zs, 1), :][:, 0:1]

    w_qkv.ready()

    def project(base):
        rows = pl.ds(mo(base, 16), 2 * T)
        a = A1[rows, :]
        QKV[0, rows, :] = ((dot_t(a, WQ[0]) + bias_q).astype(BF).astype(F32) * (HEAD_DIM**-0.5)).astype(BF)
        QKV[1, rows, :] = dot_t(a, WQ[1]).astype(BF)
        QKV[2, rows, :] = (dot_t(a, WQ[2]) + bias_v).astype(BF)

    project(own)
    for s in range(2):
        arrive(lambda: A1.at[pl.ds(mo(other + s * T, 16), T), :], a1_sem + s)
    w_out.push()
    w_fc.push()
    project(other)

    key_place = lax.broadcasted_iota(jnp.int32, (L, 128), 0).astype(F32)
    KB[...] = jnp.where(key_place < length, 0.0, MASKED)

    QB = T
    NQ = L // QB
    low_lane = lax.broadcasted_iota(jnp.int32, (1, 128), 1) < HEAD_DIM
    low_row = lax.broadcasted_iota(jnp.int32, (128, 1), 0) < HEAD_DIM
    diag = lax.broadcasted_iota(jnp.int32, (QB, QB), 0) <= lax.broadcasted_iota(jnp.int32, (QB, QB), 1)

    def keep_lane(v, h):
        return jnp.where(low_lane if h == 0 else jnp.logical_not(low_lane), v, jnp.zeros_like(v))

    def scores_t(kp, qm, qb):
        kv = (qb + 1) * QB
        s = dot_t(kp[:kv], qm)
        kb = KB[0:kv, :]
        s = s + jnp.concatenate([kb] * (QB // 128), axis=1)
        last = jnp.where(diag, s[kv - QB :], MASKED)
        if qb == 0:
            return last
        return jnp.concatenate([s[: kv - QB], last], axis=0)

    def send_cot():
        return line_send(lambda i: CS.at[i], lambda i: GF.at[pl.ds(mo(z * T, 16), T), :])

    between = {
        (0, 3): (w_out.hop, w_fc2.push),
        (1, 0): (w_fc.hop,),
        (1, 2): (w_out.forward, w_proj.push),
        (1, 3): (w_fc.forward, w_fc2.hop),
        (2, 0): (w_out.relay, w_proj2.push),
        (2, 2): (w_fc.relay, w_proj.hop),
        (2, 3): (w_fc2.forward,),
    }

    def attend(p, c):
        lanes = pl.ds(mo(p * 128, 128), 128)
        kp, vp = QKV[1, :, lanes], QKV[2, :, lanes]
        vt = vp.T
        for qb in range(NQ):
            for (step, at_qb), work in between.items():
                if at_qb == qb:

                    @pl.when(p == step)
                    def _():
                        for do in work:
                            do()

            kv = (qb + 1) * QB
            qp = QKV[0, qb * QB : kv, lanes]
            parts = []
            for h in range(2):
                s = scores_t(kp, keep_lane(qp, h), qb)
                top = jnp.max(s, axis=0, keepdims=True)
                e = jnp.exp(s - top)
                total = jnp.sum(e, axis=0, keepdims=True)
                LSE[pl.ds(2 * p + h, 1), qb * QB : kv] = top + jnp.log(total)
                parts.append(dot(vt[:, :kv], e.astype(BF)) / total)
            CTX[qb * QB : kv, lanes] = jnp.where(low_row, parts[0], parts[1]).T.astype(BF)
        return c

    lax.fori_loop(0, HC // 128, attend, 0)
    w_proj2.hop()

    def split_sum(n, product):
        base = new_recv(2)
        PS[n] = product(pl.ds(mo(other, 16), 2 * T)).astype(BF).reshape(2, T, D)
        for s in range(2):
            send(lambda s=s: PS.at[n, s], lambda s=s: PR.at[n, s], base + s, mate)
        ACC[...] = product(pl.ds(mo(own, 16), 2 * T)).reshape(2, T, D)
        return base

    def split_wait(n, base, s):
        arrive(lambda: PR.at[n, s], base + s)

    w_out.ready()
    ex = split_sum(0, lambda rows: dot(CTX[rows, :], WO[...]))
    w_proj.forward()
    cot_sem = send_cot()
    a2_sem = new_recv(2)
    for s in range(2):
        split_wait(0, ex, s)

        def second_norm(i, c):
            rows = rows_of(0, i, RB)
            h = XR[s, rows, :].astype(F32) + ACC[s, rows, :] + PR[0, s, rows, :].astype(F32) + b_out
            H[s, rows, :] = h
            scaled, _ = norm_stats(h)
            A2[rows_of(own + s * T, i, RB), :] = (scaled * ln2_g + ln2_b).astype(BF)
            return c

        lax.fori_loop(0, T // RB, second_norm, 0)
        mine = lambda s=s: A2.at[pl.ds(mo(own + s * T, 16), T), :]
        send(mine, mine, a2_sem + s, mate)

    VF[...] = jnp.concatenate([MISC[0, 2 * k, 0:1, :], MISC[0, 2 * k + 1, 0:1, :]], axis=1)

    def hidden(base, start, width):
        rows = pl.ds(mo(base, 16), 2 * T)

        def body(i, c):
            cs = pl.ds(mo(i * FC + start, 128), width)
            u = dot(A2[rows, :], WF[:, :, cs].reshape(D, width)) + VF[:, cs]
            t = jnp.tanh(GELU_C * (u + GELU_A * u * u * u))
            M[rows, cs] = (0.5 * u * (1.0 + t)).astype(BF)
            SL[rows, cs] = (
                0.5 * (1.0 + t) + 0.5 * u * (1.0 - t * t) * GELU_C * (1.0 + 3.0 * GELU_A * u * u)
            ).astype(BF)
            return c

        lax.fori_loop(0, 2, body, 0)

    w_fc.ready()
    hidden(own, 0, first)
    w_fc2.relay()
    for s in range(2):
        arrive(lambda: A2.at[pl.ds(mo(other + s * T, 16), T), :], a2_sem + s)
    hidden(other, 0, first)
    w_proj2.forward()
    w_proj.relay()
    w_fc2.ready()
    hidden(own, first, FC - first)
    w_proj2.relay()
    hidden(other, first, FC - first)
    w_proj.ready()
    w_proj2.ready()
    ex = split_sum(1, lambda rows: dot(M[rows, :], WP[...]))

    gf_sem = new_recv(2)
    for s in range(2):
        line_wait(lambda i: GF.at[pl.ds(mo(own + i * T, 16), T), :], cot_sem, s)

        def mask_rows(i, c):
            rows = rows_of(own + s * T, i, RB)
            place = (lax.broadcasted_iota(jnp.int32, (RB, 1), 0) + (own + s * T + i * RB)).astype(F32)
            g = jnp.where(place < length, GF[rows, :].astype(F32), 0.0)
            GF[rows, :] = g.astype(BF)
            V8[V_BPROJ] += fold8(g)
            return c

        lax.fori_loop(0, T // RB, mask_rows, 0)
        mine = lambda s=s: GF.at[pl.ds(mo(own + s * T, 16), T), :]
        send(mine, mine, gf_sem + s, mate)

    for s in range(2):
        split_wait(1, ex, s)

        def output_rows(i, c):
            rows = rows_of(0, i, RB)
            LO[s, rows, :] = (H[s, rows, :] + ACC[s, rows, :] + PR[1, s, rows, :].astype(F32) + b_proj).astype(BF)
            return c

        lax.fori_loop(0, T // RB, output_rows, 0)
    lo_sem = line_send(lambda i: LO.at[i], lambda i: lo_out.at[i])

    for s in range(2):
        arrive(lambda: GF.at[pl.ds(mo(other + s * T, 16), T), :], gf_sem + s)

    bit = (lax.rem(dq, 2), dq // 2)

    def wide_factors(count, width):
        return [jnp.concatenate([FAC[dq ^ j, 0:1, :]] * (width // 128), axis=1) for j in range(count)]

    class Part:
        def __init__(self, plane, S, B, U, Z, E, slab, piece, place):
            self.S, self.B, self.U, self.Z, self.E = S, B, U, Z, E
            self.slab, self.piece, self.place = slab, piece, place
            self.pair, self.zsem, self.end = new_recv(1), new_recv(2), new_recv(4)
            self.setup(*plane)

        def pass_on(self):
            send(lambda: self.slab(1 - zs), lambda: self.B, self.pair, at(d, k, z ^ 1))

        def middle(self):
            arrive(lambda: self.B, self.pair)
            self.U[...] = (self.slab(zs)[...].astype(F32) + self.B[...].astype(F32)).astype(BF)
            for r in range(2):
                mine = (far == 0) & (r == k)
                piece = lambda r=r: self.piece(r)
                send(piece, lambda: self.Z.at[far], self.zsem + far, at(d, r, target), jnp.logical_not(mine))
                local(piece, lambda: self.Z.at[far], self.zsem + far, mine)

        def finish(self):
            arrive(lambda: self.Z.at[0], self.zsem, is_far)
            arrive_local(lambda: self.Z.at[0], self.zsem, is_near)
            arrive(lambda: self.Z.at[1], self.zsem + 1)
            self.E[...] = (self.Z[0].astype(F32) + self.Z[1].astype(F32)).astype(BF)
            for j in (1, 2, 3):
                send(lambda: self.E, lambda: self.place(dq), self.end + j, quad[j - 1])
            local(lambda: self.E, lambda: self.place(dq), self.end)

        def done(self):
            arrive_local(lambda: self.place(dq), self.end)
            for j in (1, 2, 3):
                arrive(lambda: self.place(dq ^ j), self.end + j)

    class DirectPart(Part):
        def setup(self, G, R):
            self.G, self.R, self.raw = G, R, new_recv(3)

        def quarter(self, q):
            return self.G.at[:, q // 2, lax.rem(q, 2)]

        def spread(self):
            for j in (1, 2, 3):
                send(lambda j=j: self.quarter(dq ^ j), lambda j=j: self.R.at[j - 1], self.raw + j - 1, quad[j - 1])

        def reduce(self):
            for j in (1, 2, 3):
                arrive(lambda: self.R.at[j - 1], self.raw + j - 1)
            G, (_, n, width) = self.quarter(dq), self.S.shape
            factors, steps = wide_factors(QUAD, width), n // 16

            def add(i, c):
                a, rows = i // steps, pl.ds(mo(lax.rem(i, steps) * 16, 16), 16)
                v = G[a, rows, :].astype(F32) * factors[0]
                for j in (1, 2, 3):
                    v = v + self.R[j - 1, a, rows, :].astype(F32) * factors[j]
                self.S[a, rows, :] = v.astype(BF)
                return c

            lax.fori_loop(0, 2 * steps, add, 0)
            self.pass_on()

    class CrossPart(Part):
        def setup(self, G, X, O, Y):
            self.G, self.X, self.O, self.Y = G, X, O, Y
            self.raw, self.cross = new_recv(2), new_recv(2)

        def spread(self):
            send(lambda: self.G.at[0, :, 1 - bit[0]], lambda: self.X.at[0], self.raw, quad[0])
            send(lambda: self.G.at[1, 1 - bit[1]], lambda: self.X.at[1], self.raw + 1, quad[1])

        def scale(self):
            _, n, width = self.S.shape
            factors = wide_factors(3, width)
            for a in range(2):
                arrive(lambda: self.X.at[a], self.raw + a)

                def add(i, c, a=a):
                    rows = pl.ds(mo(i * 16, 16), 16)
                    for b, to in ((bit[1 - a], self.S), (1 - bit[1 - a], self.O)):
                        mine = self.G[0, b, bit[0], rows, :] if a == 0 else self.G[1, bit[1], b, rows, :]
                        v = mine.astype(F32) * factors[0] + self.X[a, b, rows, :].astype(F32) * factors[1 + a]
                        to[a, rows, :] = v.astype(BF)
                    return c

                lax.fori_loop(0, n // 16, add, 0)
                send(lambda a=a: self.O.at[a], lambda a=a: self.Y.at[a], self.cross + a, quad[1 - a])

        def reduce(self):
            for a in range(2):
                arrive(lambda: self.Y.at[a], self.cross + a)
            self.S[...] = (self.S[...].astype(F32) + self.Y[...].astype(F32)).astype(BF)
            self.pass_on()

    g_proj = DirectPart(
        (GWP, RP), SPW, BP, UP, ZP, EP,
        lambda cs: SPW.at[cs],
        lambda r: UP.at[:, cols(r)],
        lambda q: gp_out.at[pl.ds(mo(q * p192, 16), p192), :],
    )
    g_out = CrossPart(
        (GWO, XO, OO, YO), SOW, BO, UO, ZO, EO,
        lambda cs: SOW.at[cs],
        lambda r: UO.at[:, cols(r)],
        lambda q: go_out.at[pl.ds(mo(q * o48, 16), o48), :],
    )

    def fc_grad(plane, S, B, U, Z, E, start, n):
        return CrossPart(
            plane, S, B, U, Z, E,
            lambda cs: S.at[:, :, pl.ds(mo(cs * FC, 128), FC)],
            lambda r: U.at[r],
            lambda q: gf_out.at[pl.ds(mo(start + q * n, 16), n), :],
        )

    g_fc = fc_grad((GWF, XF, OF, YF), SFW, BF1, UF, ZF, EF, 0, 128 // QUAD)
    g_fc2 = fc_grad((GWF2, XF2, OF2, YF2), SFW2, BF2, UF2, ZF2, EF2, 128, (FR - 128) // QUAD)

    def qkv_grad(i):
        return CrossPart(
            [v.at[i] for v in (GWQ, XQ, OQ, YQ)],
            *(v.at[i] for v in (SQW, BQ, UQ, ZQ, EQ)),
            lambda cs: SQW.at[i, cs],
            lambda r: UQ.at[i, :, cols(r)],
            lambda q: gq_out.at[i, pl.ds(mo(q * q48, 16), q48), :],
        )

    g_qkv = [qkv_grad(i) for i in range(3)]

    def grad_proj(i, c):
        cs = pl.ds(mo(i * (FC // 2), 128), FC // 2)
        g = t_dot(M[:, cs], GF[...])
        SQ[...] += fold8(g * g)
        GWP[i // 2, lax.rem(i, 2)] = g.astype(BF).reshape(2, p192, D)
        return c

    lax.fori_loop(0, 4, grad_proj, 0)
    g_proj.spread()

    NB = 512
    NN = FH // NB

    def grad_hidden(i, c):
        rows = pl.ds(mo(i // NN * 2 * T, 16), 2 * T)
        cs = pl.ds(mo(lax.rem(i, NN) * NB, 128), NB)
        g = dot_t(GF[rows, :], WP[cs, :]) * SL[rows, cs].astype(F32)
        low = g.astype(BF)
        SL[rows, cs] = low
        VF[:, cs] = jnp.where(i < NN, 0.0, VF[:, cs]) + jnp.sum(low.astype(F32), axis=0, keepdims=True)
        return c

    lax.fori_loop(0, 2 * NN, grad_hidden, 0)
    ex = split_sum(2, lambda rows: dot_t(SL[rows, :], WF[...].reshape(D, FH)))

    ga_sem = new_recv(2)
    for s in range(2):
        split_wait(2, ex, s)

        def second_back(i, c):
            rows = rows_of(0, i, RB)
            full = rows_of(own + s * T, i, RB)
            up = ACC[s, rows, :] + PR[2, s, rows, :].astype(F32)
            scaled, inverse = norm_stats(H[s, rows, :])
            through = up * ln2_g
            V8[V_LN2G] += fold8(up * scaled)
            V8[V_LN2B] += fold8(up)
            g = GF[full, :].astype(F32) + inverse * (
                through
                - jnp.mean(through, axis=-1, keepdims=True)
                - scaled * jnp.mean(through * scaled, axis=-1, keepdims=True)
            )
            V8[V_BOUT] += fold8(g)
            H[s, rows, :] = g
            GA[full, :] = g.astype(BF)
            return c

        lax.fori_loop(0, T // RB, second_back, 0)
        mine = lambda s=s: GA.at[pl.ds(mo(own + s * T, 16), T), :]
        send(mine, mine, ga_sem + s, mate)
    for s in range(2):
        arrive(lambda: GA.at[pl.ds(mo(other + s * T, 16), T), :], ga_sem + s)

    GCTX[...] = dot_t(GA[...], WO[...]).astype(BF)
    g = t_dot(CTX[...], GA[...])
    SQ[...] += fold8(g * g)
    GWO[...] = g.astype(BF).reshape(2, 2, 2, o48, D)
    g_out.spread()

    def grad_fc(G, start, n):
        g = t_dot(jnp.concatenate([A2[:, start : start + n], A2[:, FR + start : FR + start + n]], axis=1), SL[...])
        q = fold8(g * g)
        SQ[...] += q[:, :D] + q[:, D:]
        G[...] = g.astype(BF).reshape(2, 2, 2, n // QUAD, FH)

    grad_fc(GWF, 0, 128)
    g_fc.spread()

    def attend_back(p):
        lanes = pl.ds(mo(p * 128, 128), 128)
        kp, vp = QKV[1, :, lanes], QKV[2, :, lanes]
        kt = kp.T
        DK[...] = jnp.zeros_like(DK)
        DV[...] = jnp.zeros_like(DV)
        for qb in range(NQ):
            kv = (qb + 1) * QB
            qp = QKV[0, qb * QB : kv, lanes]
            do = GCTX[qb * QB : kv, lanes]
            dqt = []
            for h in range(2):
                qm, dm = keep_lane(qp, h), keep_lane(do, h)
                pt = jnp.exp(scores_t(kp, qm, qb) - LSE[pl.ds(2 * p + h, 1), qb * QB : kv])
                gp = dot_t(vp[:kv], dm)
                both = pt * gp
                gs = (both - pt * jnp.sum(both, axis=0, keepdims=True)).astype(BF)
                DV[0:kv, :] += dot(pt.astype(BF), dm)
                DK[0:kv, :] += dot(gs, qm)
                dqt.append(dot(kt[:, :kv], gs))
            GQKV[0, qb * QB : kv, lanes] = (
                jnp.where(low_row, dqt[0], dqt[1]).T * (HEAD_DIM**-0.5)
            ).astype(BF)
        GQKV[1, :, lanes] = DK[...].astype(BF)
        GQKV[2, :, lanes] = DV[...].astype(BF)

    def attend_back_step(p, c):
        attend_back(p)
        return c

    lax.fori_loop(0, HC // 128, attend_back_step, 0)

    def grad_norm_in(rows):
        return dot(GQKV[0, rows, :], WQ[0]) + dot(GQKV[1, rows, :], WQ[1]) + dot(GQKV[2, rows, :], WQ[2])

    ex = split_sum(3, grad_norm_in)
    grad_fc(GWF2, 128, FR - 128)
    g_fc2.spread()
    for s in range(2):
        split_wait(3, ex, s)

        def first_back(i, c):
            rows = rows_of(0, i, RB)
            up = ACC[s, rows, :] + PR[3, s, rows, :].astype(F32)
            scaled, inverse = norm_stats(XR[s, rows, :].astype(F32))
            through = up * ln1_g
            V8[V_LN1G] += fold8(up * scaled)
            V8[V_LN1B] += fold8(up)
            g = H[s, rows, :] + inverse * (
                through
                - jnp.mean(through, axis=-1, keepdims=True)
                - scaled * jnp.mean(through * scaled, axis=-1, keepdims=True)
            )
            GI[s, rows, :] = g.astype(BF)
            return c

        lax.fori_loop(0, T // RB, first_back, 0)

    gi_sem = line_send(lambda i: GI.at[i], lambda i: gi_out.at[i], (0,))

    def grad_qkv(i, c):
        g = t_dot(GQKV[i], A1[...])
        SQ[...] += fold8(g * g)
        GWQ[i] = g.astype(BF).reshape(2, 2, 2, q48, D)
        return c

    lax.fori_loop(0, 3, grad_qkv, 0)
    VK[k] = jnp.zeros(VK.shape[1:], F32)
    for i in range(6):
        VK[k, i : i + 1, :] = jnp.sum(V8[i], axis=0, keepdims=True)
    VK[k, V_BQV : V_BQV + 1, :] = jnp.concatenate(
        [jnp.sum(GQKV[i].astype(F32), axis=0, keepdims=True) for i in (0, 2)], axis=1
    )
    VK[k, V_BFC : V_BFC + 1, :] = VF[:, :D]
    VK[k, V_BFC + 1 : V_BFC + 2, :] = VF[:, D:]
    VK[k, V_SQ : V_SQ + 1, :] = jnp.sum(SQ[...], axis=0, keepdims=True)
    vk_sem = new_recv(1)
    send(lambda: VK.at[k], lambda: VK.at[k], vk_sem, mate)
    arrive(lambda: VK.at[1 - k], vk_sem)
    va, vb = VK[0], VK[1]
    pack = jnp.concatenate([va[0:6] + vb[0:6], va[6:9], vb[6:9]], axis=0)
    squares = jnp.sum(jnp.sum(pack * pack, axis=0, keepdims=True) + va[9:10] + vb[9:10], axis=1, keepdims=True)
    norm = jnp.sqrt(squares)
    factor = CLIP_BOUND / jnp.maximum(norm, CLIP_BOUND)
    FAC[dq] = jnp.broadcast_to(factor, (8, 128))
    fac_sem, vp_sem = new_recv(3), new_recv(3)
    for j in (1, 2, 3):
        send(lambda: FAC.at[dq], lambda: FAC.at[dq], fac_sem + j - 1, quad[j - 1])
    VP[dq] = jnp.concatenate([pack, jnp.zeros((4, D), F32)], axis=0)
    for part in g_qkv:
        part.spread()

    for j in (1, 2, 3):
        arrive(lambda: FAC.at[dq ^ j], fac_sem + j - 1)

    order = [g_proj, g_out, g_fc, g_fc2, *g_qkv]
    g_proj.reduce()
    for part in order[1:]:
        part.scale()
    for j in (1, 2, 3):
        send(lambda: VP.at[dq], lambda: VP.at[dq], vp_sem + j - 1, quad[j - 1])
    g_out.reduce()
    g_fc.reduce()
    g_proj.middle()
    g_out.middle()
    g_fc2.reduce()
    g_fc.middle()
    for j in (1, 2, 3):
        arrive(lambda: VP.at[dq ^ j], vp_sem + j - 1)
    total = jnp.zeros((12, D), F32)
    for q in range(QUAD):
        total = total + VP[q, 0:12, :] * FAC[q, 0:1, 0:1]
    VZ[z] = jnp.concatenate([total, jnp.broadcast_to(norm, (4, D))], axis=0)
    vz_sem = new_recv(3)
    for j in (1, 2, 3):
        send(lambda: VZ.at[z], lambda: VZ.at[z], vz_sem + j - 1, at(d, k, z ^ j))
    for part in g_qkv:
        part.reduce()
    g_proj.finish()
    g_fc2.middle()
    g_out.finish()
    g_fc.finish()
    for part in g_qkv:
        part.middle()
    line_send(lambda i: GI.at[i], lambda i: gi_out.at[i], (1,), gi_sem)
    g_fc2.finish()
    for part in g_qkv:
        part.finish()

    for j in (1, 2, 3):
        arrive(lambda: VZ.at[z ^ j], vz_sem + j - 1)
    total = VZ[0] + VZ[1] + VZ[2] + VZ[3]
    vec_out[0:6, :] = total[0:6]
    V8[0, 0:6, :] = total[6:12]
    vec_out[6:7, :] = V8[0, pl.ds(V_BFC - V_BQV + 3 * zk + zs, 1), :]
    pair = V8[0, pl.ds(3 * zk, 1), :]
    spare = jnp.zeros((1, D - QR), F32)
    for i in range(2):
        a, b = pair[:, i * HC : i * HC + QR], pair[:, i * HC + QR : (i + 1) * HC]
        vec_out[7 + i : 8 + i, :] = jnp.concatenate([jnp.where(zs == 0, a, b), spare], axis=1)
    first_place = lax.broadcasted_iota(jnp.int32, (1, D), 1) == 0
    vec_out[9:10, :] = jnp.where(
        first_place, VZ[2 * k, V_NORM : V_NORM + 1, :], VZ[2 * k + 1, V_NORM : V_NORM + 1, :]
    )
    vec_out[10:12, :] = jnp.zeros((2, D), F32)

    for part in order:
        part.done()
    for i in range(2):
        line_wait(lambda i: lo_out.at[i], lo_sem, i)
        line_wait(lambda i: gi_out.at[i], gi_sem, i)
    for cond, make in pending:
        when(cond, lambda: make().wait_send())


def widen(*refs):
    low, vec, wide, (b_out, ln1_g, ln1_b, ln2_g, ln2_b, b_proj, b_fc, b_qv, norms) = (
        refs[:6], refs[6], refs[7:13], refs[13:22]
    )
    before, after, sems = refs[22:28], refs[28:34], refs[34]
    parts = []
    for i, v in enumerate(low):
        parts += [(i, (e,)) for e in range(2)] if i < 2 else [(i, (...,))]

    def load(n, i, at):
        return pltpu.make_async_copy(low[i].at[at], before[i].at[at], sems.at[2 * n])

    def store(n, i, at):
        return pltpu.make_async_copy(after[i].at[at], wide[i].at[at], sems.at[2 * n + 1])

    for n, (i, at) in enumerate(parts):
        load(n, i, at).start()
    for row, out in enumerate((b_out, ln1_g, ln1_b, ln2_g, ln2_b, b_proj, b_fc)):
        out[...] = vec[row, :]
    b_qv[...] = vec[7:9, : b_qv.shape[1]]
    norms[...] = vec[9, :2]
    for n, (i, at) in enumerate(parts):
        load(n, i, at).wait()
        after[i][at] = before[i][at].astype(F32)
        store(n, i, at).start()
    for n, (i, at) in enumerate(parts):
        store(n, i, at).wait()


def shards(
    layer_in, w_qkv, b_qv, w_out, b_out, ln1_g, ln1_b, ln2_g, ln2_b, w_fc, b_fc, w_proj, b_proj, lengths, cotangent
):
    E, T, D = layer_in.shape
    n_col, n_row = lax.axis_size("col"), lax.axis_size("row")
    assert lax.axis_size("dp") == QUAD and n_col == 4 and n_row % 2 == 0
    pairs = n_row // 2
    r = lax.axis_index("row")
    core = lax.rem(r, 2)
    half_rows = w_fc.shape[0] * pairs

    def halves(w, axis):
        if pairs == 1:
            return w
        whole = lax.all_gather(w, "row", axis=axis, tiled=True)
        return lax.dynamic_slice_in_dim(whole, core * half_rows, half_rows, axis)

    w_qkv, w_out, w_fc, w_proj = halves(w_qkv, 0), halves(w_out, 1), halves(w_fc, 0), halves(w_proj, 1)
    L = T * n_col
    HQ = w_qkv.shape[2]
    HC = HQ * n_col // 2
    FQ = w_fc.shape[1]
    FH = FQ * n_col // 2
    DH = w_fc.shape[0]
    wq_t = jnp.transpose(w_qkv, (1, 2, 0))
    q48, o48, p192 = HQ // QUAD, HQ // QUAD, FQ // QUAD
    fa, fb = 128 // QUAD, (DH - 128) // QUAD

    anyspec = pl.BlockSpec(memory_space=pl.ANY)
    vm = pl.BlockSpec(memory_space=pltpu.VMEM)
    V = pltpu.VMEM
    outs = pl.pallas_call(
        kernel,
        name="layer",
        out_shape=(
            jax.ShapeDtypeStruct((E, T, D), BF),
            jax.ShapeDtypeStruct((E, T, D), BF),
            jax.ShapeDtypeStruct((3, HQ, DH), BF),
            jax.ShapeDtypeStruct((HQ, DH), BF),
            jax.ShapeDtypeStruct((DH, FQ), BF),
            jax.ShapeDtypeStruct((FQ, DH), BF),
            jax.ShapeDtypeStruct((12, D), F32),
        ),
        in_specs=[anyspec] * 6 + [vm, vm, pl.BlockSpec(memory_space=pltpu.SMEM)] + [vm] * 6,
        out_specs=(anyspec,) * 6 + (vm,),
        scratch_shapes=[
            V((2, T, D), BF),
            V((2, T // 2, D), BF),
            V((2, T, D), BF),
            V((8, D), F32),
            V((2, T, D), BF),
            V((2, T, D), F32),
            V((L, D), BF),
            V((3, HC, D), BF),
            V((HC, D), BF),
            V((2, DH, FH), BF),
            V((FH, D), BF),
            V((2, n_col, 8, D), F32),
            V((3, L, HC), BF),
            V((L, HC), BF),
            V((8, L), F32),
            V((L, 128), F32),
            V((2, T, D), F32),
            V((4, 2, T, D), BF),
            V((4, 2, T, D), BF),
            V((L, D), BF),
            V((L, FH), BF),
            V((L, FH), BF),
            V((L, D), BF),
            V((L, D), BF),
            V((L, HC), BF),
            V((3, L, HC), BF),
            V((L, 128), F32),
            V((L, 128), F32),
            V((2, T, D), BF),
            V((2, T, D), BF),
            V((6, 8, D), F32),
            V((8, D), F32),
            V((1, FH), F32),
            V((2, 16, D), F32),
            V((QUAD, 8, 128), F32),
            V((QUAD, 16, D), F32),
            V((n_col, 16, D), F32),
            V((3, 2, 2, 2, q48, D), BF),
            V((2, 2, 2, o48, D), BF),
            V((2, 2, 2, fa, FH), BF),
            V((2, 2, 2, fb, FH), BF),
            V((2, 2, 2, p192, D), BF),
            V((3, 2, p192, D), BF),
            *[
                V(shape, BF)
                for shape in ((3, 2, 2, q48, D), (2, 2, o48, D), (2, 2, fa, FH), (2, 2, fb, FH))
            ],
            *[
                V(shape, BF)
                for _ in "OY"
                for shape in ((3, 2, q48, D), (2, o48, D), (2, fa, FH), (2, fb, FH))
            ],
            V((3, 2, q48, D), BF),
            V((2, o48, D), BF),
            V((2, fa, FH), BF),
            V((2, fb, FH), BF),
            V((2, p192, D), BF),
            *[
                V(shape, BF)
                for _ in "BU"
                for shape in ((3, q48, D), (o48, D), (2, fa, FQ), (2, fb, FQ), (p192, D))
            ],
            V((3, 2, q48, DH), BF),
            V((2, o48, DH), BF),
            V((2, fa, FQ), BF),
            V((2, fb, FQ), BF),
            V((2, p192, DH), BF),
            V((3, q48, DH), BF),
            V((o48, DH), BF),
            V((fa, FQ), BF),
            V((fb, FQ), BF),
            V((p192, DH), BF),
            pltpu.SemaphoreType.DMA((240,)),
            pltpu.SemaphoreType.DMA((240,)),
        ],
        compiler_params=pltpu.CompilerParams(
            collective_id=0, has_side_effects=True, vmem_limit_bytes=63 * 2**20
        ),
    )(
        layer_in, cotangent, wq_t, w_out, w_fc, w_proj, b_fc, b_qv, lengths,
        b_out, ln1_g, ln1_b, ln2_g, ln2_b, b_proj,
    )
    low, vec = outs[:6], outs[6]
    line = jax.ShapeDtypeStruct((D,), F32)
    outs = pl.pallas_call(
        widen,
        name="widen",
        out_shape=(
            *(jax.ShapeDtypeStruct(v.shape, F32) for v in low),
            *(line,) * 7,
            jax.ShapeDtypeStruct((2, HQ), F32),
            jax.ShapeDtypeStruct((2,), F32),
        ),
        in_specs=[anyspec] * 6 + [vm],
        out_specs=(anyspec,) * 6 + (vm,) * 9,
        scratch_shapes=[
            *(V(v.shape, BF) for v in low), *(V(v.shape, F32) for v in low), pltpu.SemaphoreType.DMA((16,))
        ],
        compiler_params=pltpu.CompilerParams(vmem_limit_bytes=63 * 2**20),
    )(*low, vec)
    lo, gi, gq, go, gf, gp = outs[:6]
    vec, norms = outs[6:14], outs[14]
    gq = jnp.transpose(gq, (2, 0, 1))
    if pairs > 1:
        groups = [[2 * p + q for p in range(pairs)] for q in range(2)]
        cores = [[2 * p, 2 * p + 1] for p in range(pairs)]
        gq, go, gf, gp, *vec = (
            lax.psum(v, "row", axis_index_groups=groups) for v in (gq, go, gf, gp, *vec)
        )

        def share(v, axis):
            whole = lax.all_gather(v, "row", axis=axis, tiled=True, axis_index_groups=cores)
            part = whole.shape[axis] // n_row
            return lax.dynamic_slice_in_dim(whole, r * part, part, axis)

        gq, go, gf, gp = share(gq, 0), share(go, 1), share(gf, 0), share(gp, 1)
    gb_out, g1, b1, g2, b2, gb_proj, gb_fc, gb_qv = vec
    return (lo, gi, norms, gq, gb_qv, go, gb_out, g1, b1, g2, b2, gf, gb_fc, gp, gb_proj)


def solution(mesh):
    in_specs = (
        P(("dp", "row"), "col", None),
        P("row", None, "col"),
        P(None, "col"),
        P("col", "row"),
        P(),
        P(),
        P(),
        P(),
        P(),
        P("row", "col"),
        P("col"),
        P("col", "row"),
        P(),
        P(("dp", "row")),
        P(("dp", "row"), "col", None),
    )
    out_specs = (
        P(("dp", "row"), "col", None),
        P(("dp", "row"), "col", None),
        P(("dp", "row")),
        P("row", None, "col"),
        P(None, "col"),
        P("col", "row"),
        P(),
        P(),
        P(),
        P(),
        P(),
        P("row", "col"),
        P("col"),
        P("col", "row"),
        P(),
    )
    return jax.shard_map(shards, mesh=mesh, in_specs=in_specs, out_specs=out_specs, check_vma=False)
```

```python
import functools

import jax
import jax.numpy as jnp
from jax import lax
from jax.experimental import pallas as pl
from jax.experimental.pallas import tpu as pltpu
from jax.sharding import PartitionSpec as P

MESH = pl.DeviceIdType.MESH
EPSILON = 1e-05
CLIP_BOUND = 1.0
GELU_C = 0.7978845608028654
GELU_A = 0.044715
MASKED = -1e30
HEAD_DIM = 64
QUAD = 4
BF = jnp.bfloat16
F32 = jnp.float32

V_BOUT, V_LN1G, V_LN1B, V_LN2G, V_LN2B, V_BPROJ, V_BQV, V_BFC, V_SQ = 0, 1, 2, 3, 4, 5, 6, 7, 9
V_NORM = 12


def dot(a, b):
    return lax.dot_general(a, b, (((1,), (0,)), ((), ())), preferred_element_type=F32)


def dot_t(a, b):
    return lax.dot_general(a, b, (((1,), (1,)), ((), ())), preferred_element_type=F32)


def t_dot(a, b):
    return lax.dot_general(a, b, (((0,), (0,)), ((), ())), preferred_element_type=F32)


def fold8(v):
    return jnp.sum(v.reshape(v.shape[0] // 8, 8, v.shape[1]), axis=0)


def norm_stats(v):
    center = v - jnp.mean(v, axis=-1, keepdims=True)
    inverse = lax.rsqrt(jnp.mean(center * center, axis=-1, keepdims=True) + EPSILON)
    return center * inverse, inverse


def kernel(
    x_in, cot_in, wq_in, wo_in, wf_in, wp_in, bfc_in, bqv_in, len_in, b_out, ln1_g, ln1_b, ln2_g, ln2_b, b_proj,
    lo_out, gi_out, gq_out, go_out, gf_out, gp_out, vec_out,
    XS, XH, CS, misc_in, XR, H, HG, A1, WQ, WO, WF, WP, MISC, QKV, CTX, LSE, KB, ACC,
    PS, PR, A2, M, SL, GF, GA, GCTX, GQKV, DK, DV,
    V8, SQ, VF, VK, FAC, VP, VZ,
    GWQ, GWO, GWF, GWF2, GWP, RP, XQ, XO, XF, XF2, OQ, OO, OF, OF2, YQ, YO, YF, YF2, SQW, SOW, SFW, SFW2, SPW, BQ, BO, BF1, BF2, BP, UQ, UO, UF, UF2, UP, ZQ, ZO, ZF, ZF2, ZP, EQ, EO, EF, EF2, EP,
    ss, rs,
):
    d, row, z = lax.axis_index("dp"), lax.axis_index("row"), lax.axis_index("col")
    k = lax.rem(row, 2)
    dq = d

    def at(plane, core, place):
        return (plane, row - k + core, place)

    zk, zs = z // 2, lax.rem(z, 2)
    L, D = A1.shape
    T = XR.shape[1]
    HC = CTX.shape[1]
    FH = M.shape[1]
    QR, OR_, FR, PR_ = wq_in.shape[1], wo_in.shape[0], wf_in.shape[0], wp_in.shape[0]
    DH = wo_in.shape[1]
    own, other = k * 2 * T, (1 - k) * 2 * T

    def mo(v, n):
        return pl.multiple_of(v, n)

    def when(cond, f):
        if cond is True:
            f()
        else:
            pl.when(cond)(f)

    n_send = [0]
    n_recv = [0]
    pending = []

    def new_send():
        n_send[0] += 1
        assert n_send[0] <= ss.shape[0]
        return n_send[0] - 1

    def new_recv(n):
        n_recv[0] += n
        assert n_recv[0] <= rs.shape[0]
        return n_recv[0] - n

    def send(src, dst, rsem, dev, cond=True):
        sem = new_send()

        def make():
            return pltpu.make_async_remote_copy(
                src(),
                dst(),
                ss.at[sem],
                rs.at[rsem() if callable(rsem) else rsem],
                device_id=dev() if callable(dev) else dev,
                device_id_type=MESH,
            )

        when(cond, lambda: make().start())
        pending.append((cond, make))

    def flush(count):
        for cond, make in pending[:count]:
            when(cond, lambda: make().wait_send())
        del pending[:count]

    def local(src, dst, rsem, cond=True):
        when(cond, lambda: pltpu.make_async_copy(src(), dst(), rs.at[rsem]).start())

    def arrive(dst, rsem, cond=True):
        def f():
            pltpu.make_async_remote_copy(
                dst(), dst(), ss.at[0], rs.at[rsem], device_id=at(d, k, z), device_id_type=MESH
            ).wait_recv()

        when(cond, f)

    def arrive_local(dst, rsem, cond=True):
        when(cond, lambda: pltpu.make_async_copy(dst(), dst(), rs.at[rsem]).wait())

    mate = at(d, 1 - k, z)
    quad = [at(d ^ j, k, z) for j in (1, 2, 3)]

    barrier = pltpu.get_barrier_semaphore()
    line = [at(d, k, z ^ j) for j in (1, 2, 3)] + [at(d, 1 - k, z ^ j) for j in (0, 1, 2, 3)]
    quad_mates = [at(d ^ j, 1 - k, z) for j in (1, 2, 3)]
    for dev in quad + quad_mates + line:
        pl.semaphore_signal(barrier, inc=1, device_id=dev, device_id_type=MESH)
    pl.semaphore_wait(barrier, len(quad) + len(quad_mates) + len(line))

    def line_send(src, dst):
        base = new_recv(2)
        for i in range(2):
            mine = (zk == k) & (2 * k + i == z)
            send(lambda i=i: src(i), lambda: dst(zs), base + zs, at(d, zk, 2 * k + i), jnp.logical_not(mine))
            local(lambda i=i: src(i), lambda: dst(zs), base + zs, mine)
        return base

    def line_wait(dst, base, i):
        mine = (zk == k) & (2 * k + i == z)
        arrive(lambda: dst(i), base + i, jnp.logical_not(mine))
        arrive_local(lambda: dst(i), base + i, mine)

    far = lax.rem(k + zk, 2)
    target = z ^ (2 * far)
    is_near, is_far = far == 0, far == 1
    zo = 1 - zs

    class Weight:
        def __init__(self, src, src_quarter, piece, full, slab):
            self.src, self.src_quarter, self.piece, self.full, self.slab = src, src_quarter, piece, full, slab
            self.zsem, self.xsem = new_recv(4), new_recv(8)

        def push(self):
            sem = lambda: self.zsem + zs * 2 + k
            for j in (2, 1):
                send(self.src_quarter, lambda: self.piece(zs, k, dq), sem, lambda j=j: at(d, zk, z ^ j))
            send(self.src, lambda: self.full(zs, k), sem, mate, is_far)
            local(self.src, lambda: self.full(zs, k), self.zsem + zs * 2 + k, is_near)

        def spread(self, cs, cond):
            mine = lambda: self.slab(cs, dq)
            for j in (1, 2):
                send(mine, mine, lambda j=j: self.xsem + cs * 4 + j - 1, quad[j - 1], cond)

        def hop(self):
            for r in range(2):
                arrive(lambda: self.piece(zo, r, dq), self.zsem + zo * 2 + r, is_near)
                arrive(lambda: self.piece(zs, r, dq), self.zsem + zs * 2 + r, is_far)
                mine = lambda r=r: self.piece(zs, r, dq)
                send(mine, mine, lambda r=r: self.zsem + zs * 2 + r, lambda: at(d, k, z ^ 1), is_far)
            self.spread(zo, is_near)
            self.spread(zs, is_far)

        def forward(self):
            for r in range(2):
                arrive(lambda: self.piece(zo, r, dq), self.zsem + zo * 2 + r, is_far)
            self.spread(zo, is_far)

        def relay(self):
            for cs, cond in ((zs, is_far), (zo, True)):
                for j in (1, 2):
                    arrive(lambda: self.slab(cs, dq ^ j), self.xsem + cs * 4 + j - 1, cond)
                    half = lambda cs=cs, j=j: self.piece(cs, j - 1, dq ^ j)
                    send(half, half, lambda cs=cs, j=j: self.xsem + cs * 4 + 1 + j, quad[2 - j], cond)

        def ready(self):
            for r in range(2):
                arrive(lambda: self.full(zs, r), self.zsem + zs * 2 + r, is_near & (k != r))
                arrive_local(lambda: self.full(zs, r), self.zsem + zs * 2 + r, is_near & (k == r))
            for cs, cond in ((zs, is_far), (zo, True)):
                for j in (1, 2):
                    arrive(lambda: self.piece(cs, j - 1, dq ^ 3), self.xsem + cs * 4 + 1 + j, cond)

    q48, o48, f96, p192 = QR // QUAD, OR_ // QUAD, FR // QUAD, PR_ // QUAD

    def cols(r):
        return pl.ds(mo(r * DH, 128), DH)

    w_qkv = Weight(
        lambda: wq_in,
        lambda: wq_in.at[:, pl.ds(mo(dq * q48, 16), q48), :],
        lambda cs, r, q: WQ.at[:, pl.ds(mo(cs * QR + q * q48, 16), q48), cols(r)],
        lambda cs, r: WQ.at[:, pl.ds(mo(cs * QR, 16), QR), cols(r)],
        lambda cs, q: WQ.at[:, pl.ds(mo(cs * QR + q * q48, 16), q48), :],
    )
    w_out = Weight(
        lambda: wo_in,
        lambda: wo_in.at[pl.ds(mo(dq * o48, 16), o48), :],
        lambda cs, r, q: WO.at[pl.ds(mo(cs * OR_ + q * o48, 16), o48), cols(r)],
        lambda cs, r: WO.at[pl.ds(mo(cs * OR_, 16), OR_), cols(r)],
        lambda cs, q: WO.at[pl.ds(mo(cs * OR_ + q * o48, 16), o48), :],
    )
    FC = wf_in.shape[1]

    def fc_part(at0, n):
        return Weight(
            lambda: wf_in.at[:, pl.ds(at0, n)],
            lambda: wf_in.at[pl.ds(mo(dq * f96, 16), f96), pl.ds(at0, n)],
            lambda cs, r, q: WF.at[r, pl.ds(mo(q * f96, 16), f96), pl.ds(mo(cs * FC + at0, 128), n)],
            lambda cs, r: WF.at[r, :, pl.ds(mo(cs * FC + at0, 128), n)],
            lambda cs, q: WF.at[:, pl.ds(mo(q * f96, 16), f96), pl.ds(mo(cs * FC + at0, 128), n)],
        )

    def proj_part(at0, n):
        n4 = n // QUAD
        return Weight(
            lambda: wp_in.at[pl.ds(at0, n), :],
            lambda: wp_in.at[pl.ds(mo(at0 + dq * n4, 16), n4), :],
            lambda cs, r, q: WP.at[pl.ds(mo(cs * PR_ + at0 + q * n4, 16), n4), cols(r)],
            lambda cs, r: WP.at[pl.ds(mo(cs * PR_ + at0, 16), n), cols(r)],
            lambda cs, q: WP.at[pl.ds(mo(cs * PR_ + at0 + q * n4, 16), n4), :],
        )

    first = FC // 3
    w_fc, w_fc2 = fc_part(0, first), fc_part(first, FC - first)
    w_proj, w_proj2 = proj_part(0, first), proj_part(first, FC - first)

    stage = new_recv(2)
    pltpu.make_async_copy(x_in, H, rs.at[stage]).start()
    pltpu.make_async_copy(cot_in, ACC, rs.at[stage + 1]).start()
    bq, bv = bqv_in[0:1, :], bqv_in[1:2, :]
    gap = jnp.zeros_like(bq)
    misc_in[...] = jnp.concatenate(
        [
            bfc_in[...].reshape(1, D),
            jnp.where(zs == 0, jnp.concatenate([bq, gap, bv, gap], axis=1), jnp.concatenate([gap, bq, gap, bv], axis=1)),
            jnp.full((1, D), len_in[0].astype(F32)),
            jnp.full((1, D), len_in[1].astype(F32)),
            jnp.zeros((4, D), F32),
        ],
        axis=0,
    )
    misc_sem = new_recv(8)
    for dev in line:
        send(lambda: misc_in, lambda: MISC.at[k, z], misc_sem + k * 4 + z, dev)
    local(lambda: misc_in, lambda: MISC.at[k, z], misc_sem + k * 4 + z)
    w_qkv.push()
    pltpu.make_async_copy(x_in, H, rs.at[stage]).wait()
    XS[...] = H[...].astype(BF)
    half_rows = T // 2
    xh_sem, x_sem = new_recv(1), new_recv(4)
    part_of = lambda core: pl.ds(mo(core * half_rows, 16), half_rows)
    send(lambda: XS.at[:, part_of(1 - k)], lambda: XH, xh_sem, mate)
    for i in range(2):
        mine = is_near & (zs == i)
        src, dst = lambda i=i: XS.at[i, part_of(k)], lambda: XR.at[zs, part_of(k)]
        send(src, dst, x_sem + zs * 2 + k, at(d, zk, 2 * k + i), jnp.logical_not(mine))
        local(src, dst, x_sem + zs * 2 + k, mine)
    pltpu.make_async_copy(cot_in, ACC, rs.at[stage + 1]).wait()
    CS[...] = ACC[...].astype(BF)

    V8[...] = jnp.zeros_like(V8)
    SQ[...] = jnp.zeros_like(SQ)

    b_out, ln1_g, ln1_b, ln2_g, ln2_b, b_proj = (
        v[...].reshape(1, D) for v in (b_out, ln1_g, ln1_b, ln2_g, ln2_b, b_proj)
    )

    w_qkv.hop()
    arrive(lambda: XH, xh_sem)
    for i in range(2):
        send(lambda i=i: XH.at[i], dst, x_sem + zs * 2 + k, at(d, zk, 2 * (1 - k) + i))
    w_qkv.forward()
    w_qkv.relay()

    RB = 128
    a1_sem = new_recv(2)

    def rows_of(base, i, n):
        return pl.ds(mo(base + i * n, 16), n)

    for s in range(2):
        for core in range(2):
            here = is_near & (zs == s) & (k == core)
            arrive(lambda: XR.at[s, part_of(core)], x_sem + s * 2 + core, jnp.logical_not(here))
            arrive_local(lambda: XR.at[s, part_of(core)], x_sem + s * 2 + core, here)

        def first_norm(i, c):
            scaled, _ = norm_stats(XR[s, rows_of(0, i, RB), :].astype(F32))
            A1[rows_of(own + s * T, i, RB), :] = (scaled * ln1_g + ln1_b).astype(BF)
            return c

        lax.fori_loop(0, T // RB, first_norm, 0)
        mine = lambda s=s: A1.at[pl.ds(mo(own + s * T, 16), T), :]
        send(mine, mine, a1_sem + s, mate)

    for r in range(2):
        for c in range(4):
            here = (k == r) & (z == c)
            arrive(lambda: MISC.at[r, c], misc_sem + r * 4 + c, jnp.logical_not(here))
            arrive_local(lambda: MISC.at[r, c], misc_sem + r * 4 + c, here)
    pair_misc = MISC[0, 2 * k] + MISC[0, 2 * k + 1]
    bias_q, bias_v = pair_misc[1:2, :HC], pair_misc[1:2, HC:]
    length = MISC[zk, 0, pl.ds(2 + zs, 1), :][:, 0:1]

    w_qkv.ready()

    def project(base):
        rows = pl.ds(mo(base, 16), 2 * T)
        a = A1[rows, :]
        QKV[0, rows, :] = ((dot_t(a, WQ[0]) + bias_q).astype(BF).astype(F32) * (HEAD_DIM**-0.5)).astype(BF)
        QKV[1, rows, :] = dot_t(a, WQ[1]).astype(BF)
        QKV[2, rows, :] = (dot_t(a, WQ[2]) + bias_v).astype(BF)

    project(own)
    for s in range(2):
        arrive(lambda: A1.at[pl.ds(mo(other + s * T, 16), T), :], a1_sem + s)
    w_out.push()
    w_fc.push()
    project(other)

    key_place = lax.broadcasted_iota(jnp.int32, (L, 128), 0).astype(F32)
    KB[...] = jnp.where(key_place < length, 0.0, MASKED)

    QB = T
    NQ = L // QB
    low_lane = lax.broadcasted_iota(jnp.int32, (1, 128), 1) < HEAD_DIM
    low_row = lax.broadcasted_iota(jnp.int32, (128, 1), 0) < HEAD_DIM
    diag = lax.broadcasted_iota(jnp.int32, (QB, QB), 0) <= lax.broadcasted_iota(jnp.int32, (QB, QB), 1)

    def keep_lane(v, h):
        return jnp.where(low_lane if h == 0 else jnp.logical_not(low_lane), v, jnp.zeros_like(v))

    def scores_t(kp, qm, qb):
        kv = (qb + 1) * QB
        s = dot_t(kp[:kv], qm)
        kb = KB[0:kv, :]
        s = s + jnp.concatenate([kb] * (QB // 128), axis=1)
        last = jnp.where(diag, s[kv - QB :], MASKED)
        if qb == 0:
            return last
        return jnp.concatenate([s[: kv - QB], last], axis=0)

    def send_cot():
        return line_send(lambda i: CS.at[i], lambda i: GF.at[pl.ds(mo(z * T, 16), T), :])

    between = {
        (0, 3): (w_out.hop, w_fc2.push),
        (1, 0): (w_fc.hop,),
        (1, 2): (w_out.forward, w_proj.push),
        (1, 3): (w_fc.forward, w_fc2.hop),
        (2, 0): (w_out.relay, w_proj2.push),
        (2, 2): (w_fc.relay, w_proj.hop),
        (2, 3): (w_fc2.forward,),
    }

    def attend(p, c):
        lanes = pl.ds(mo(p * 128, 128), 128)
        kp, vp = QKV[1, :, lanes], QKV[2, :, lanes]
        vt = vp.T
        for qb in range(NQ):
            for (step, at_qb), work in between.items():
                if at_qb == qb:

                    @pl.when(p == step)
                    def _():
                        for do in work:
                            do()

            kv = (qb + 1) * QB
            qp = QKV[0, qb * QB : kv, lanes]
            parts = []
            for h in range(2):
                s = scores_t(kp, keep_lane(qp, h), qb)
                top = jnp.max(s, axis=0, keepdims=True)
                e = jnp.exp(s - top)
                total = jnp.sum(e, axis=0, keepdims=True)
                LSE[pl.ds(2 * p + h, 1), qb * QB : kv] = top + jnp.log(total)
                parts.append(dot(vt[:, :kv], e.astype(BF)) / total)
            CTX[qb * QB : kv, lanes] = jnp.where(low_row, parts[0], parts[1]).T.astype(BF)
        return c

    lax.fori_loop(0, HC // 128, attend, 0)
    w_proj2.hop()

    def split_other(n, product):
        base = new_recv(2)
        PS[n] = product(pl.ds(mo(other, 16), 2 * T)).astype(BF).reshape(2, T, D)
        for s in range(2):
            send(lambda s=s: PS.at[n, s], lambda s=s: PR.at[n, s], base + s, mate)
        return base

    def split_own(product):
        ACC[...] = product(pl.ds(mo(own, 16), 2 * T)).reshape(2, T, D)

    def split_sum(n, product):
        base = split_other(n, product)
        split_own(product)
        return base

    def split_wait(n, base, s):
        arrive(lambda: PR.at[n, s], base + s)

    w_out.ready()
    ex = split_sum(0, lambda rows: dot(CTX[rows, :], WO[...]))
    w_proj.forward()
    cot_sem = send_cot()
    sent = len(pending)
    a2_sem = new_recv(2)
    for s in range(2):
        split_wait(0, ex, s)

        def second_norm(i, c):
            rows = rows_of(0, i, RB)
            h = XR[s, rows, :].astype(F32) + ACC[s, rows, :] + PR[0, s, rows, :].astype(F32) + b_out
            H[s, rows, :] = h
            scaled, _ = norm_stats(h)
            A2[rows_of(own + s * T, i, RB), :] = (scaled * ln2_g + ln2_b).astype(BF)
            return c

        lax.fori_loop(0, T // RB, second_norm, 0)
        mine = lambda s=s: A2.at[pl.ds(mo(own + s * T, 16), T), :]
        send(mine, mine, a2_sem + s, mate)

    VF[...] = jnp.concatenate([MISC[0, 2 * k, 0:1, :], MISC[0, 2 * k + 1, 0:1, :]], axis=1)

    def hidden(base, start, width):
        rows = pl.ds(mo(base, 16), 2 * T)

        def body(i, c):
            cs = pl.ds(mo(i * FC + start, 128), width)
            u = dot(A2[rows, :], WF[:, :, cs].reshape(D, width)) + VF[:, cs]
            t = jnp.tanh(GELU_C * (u + GELU_A * u * u * u))
            M[rows, cs] = (0.5 * u * (1.0 + t)).astype(BF)
            SL[rows, cs] = (
                0.5 * (1.0 + t) + 0.5 * u * (1.0 - t * t) * GELU_C * (1.0 + 3.0 * GELU_A * u * u)
            ).astype(BF)
            return c

        lax.fori_loop(0, 2, body, 0)

    w_fc.ready()
    hidden(own, 0, first)
    w_fc2.relay()
    for s in range(2):
        arrive(lambda: A2.at[pl.ds(mo(other + s * T, 16), T), :], a2_sem + s)
    hidden(other, 0, first)
    w_proj2.forward()
    w_proj.relay()
    w_fc2.ready()
    hidden(own, first, FC - first)
    w_proj2.relay()
    hidden(other, first, FC - first)
    gf_sem = new_recv(2)
    for s in range(2):
        line_wait(lambda i: GF.at[pl.ds(mo(own + i * T, 16), T), :], cot_sem, s)

        def mask_rows(i, c):
            rows = rows_of(own + s * T, i, RB)
            place = (lax.broadcasted_iota(jnp.int32, (RB, 1), 0) + (own + s * T + i * RB)).astype(F32)
            g = jnp.where(place < length, GF[rows, :].astype(F32), 0.0)
            GF[rows, :] = g.astype(BF)
            V8[V_BPROJ] += fold8(g)
            return c

        lax.fori_loop(0, T // RB, mask_rows, 0)
        mine = lambda s=s: GF.at[pl.ds(mo(own + s * T, 16), T), :]
        send(mine, mine, gf_sem + s, mate)

    w_proj.ready()
    w_proj2.ready()
    mlp_rows = lambda rows: dot(M[rows, :], WP[...])
    mlp_ex = split_other(1, mlp_rows)
    for s in range(2):
        arrive(lambda: GF.at[pl.ds(mo(other + s * T, 16), T), :], gf_sem + s)

    bit = (lax.rem(dq, 2), dq // 2)

    def wide_factors(count, width):
        return [jnp.concatenate([FAC[dq ^ j, 0:1, :]] * (width // 128), axis=1) for j in range(count)]

    class Part:
        def __init__(self, plane, S, B, U, Z, E, slab, piece, place):
            self.S, self.B, self.U, self.Z, self.E = S, B, U, Z, E
            self.slab, self.piece, self.place = slab, piece, place
            self.pair, self.zsem, self.end = new_recv(1), new_recv(2), new_recv(4)
            self.setup(*plane)

        def pass_on(self):
            send(lambda: self.slab(1 - zs), lambda: self.B, self.pair, at(d, k, z ^ 1))

        def middle(self):
            arrive(lambda: self.B, self.pair)
            self.U[...] = (self.slab(zs)[...].astype(F32) + self.B[...].astype(F32)).astype(BF)
            for r in range(2):
                mine = (far == 0) & (r == k)
                piece = lambda r=r: self.piece(r)
                send(piece, lambda: self.Z.at[far], self.zsem + far, at(d, r, target), jnp.logical_not(mine))
                local(piece, lambda: self.Z.at[far], self.zsem + far, mine)

        def finish(self):
            arrive(lambda: self.Z.at[0], self.zsem, is_far)
            arrive_local(lambda: self.Z.at[0], self.zsem, is_near)
            arrive(lambda: self.Z.at[1], self.zsem + 1)
            self.E[...] = (self.Z[0].astype(F32) + self.Z[1].astype(F32)).astype(BF)
            for j in (1, 2, 3):
                send(lambda: self.E, lambda: self.place(dq), self.end + j, quad[j - 1])
            local(lambda: self.E, lambda: self.place(dq), self.end)

        def done(self):
            arrive_local(lambda: self.place(dq), self.end)
            for j in (1, 2, 3):
                arrive(lambda: self.place(dq ^ j), self.end + j)

    class DirectPart(Part):
        def setup(self, G, R):
            self.G, self.R, self.raw = G, R, new_recv(3)

        def quarter(self, q):
            return self.G.at[:, q // 2, lax.rem(q, 2)]

        def spread(self):
            for j in (1, 2, 3):
                send(lambda j=j: self.quarter(dq ^ j), lambda j=j: self.R.at[j - 1], self.raw + j - 1, quad[j - 1])

        def reduce(self):
            for j in (1, 2, 3):
                arrive(lambda: self.R.at[j - 1], self.raw + j - 1)
            G, (_, n, width) = self.quarter(dq), self.S.shape
            factors, steps = wide_factors(QUAD, width), n // 16

            def add(i, c):
                a, rows = i // steps, pl.ds(mo(lax.rem(i, steps) * 16, 16), 16)
                v = G[a, rows, :].astype(F32) * factors[0]
                for j in (1, 2, 3):
                    v = v + self.R[j - 1, a, rows, :].astype(F32) * factors[j]
                self.S[a, rows, :] = v.astype(BF)
                return c

            lax.fori_loop(0, 2 * steps, add, 0)
            self.pass_on()

    class CrossPart(Part):
        def setup(self, G, X, O, Y):
            self.G, self.X, self.O, self.Y = G, X, O, Y
            self.raw, self.cross = new_recv(2), new_recv(2)

        def spread(self, cond=True):
            send(lambda: self.G.at[0, :, 1 - bit[0]], lambda: self.X.at[0], self.raw, quad[0], cond)
            send(lambda: self.G.at[1, 1 - bit[1]], lambda: self.X.at[1], self.raw + 1, quad[1], cond)

        def scale(self):
            _, n, width = self.S.shape
            factors = wide_factors(3, width)
            for a in range(2):
                arrive(lambda: self.X.at[a], self.raw + a)

                def add(i, c, a=a):
                    rows = pl.ds(mo(i * 16, 16), 16)
                    for b, to in ((bit[1 - a], self.S), (1 - bit[1 - a], self.O)):
                        mine = self.G[0, b, bit[0], rows, :] if a == 0 else self.G[1, bit[1], b, rows, :]
                        v = mine.astype(F32) * factors[0] + self.X[a, b, rows, :].astype(F32) * factors[1 + a]
                        to[a, rows, :] = v.astype(BF)
                    return c

                lax.fori_loop(0, n // 16, add, 0)
                send(lambda a=a: self.O.at[a], lambda a=a: self.Y.at[a], self.cross + a, quad[1 - a])

        def reduce(self):
            for a in range(2):
                arrive(lambda: self.Y.at[a], self.cross + a)
            self.S[...] = (self.S[...].astype(F32) + self.Y[...].astype(F32)).astype(BF)
            self.pass_on()

    g_proj = DirectPart(
        (GWP, RP), SPW, BP, UP, ZP, EP,
        lambda cs: SPW.at[cs],
        lambda r: UP.at[:, cols(r)],
        lambda q: gp_out.at[pl.ds(mo(q * p192, 16), p192), :],
    )
    g_out = CrossPart(
        (GWO, XO, OO, YO), SOW, BO, UO, ZO, EO,
        lambda cs: SOW.at[cs],
        lambda r: UO.at[:, cols(r)],
        lambda q: go_out.at[pl.ds(mo(q * o48, 16), o48), :],
    )

    def fc_grad(plane, S, B, U, Z, E, start, n):
        return CrossPart(
            plane, S, B, U, Z, E,
            lambda cs: S.at[:, :, pl.ds(mo(cs * FC, 128), FC)],
            lambda r: U.at[r],
            lambda q: gf_out.at[pl.ds(mo(start + q * n, 16), n), :],
        )

    g_fc = fc_grad((GWF, XF, OF, YF), SFW, BF1, UF, ZF, EF, 0, 128 // QUAD)
    g_fc2 = fc_grad((GWF2, XF2, OF2, YF2), SFW2, BF2, UF2, ZF2, EF2, 128, (FR - 128) // QUAD)

    def qkv_grad(i):
        return CrossPart(
            [v.at[i] for v in (GWQ, XQ, OQ, YQ)],
            *(v.at[i] for v in (SQW, BQ, UQ, ZQ, EQ)),
            lambda cs: SQW.at[i, cs],
            lambda r: UQ.at[i, :, cols(r)],
            lambda q: gq_out.at[i, pl.ds(mo(q * q48, 16), q48), :],
        )

    g_qkv = [qkv_grad(i) for i in range(3)]

    def grad_proj(i, c):
        cs = pl.ds(mo(i * (FC // 2), 128), FC // 2)
        g = t_dot(M[:, cs], GF[...])
        SQ[...] += fold8(g * g)
        GWP[i // 2, lax.rem(i, 2)] = g.astype(BF).reshape(2, p192, D)
        return c

    lax.fori_loop(0, 4, grad_proj, 0)
    g_proj.spread()

    NB = 512
    NN = FH // NB

    def grad_hidden(i, c):
        rows = pl.ds(mo(i // NN * 2 * T, 16), 2 * T)
        cs = pl.ds(mo(lax.rem(i, NN) * NB, 128), NB)
        g = dot_t(GF[rows, :], WP[cs, :]) * SL[rows, cs].astype(F32)
        low = g.astype(BF)
        SL[rows, cs] = low
        VF[:, cs] = jnp.where(i < NN, 0.0, VF[:, cs]) + jnp.sum(low.astype(F32), axis=0, keepdims=True)
        return c

    lax.fori_loop(0, 2 * NN, grad_hidden, 0)
    ex = split_sum(2, lambda rows: dot_t(SL[rows, :], WF[...].reshape(D, FH)))

    ga_sem = new_recv(2)
    for s in range(2):
        split_wait(2, ex, s)

        def second_back(i, c):
            rows = rows_of(0, i, RB)
            full = rows_of(own + s * T, i, RB)
            up = ACC[s, rows, :] + PR[2, s, rows, :].astype(F32)
            scaled, inverse = norm_stats(H[s, rows, :])
            through = up * ln2_g
            V8[V_LN2G] += fold8(up * scaled)
            V8[V_LN2B] += fold8(up)
            g = GF[full, :].astype(F32) + inverse * (
                through
                - jnp.mean(through, axis=-1, keepdims=True)
                - scaled * jnp.mean(through * scaled, axis=-1, keepdims=True)
            )
            V8[V_BOUT] += fold8(g)
            HG[s, rows, :] = g
            GA[full, :] = g.astype(BF)
            return c

        lax.fori_loop(0, T // RB, second_back, 0)
        mine = lambda s=s: GA.at[pl.ds(mo(own + s * T, 16), T), :]
        send(mine, mine, ga_sem + s, mate)
    split_own(mlp_rows)
    flush(sent)
    LO, GI = CS, XS
    for s in range(2):
        split_wait(1, mlp_ex, s)

        def output_rows(i, c):
            rows = rows_of(0, i, RB)
            LO[s, rows, :] = (H[s, rows, :] + ACC[s, rows, :] + PR[1, s, rows, :].astype(F32) + b_proj).astype(BF)
            return c

        lax.fori_loop(0, T // RB, output_rows, 0)
    lo_sem = line_send(lambda i: LO.at[i], lambda i: lo_out.at[i])

    for s in range(2):
        arrive(lambda: GA.at[pl.ds(mo(other + s * T, 16), T), :], ga_sem + s)

    GCTX[...] = dot_t(GA[...], WO[...]).astype(BF)
    g = t_dot(CTX[...], GA[...])
    SQ[...] += fold8(g * g)
    GWO[...] = g.astype(BF).reshape(2, 2, 2, o48, D)
    g_out.spread()

    def grad_fc(G, start, n):
        g = t_dot(jnp.concatenate([A2[:, start : start + n], A2[:, FR + start : FR + start + n]], axis=1), SL[...])
        q = fold8(g * g)
        SQ[...] += q[:, :D] + q[:, D:]
        G[...] = g.astype(BF).reshape(2, 2, 2, n // QUAD, FH)

    grad_fc(GWF, 0, 128)
    g_fc.spread()

    def attend_back(p):
        lanes = pl.ds(mo(p * 128, 128), 128)
        kp, vp = QKV[1, :, lanes], QKV[2, :, lanes]
        kt = kp.T
        DK[...] = jnp.zeros_like(DK)
        DV[...] = jnp.zeros_like(DV)
        for qb in range(NQ):
            kv = (qb + 1) * QB
            qp = QKV[0, qb * QB : kv, lanes]
            do = GCTX[qb * QB : kv, lanes]
            dqt = []
            for h in range(2):
                qm, dm = keep_lane(qp, h), keep_lane(do, h)
                pt = jnp.exp(scores_t(kp, qm, qb) - LSE[pl.ds(2 * p + h, 1), qb * QB : kv])
                gp = dot_t(vp[:kv], dm)
                both = pt * gp
                gs = (both - pt * jnp.sum(both, axis=0, keepdims=True)).astype(BF)
                DV[0:kv, :] += dot(pt.astype(BF), dm)
                DK[0:kv, :] += dot(gs, qm)
                dqt.append(dot(kt[:, :kv], gs))
            GQKV[0, qb * QB : kv, lanes] = (
                jnp.where(low_row, dqt[0], dqt[1]).T * (HEAD_DIM**-0.5)
            ).astype(BF)
        GQKV[1, :, lanes] = DK[...].astype(BF)
        GQKV[2, :, lanes] = DV[...].astype(BF)

    def attend_back_step(p, c):
        attend_back(p)
        return c

    lax.fori_loop(0, HC // 128, attend_back_step, 0)

    def grad_norm_in(rows):
        return dot(GQKV[0, rows, :], WQ[0]) + dot(GQKV[1, rows, :], WQ[1]) + dot(GQKV[2, rows, :], WQ[2])

    ex = split_sum(3, grad_norm_in)
    grad_fc(GWF2, 128, FR - 128)
    g_fc2.spread(k == 0)
    for s in range(2):
        split_wait(3, ex, s)

        def first_back(i, c):
            rows = rows_of(0, i, RB)
            up = ACC[s, rows, :] + PR[3, s, rows, :].astype(F32)
            scaled, inverse = norm_stats(XR[s, rows, :].astype(F32))
            through = up * ln1_g
            V8[V_LN1G] += fold8(up * scaled)
            V8[V_LN1B] += fold8(up)
            g = HG[s, rows, :] + inverse * (
                through
                - jnp.mean(through, axis=-1, keepdims=True)
                - scaled * jnp.mean(through * scaled, axis=-1, keepdims=True)
            )
            GI[s, rows, :] = g.astype(BF)
            return c

        lax.fori_loop(0, T // RB, first_back, 0)

    send_gi = lambda b: line_send(lambda i: GI.at[i, part_of(b)], lambda i: gi_out.at[i, part_of(b)])
    gi_sems = [send_gi(0)]

    def grad_qkv(i, c):
        g = t_dot(GQKV[i], A1[...])
        SQ[...] += fold8(g * g)
        GWQ[i] = g.astype(BF).reshape(2, 2, 2, q48, D)
        return c

    lax.fori_loop(0, 3, grad_qkv, 0)
    VK[k] = jnp.zeros(VK.shape[1:], F32)
    for i in range(6):
        VK[k, i : i + 1, :] = jnp.sum(V8[i], axis=0, keepdims=True)
    VK[k, V_BQV : V_BQV + 1, :] = jnp.concatenate(
        [jnp.sum(GQKV[i].astype(F32), axis=0, keepdims=True) for i in (0, 2)], axis=1
    )
    VK[k, V_BFC : V_BFC + 1, :] = VF[:, :D]
    VK[k, V_BFC + 1 : V_BFC + 2, :] = VF[:, D:]
    VK[k, V_SQ : V_SQ + 1, :] = jnp.sum(SQ[...], axis=0, keepdims=True)
    vk_sem = new_recv(1)
    send(lambda: VK.at[k], lambda: VK.at[k], vk_sem, mate)
    arrive(lambda: VK.at[1 - k], vk_sem)
    va, vb = VK[0], VK[1]
    pack = jnp.concatenate([va[0:6] + vb[0:6], va[6:9], vb[6:9]], axis=0)
    squares = jnp.sum(jnp.sum(pack * pack, axis=0, keepdims=True) + va[9:10] + vb[9:10], axis=1, keepdims=True)
    norm = jnp.sqrt(squares)
    factor = CLIP_BOUND / jnp.maximum(norm, CLIP_BOUND)
    FAC[dq] = jnp.broadcast_to(factor, (8, 128))
    fac_sem, vp_sem = new_recv(3), new_recv(3)
    for j in (1, 2, 3):
        for dev in (quad[j - 1], quad_mates[j - 1]):
            send(lambda: FAC.at[dq], lambda: FAC.at[dq], fac_sem + j - 1, dev, k == 1)
    VP[dq] = jnp.concatenate([pack, jnp.zeros((4, D), F32)], axis=0)
    for j in (1, 2, 3):
        arrive(lambda: FAC.at[dq ^ j], fac_sem + j - 1)

    order = [g_proj, g_out, g_fc, g_fc2, *g_qkv]
    g_proj.reduce()
    g_out.scale()
    g_fc.scale()
    g_fc2.spread(k == 1)
    for part in g_qkv:
        part.spread()
    for j in (1, 2, 3):
        send(lambda: VP.at[dq], lambda: VP.at[dq], vp_sem + j - 1, quad[j - 1])
    g_out.reduce()
    g_fc.reduce()
    g_proj.middle()
    g_out.middle()
    g_fc.middle()
    gi_sems.append(send_gi(1))
    for part in (g_fc2, *g_qkv):
        part.scale()
    g_proj.finish()
    g_fc2.reduce()
    for j in (1, 2, 3):
        arrive(lambda: VP.at[dq ^ j], vp_sem + j - 1)
    total = jnp.zeros((12, D), F32)
    for q in range(QUAD):
        total = total + VP[q, 0:12, :] * FAC[q, 0:1, 0:1]
    VZ[z] = jnp.concatenate([total, jnp.broadcast_to(norm, (4, D))], axis=0)
    vz_sem = new_recv(3)
    for j in (1, 2, 3):
        send(lambda: VZ.at[z], lambda: VZ.at[z], vz_sem + j - 1, at(d, k, z ^ j))
    for part in g_qkv:
        part.reduce()
    g_out.finish()
    g_fc.finish()
    g_fc2.middle()
    for part in g_qkv:
        part.middle()
    g_fc2.finish()
    for part in g_qkv:
        part.finish()

    for j in (1, 2, 3):
        arrive(lambda: VZ.at[z ^ j], vz_sem + j - 1)
    total = VZ[0] + VZ[1] + VZ[2] + VZ[3]
    vec_out[0:6, :] = total[0:6]
    V8[0, 0:6, :] = total[6:12]
    vec_out[6:7, :] = V8[0, pl.ds(V_BFC - V_BQV + 3 * zk + zs, 1), :]
    pair = V8[0, pl.ds(3 * zk, 1), :]
    spare = jnp.zeros((1, D - QR), F32)
    for i in range(2):
        a, b = pair[:, i * HC : i * HC + QR], pair[:, i * HC + QR : (i + 1) * HC]
        vec_out[7 + i : 8 + i, :] = jnp.concatenate([jnp.where(zs == 0, a, b), spare], axis=1)
    first_place = lax.broadcasted_iota(jnp.int32, (1, D), 1) == 0
    vec_out[9:10, :] = jnp.where(
        first_place, VZ[2 * k, V_NORM : V_NORM + 1, :], VZ[2 * k + 1, V_NORM : V_NORM + 1, :]
    )
    vec_out[10:12, :] = jnp.zeros((2, D), F32)

    for part in order:
        part.done()
    for i in range(2):
        line_wait(lambda i: lo_out.at[i], lo_sem, i)
        for b in range(2):
            line_wait(lambda i: gi_out.at[i, part_of(b)], gi_sems[b], i)
    flush(len(pending))


def widen(*refs):
    low, vec, wide, (b_out, ln1_g, ln1_b, ln2_g, ln2_b, b_proj, b_fc, b_qv, norms) = (
        refs[:6], refs[6], refs[7:13], refs[13:22]
    )
    before, after, sems = refs[22:28], refs[28:34], refs[34]
    parts = []
    for i, v in enumerate(low):
        parts += [(i, (e,)) for e in range(2)] if i < 2 else [(i, (...,))]

    def load(n, i, at):
        return pltpu.make_async_copy(low[i].at[at], before[i].at[at], sems.at[2 * n])

    def store(n, i, at):
        return pltpu.make_async_copy(after[i].at[at], wide[i].at[at], sems.at[2 * n + 1])

    for n, (i, at) in enumerate(parts):
        load(n, i, at).start()
    for row, out in enumerate((b_out, ln1_g, ln1_b, ln2_g, ln2_b, b_proj, b_fc)):
        out[...] = vec[row, :]
    b_qv[...] = vec[7:9, : b_qv.shape[1]]
    norms[...] = vec[9, :2]
    for n, (i, at) in enumerate(parts):
        load(n, i, at).wait()
        after[i][at] = before[i][at].astype(F32)
        store(n, i, at).start()
    for n, (i, at) in enumerate(parts):
        store(n, i, at).wait()


def shards(
    layer_in, w_qkv, b_qv, w_out, b_out, ln1_g, ln1_b, ln2_g, ln2_b, w_fc, b_fc, w_proj, b_proj, lengths, cotangent
):
    E, T, D = layer_in.shape
    n_col, n_row = lax.axis_size("col"), lax.axis_size("row")
    assert lax.axis_size("dp") == QUAD and n_col == 4 and n_row % 2 == 0
    pairs = n_row // 2
    r = lax.axis_index("row")
    core = lax.rem(r, 2)
    half_rows = w_fc.shape[0] * pairs

    def halves(w, axis):
        if pairs == 1:
            return w
        whole = lax.all_gather(w, "row", axis=axis, tiled=True)
        return lax.dynamic_slice_in_dim(whole, core * half_rows, half_rows, axis)

    w_qkv, w_out, w_fc, w_proj = halves(w_qkv, 0), halves(w_out, 1), halves(w_fc, 0), halves(w_proj, 1)
    L = T * n_col
    HQ = w_qkv.shape[2]
    HC = HQ * n_col // 2
    FQ = w_fc.shape[1]
    FH = FQ * n_col // 2
    DH = w_fc.shape[0]
    wq_t = jnp.transpose(w_qkv, (1, 2, 0))
    q48, o48, p192 = HQ // QUAD, HQ // QUAD, FQ // QUAD
    fa, fb = 128 // QUAD, (DH - 128) // QUAD

    anyspec = pl.BlockSpec(memory_space=pl.ANY)
    vm = pl.BlockSpec(memory_space=pltpu.VMEM)
    V = pltpu.VMEM
    outs = pl.pallas_call(
        kernel,
        name="layer",
        out_shape=(
            jax.ShapeDtypeStruct((E, T, D), BF),
            jax.ShapeDtypeStruct((E, T, D), BF),
            jax.ShapeDtypeStruct((3, HQ, DH), BF),
            jax.ShapeDtypeStruct((HQ, DH), BF),
            jax.ShapeDtypeStruct((DH, FQ), BF),
            jax.ShapeDtypeStruct((FQ, DH), BF),
            jax.ShapeDtypeStruct((12, D), F32),
        ),
        in_specs=[anyspec] * 6 + [vm, vm, pl.BlockSpec(memory_space=pltpu.SMEM)] + [vm] * 6,
        out_specs=(anyspec,) * 6 + (vm,),
        scratch_shapes=[
            V((2, T, D), BF),
            V((2, T // 2, D), BF),
            V((2, T, D), BF),
            V((8, D), F32),
            V((2, T, D), BF),
            V((2, T, D), F32),
            V((2, T, D), F32),
            V((L, D), BF),
            V((3, HC, D), BF),
            V((HC, D), BF),
            V((2, DH, FH), BF),
            V((FH, D), BF),
            V((2, n_col, 8, D), F32),
            V((3, L, HC), BF),
            V((L, HC), BF),
            V((8, L), F32),
            V((L, 128), F32),
            V((2, T, D), F32),
            V((4, 2, T, D), BF),
            V((4, 2, T, D), BF),
            V((L, D), BF),
            V((L, FH), BF),
            V((L, FH), BF),
            V((L, D), BF),
            V((L, D), BF),
            V((L, HC), BF),
            V((3, L, HC), BF),
            V((L, 128), F32),
            V((L, 128), F32),
            V((6, 8, D), F32),
            V((8, D), F32),
            V((1, FH), F32),
            V((2, 16, D), F32),
            V((QUAD, 8, 128), F32),
            V((QUAD, 16, D), F32),
            V((n_col, 16, D), F32),
            V((3, 2, 2, 2, q48, D), BF),
            V((2, 2, 2, o48, D), BF),
            V((2, 2, 2, fa, FH), BF),
            V((2, 2, 2, fb, FH), BF),
            V((2, 2, 2, p192, D), BF),
            V((3, 2, p192, D), BF),
            *[
                V(shape, BF)
                for shape in ((3, 2, 2, q48, D), (2, 2, o48, D), (2, 2, fa, FH), (2, 2, fb, FH))
            ],
            *[
                V(shape, BF)
                for _ in "OY"
                for shape in ((3, 2, q48, D), (2, o48, D), (2, fa, FH), (2, fb, FH))
            ],
            V((3, 2, q48, D), BF),
            V((2, o48, D), BF),
            V((2, fa, FH), BF),
            V((2, fb, FH), BF),
            V((2, p192, D), BF),
            *[
                V(shape, BF)
                for _ in "BU"
                for shape in ((3, q48, D), (o48, D), (2, fa, FQ), (2, fb, FQ), (p192, D))
            ],
            V((3, 2, q48, DH), BF),
            V((2, o48, DH), BF),
            V((2, fa, FQ), BF),
            V((2, fb, FQ), BF),
            V((2, p192, DH), BF),
            V((3, q48, DH), BF),
            V((o48, DH), BF),
            V((fa, FQ), BF),
            V((fb, FQ), BF),
            V((p192, DH), BF),
            pltpu.SemaphoreType.DMA((240,)),
            pltpu.SemaphoreType.DMA((240,)),
        ],
        compiler_params=pltpu.CompilerParams(
            collective_id=0, has_side_effects=True, vmem_limit_bytes=63 * 2**20
        ),
    )(
        layer_in, cotangent, wq_t, w_out, w_fc, w_proj, b_fc, b_qv, lengths,
        b_out, ln1_g, ln1_b, ln2_g, ln2_b, b_proj,
    )
    low, vec = outs[:6], outs[6]
    line = jax.ShapeDtypeStruct((D,), F32)
    outs = pl.pallas_call(
        widen,
        name="widen",
        out_shape=(
            *(jax.ShapeDtypeStruct(v.shape, F32) for v in low),
            *(line,) * 7,
            jax.ShapeDtypeStruct((2, HQ), F32),
            jax.ShapeDtypeStruct((2,), F32),
        ),
        in_specs=[anyspec] * 6 + [vm],
        out_specs=(anyspec,) * 6 + (vm,) * 9,
        scratch_shapes=[
            *(V(v.shape, BF) for v in low), *(V(v.shape, F32) for v in low), pltpu.SemaphoreType.DMA((16,))
        ],
        compiler_params=pltpu.CompilerParams(vmem_limit_bytes=63 * 2**20),
    )(*low, vec)
    lo, gi, gq, go, gf, gp = outs[:6]
    vec, norms = outs[6:14], outs[14]
    gq = jnp.transpose(gq, (2, 0, 1))
    if pairs > 1:
        groups = [[2 * p + q for p in range(pairs)] for q in range(2)]
        cores = [[2 * p, 2 * p + 1] for p in range(pairs)]
        gq, go, gf, gp, *vec = (
            lax.psum(v, "row", axis_index_groups=groups) for v in (gq, go, gf, gp, *vec)
        )

        def share(v, axis):
            whole = lax.all_gather(v, "row", axis=axis, tiled=True, axis_index_groups=cores)
            part = whole.shape[axis] // n_row
            return lax.dynamic_slice_in_dim(whole, r * part, part, axis)

        gq, go, gf, gp = share(gq, 0), share(go, 1), share(gf, 0), share(gp, 1)
    gb_out, g1, b1, g2, b2, gb_proj, gb_fc, gb_qv = vec
    return (lo, gi, norms, gq, gb_qv, go, gb_out, g1, b1, g2, b2, gf, gb_fc, gp, gb_proj)


def solution(mesh):
    in_specs = (
        P(("dp", "row"), "col", None),
        P("row", None, "col"),
        P(None, "col"),
        P("col", "row"),
        P(),
        P(),
        P(),
        P(),
        P(),
        P("row", "col"),
        P("col"),
        P("col", "row"),
        P(),
        P(("dp", "row")),
        P(("dp", "row"), "col", None),
    )
    out_specs = (
        P(("dp", "row"), "col", None),
        P(("dp", "row"), "col", None),
        P(("dp", "row")),
        P("row", None, "col"),
        P(None, "col"),
        P("col", "row"),
        P(),
        P(),
        P(),
        P(),
        P(),
        P("row", "col"),
        P("col"),
        P("col", "row"),
        P(),
    )
    return jax.shard_map(shards, mesh=mesh, in_specs=in_specs, out_specs=out_specs, check_vma=False)
```

```python
import functools

import jax
import jax.numpy as jnp
from jax import lax
from jax.experimental import pallas as pl
from jax.experimental.pallas import tpu as pltpu
from jax.sharding import PartitionSpec as P

MESH = pl.DeviceIdType.MESH
EPSILON = 1e-05
CLIP_BOUND = 1.0
GELU_C = 0.7978845608028654
GELU_A = 0.044715
MASKED = -1e30
HEAD_DIM = 64
QUAD = 4
BF = jnp.bfloat16
F32 = jnp.float32

V_BOUT, V_LN1G, V_LN1B, V_LN2G, V_LN2B, V_BPROJ, V_BQV, V_BFC, V_SQ = 0, 1, 2, 3, 4, 5, 6, 7, 9
V_NORM = 12


def dot(a, b):
    return lax.dot_general(a, b, (((1,), (0,)), ((), ())), preferred_element_type=F32)


def dot_t(a, b):
    return lax.dot_general(a, b, (((1,), (1,)), ((), ())), preferred_element_type=F32)


def t_dot(a, b):
    return lax.dot_general(a, b, (((0,), (0,)), ((), ())), preferred_element_type=F32)


def fold8(v):
    return jnp.sum(v.reshape(v.shape[0] // 8, 8, v.shape[1]), axis=0)


def norm_stats(v):
    center = v - jnp.mean(v, axis=-1, keepdims=True)
    inverse = lax.rsqrt(jnp.mean(center * center, axis=-1, keepdims=True) + EPSILON)
    return center * inverse, inverse


def kernel(
    x_in, cot_in, wq_in, wo_in, wf_in, wp_in, bfc_in, bqv_in, len_in, b_out, ln1_g, ln1_b, ln2_g, ln2_b, b_proj,
    lo_out, gi_out, gq_out, go_out, gf_out, gp_out, vec_out,
    XS, XH, CS, misc_in, XR, H, HG, A1, WQ, WO, WF, WP, MISC, QKV, CTX, LSE, KB, ACC,
    PS, PR, A2, M, SL, GF, GA, GCTX, GQKV, DK, DV,
    V8, SQ, VF, VK, FAC, VP, VZ,
    GWQ, GWO, GWF, GWF2, GWP, RP, XQ, XO, XF, XF2, OQ, OO, OF, OF2, YQ, YO, YF, YF2, SQW, SOW, SFW, SFW2, SPW, BQ, BO, BF1, BF2, BP, UQ, UO, UF, UF2, UP, ZQ, ZO, ZF, ZF2, ZP, EQ, EO, EF, EF2, EP,
    ss, rs,
):
    d, row, z = lax.axis_index("dp"), lax.axis_index("row"), lax.axis_index("col")
    k = lax.rem(row, 2)
    dq = d

    def at(plane, core, place):
        return (plane, row - k + core, place)

    zk, zs = z // 2, lax.rem(z, 2)
    L, D = A1.shape
    T = XR.shape[1]
    HC = CTX.shape[1]
    FH = M.shape[1]
    QR, OR_, FR, PR_ = wq_in.shape[1], wo_in.shape[0], wf_in.shape[0], wp_in.shape[0]
    DH = wo_in.shape[1]
    own, other = k * 2 * T, (1 - k) * 2 * T

    def mo(v, n):
        return pl.multiple_of(v, n)

    def when(cond, f):
        if cond is True:
            f()
        else:
            pl.when(cond)(f)

    n_send = [0]
    n_recv = [0]
    pending = []

    def new_send():
        n_send[0] += 1
        assert n_send[0] <= ss.shape[0]
        return n_send[0] - 1

    def new_recv(n):
        n_recv[0] += n
        assert n_recv[0] <= rs.shape[0]
        return n_recv[0] - n

    def send(src, dst, rsem, dev, cond=True):
        sem = new_send()

        def make():
            return pltpu.make_async_remote_copy(
                src(),
                dst(),
                ss.at[sem],
                rs.at[rsem() if callable(rsem) else rsem],
                device_id=dev() if callable(dev) else dev,
                device_id_type=MESH,
            )

        when(cond, lambda: make().start())
        pending.append((cond, make))

    def flush(count):
        for cond, make in pending[:count]:
            when(cond, lambda: make().wait_send())
        del pending[:count]

    def local(src, dst, rsem, cond=True):
        when(cond, lambda: pltpu.make_async_copy(src(), dst(), rs.at[rsem]).start())

    def arrive(dst, rsem, cond=True):
        def f():
            pltpu.make_async_remote_copy(
                dst(), dst(), ss.at[0], rs.at[rsem], device_id=at(d, k, z), device_id_type=MESH
            ).wait_recv()

        when(cond, f)

    def arrive_local(dst, rsem, cond=True):
        when(cond, lambda: pltpu.make_async_copy(dst(), dst(), rs.at[rsem]).wait())

    mate = at(d, 1 - k, z)
    quad = [at(d ^ j, k, z) for j in (1, 2, 3)]

    barrier = pltpu.get_barrier_semaphore()
    line = [at(d, k, z ^ j) for j in (1, 2, 3)] + [at(d, 1 - k, z ^ j) for j in (0, 1, 2, 3)]
    quad_mates = [at(d ^ j, 1 - k, z) for j in (1, 2, 3)]
    for dev in quad + quad_mates + line:
        pl.semaphore_signal(barrier, inc=1, device_id=dev, device_id_type=MESH)
    pl.semaphore_wait(barrier, len(quad) + len(quad_mates) + len(line))

    def line_send(src, dst):
        base = new_recv(2)
        for i in range(2):
            mine = (zk == k) & (2 * k + i == z)
            send(lambda i=i: src(i), lambda: dst(zs), base + zs, at(d, zk, 2 * k + i), jnp.logical_not(mine))
            local(lambda i=i: src(i), lambda: dst(zs), base + zs, mine)
        return base

    def line_wait(dst, base, i):
        mine = (zk == k) & (2 * k + i == z)
        arrive(lambda: dst(i), base + i, jnp.logical_not(mine))
        arrive_local(lambda: dst(i), base + i, mine)

    far = lax.rem(k + zk, 2)
    target = z ^ (2 * far)
    is_near, is_far = far == 0, far == 1
    zo = 1 - zs

    class Weight:
        def __init__(self, src, src_quarter, piece, full, slab):
            self.src, self.src_quarter, self.piece, self.full, self.slab = src, src_quarter, piece, full, slab
            self.zsem, self.xsem = new_recv(4), new_recv(8)

        def push(self):
            sem = lambda: self.zsem + zs * 2 + k
            for j in (2, 1):
                send(self.src_quarter, lambda: self.piece(zs, k, dq), sem, lambda j=j: at(d, zk, z ^ j))
            send(self.src, lambda: self.full(zs, k), sem, mate, is_far)
            local(self.src, lambda: self.full(zs, k), self.zsem + zs * 2 + k, is_near)

        def spread(self, cs, cond):
            mine = lambda: self.slab(cs, dq)
            for j in (1, 2):
                send(mine, mine, lambda j=j: self.xsem + cs * 4 + j - 1, quad[j - 1], cond)

        def hop(self):
            for r in range(2):
                arrive(lambda: self.piece(zo, r, dq), self.zsem + zo * 2 + r, is_near)
                arrive(lambda: self.piece(zs, r, dq), self.zsem + zs * 2 + r, is_far)
                mine = lambda r=r: self.piece(zs, r, dq)
                send(mine, mine, lambda r=r: self.zsem + zs * 2 + r, lambda: at(d, k, z ^ 1), is_far)
            self.spread(zo, is_near)
            self.spread(zs, is_far)

        def forward(self):
            for r in range(2):
                arrive(lambda: self.piece(zo, r, dq), self.zsem + zo * 2 + r, is_far)
            self.spread(zo, is_far)

        def relay(self):
            for cs, cond in ((zs, is_far), (zo, True)):
                for j in (1, 2):
                    arrive(lambda: self.slab(cs, dq ^ j), self.xsem + cs * 4 + j - 1, cond)
                    half = lambda cs=cs, j=j: self.piece(cs, j - 1, dq ^ j)
                    send(half, half, lambda cs=cs, j=j: self.xsem + cs * 4 + 1 + j, quad[2 - j], cond)

        def ready(self):
            for r in range(2):
                arrive(lambda: self.full(zs, r), self.zsem + zs * 2 + r, is_near & (k != r))
                arrive_local(lambda: self.full(zs, r), self.zsem + zs * 2 + r, is_near & (k == r))
            for cs, cond in ((zs, is_far), (zo, True)):
                for j in (1, 2):
                    arrive(lambda: self.piece(cs, j - 1, dq ^ 3), self.xsem + cs * 4 + 1 + j, cond)

    q48, o48, f96, p192 = QR // QUAD, OR_ // QUAD, FR // QUAD, PR_ // QUAD

    def cols(r):
        return pl.ds(mo(r * DH, 128), DH)

    w_qkv = Weight(
        lambda: wq_in,
        lambda: wq_in.at[:, pl.ds(mo(dq * q48, 16), q48), :],
        lambda cs, r, q: WQ.at[:, pl.ds(mo(cs * QR + q * q48, 16), q48), cols(r)],
        lambda cs, r: WQ.at[:, pl.ds(mo(cs * QR, 16), QR), cols(r)],
        lambda cs, q: WQ.at[:, pl.ds(mo(cs * QR + q * q48, 16), q48), :],
    )
    w_out = Weight(
        lambda: wo_in,
        lambda: wo_in.at[pl.ds(mo(dq * o48, 16), o48), :],
        lambda cs, r, q: WO.at[pl.ds(mo(cs * OR_ + q * o48, 16), o48), cols(r)],
        lambda cs, r: WO.at[pl.ds(mo(cs * OR_, 16), OR_), cols(r)],
        lambda cs, q: WO.at[pl.ds(mo(cs * OR_ + q * o48, 16), o48), :],
    )
    FC = wf_in.shape[1]

    def fc_part(at0, n):
        return Weight(
            lambda: wf_in.at[:, pl.ds(at0, n)],
            lambda: wf_in.at[pl.ds(mo(dq * f96, 16), f96), pl.ds(at0, n)],
            lambda cs, r, q: WF.at[r, pl.ds(mo(q * f96, 16), f96), pl.ds(mo(cs * FC + at0, 128), n)],
            lambda cs, r: WF.at[r, :, pl.ds(mo(cs * FC + at0, 128), n)],
            lambda cs, q: WF.at[:, pl.ds(mo(q * f96, 16), f96), pl.ds(mo(cs * FC + at0, 128), n)],
        )

    def proj_part(at0, n):
        n4 = n // QUAD
        return Weight(
            lambda: wp_in.at[pl.ds(at0, n), :],
            lambda: wp_in.at[pl.ds(mo(at0 + dq * n4, 16), n4), :],
            lambda cs, r, q: WP.at[pl.ds(mo(cs * PR_ + at0 + q * n4, 16), n4), cols(r)],
            lambda cs, r: WP.at[pl.ds(mo(cs * PR_ + at0, 16), n), cols(r)],
            lambda cs, q: WP.at[pl.ds(mo(cs * PR_ + at0 + q * n4, 16), n4), :],
        )

    first = FC // 3
    w_fc, w_fc2 = fc_part(0, first), fc_part(first, FC - first)
    w_proj, w_proj2 = proj_part(0, first), proj_part(first, FC - first)

    stage = new_recv(2)
    pltpu.make_async_copy(x_in, H, rs.at[stage]).start()
    pltpu.make_async_copy(cot_in, ACC, rs.at[stage + 1]).start()
    bq, bv = bqv_in[0:1, :], bqv_in[1:2, :]
    gap = jnp.zeros_like(bq)
    misc_in[...] = jnp.concatenate(
        [
            bfc_in[...].reshape(1, D),
            jnp.where(zs == 0, jnp.concatenate([bq, gap, bv, gap], axis=1), jnp.concatenate([gap, bq, gap, bv], axis=1)),
            jnp.full((1, D), len_in[0].astype(F32)),
            jnp.full((1, D), len_in[1].astype(F32)),
            jnp.zeros((4, D), F32),
        ],
        axis=0,
    )
    misc_sem = new_recv(8)
    for dev in line:
        send(lambda: misc_in, lambda: MISC.at[k, z], misc_sem + k * 4 + z, dev)
    local(lambda: misc_in, lambda: MISC.at[k, z], misc_sem + k * 4 + z)
    w_qkv.push()
    pltpu.make_async_copy(x_in, H, rs.at[stage]).wait()
    XS[...] = H[...].astype(BF)
    half_rows = T // 2
    xh_sem, x_sem = new_recv(1), new_recv(4)
    part_of = lambda core: pl.ds(mo(core * half_rows, 16), half_rows)
    send(lambda: XS.at[:, part_of(1 - k)], lambda: XH, xh_sem, mate)
    for i in range(2):
        mine = is_near & (zs == i)
        src, dst = lambda i=i: XS.at[i, part_of(k)], lambda: XR.at[zs, part_of(k)]
        send(src, dst, x_sem + zs * 2 + k, at(d, zk, 2 * k + i), jnp.logical_not(mine))
        local(src, dst, x_sem + zs * 2 + k, mine)
    pltpu.make_async_copy(cot_in, ACC, rs.at[stage + 1]).wait()
    CS[...] = ACC[...].astype(BF)

    V8[...] = jnp.zeros_like(V8)
    SQ[...] = jnp.zeros_like(SQ)

    b_out, ln1_g, ln1_b, ln2_g, ln2_b, b_proj = (
        v[...].reshape(1, D) for v in (b_out, ln1_g, ln1_b, ln2_g, ln2_b, b_proj)
    )

    w_qkv.hop()
    arrive(lambda: XH, xh_sem)
    for i in range(2):
        send(lambda i=i: XH.at[i], dst, x_sem + zs * 2 + k, at(d, zk, 2 * (1 - k) + i))
    w_qkv.forward()
    w_qkv.relay()

    RB = 128
    a1_sem = new_recv(2)

    def rows_of(base, i, n):
        return pl.ds(mo(base + i * n, 16), n)

    for s in range(2):
        for core in range(2):
            here = is_near & (zs == s) & (k == core)
            arrive(lambda: XR.at[s, part_of(core)], x_sem + s * 2 + core, jnp.logical_not(here))
            arrive_local(lambda: XR.at[s, part_of(core)], x_sem + s * 2 + core, here)

        def first_norm(i, c):
            scaled, _ = norm_stats(XR[s, rows_of(0, i, RB), :].astype(F32))
            A1[rows_of(own + s * T, i, RB), :] = (scaled * ln1_g + ln1_b).astype(BF)
            return c

        lax.fori_loop(0, T // RB, first_norm, 0)
        mine = lambda s=s: A1.at[pl.ds(mo(own + s * T, 16), T), :]
        send(mine, mine, a1_sem + s, mate)

    for r in range(2):
        for c in range(4):
            here = (k == r) & (z == c)
            arrive(lambda: MISC.at[r, c], misc_sem + r * 4 + c, jnp.logical_not(here))
            arrive_local(lambda: MISC.at[r, c], misc_sem + r * 4 + c, here)
    pair_misc = MISC[0, 2 * k] + MISC[0, 2 * k + 1]
    bias_q, bias_v = pair_misc[1:2, :HC], pair_misc[1:2, HC:]
    length = MISC[zk, 0, pl.ds(2 + zs, 1), :][:, 0:1]

    w_qkv.ready()

    def project(base):
        rows = pl.ds(mo(base, 16), 2 * T)
        a = A1[rows, :]
        QKV[0, rows, :] = ((dot_t(a, WQ[0]) + bias_q).astype(BF).astype(F32) * (HEAD_DIM**-0.5)).astype(BF)
        QKV[1, rows, :] = dot_t(a, WQ[1]).astype(BF)
        QKV[2, rows, :] = (dot_t(a, WQ[2]) + bias_v).astype(BF)

    project(own)
    for s in range(2):
        arrive(lambda: A1.at[pl.ds(mo(other + s * T, 16), T), :], a1_sem + s)
    w_out.push()
    w_fc.push()
    project(other)

    key_place = lax.broadcasted_iota(jnp.int32, (L, 128), 0).astype(F32)
    KB[...] = jnp.where(key_place < length, 0.0, MASKED)

    QB = T
    NQ = L // QB
    low_lane = lax.broadcasted_iota(jnp.int32, (1, 128), 1) < HEAD_DIM
    low_row = lax.broadcasted_iota(jnp.int32, (128, 1), 0) < HEAD_DIM
    diag = lax.broadcasted_iota(jnp.int32, (QB, QB), 0) <= lax.broadcasted_iota(jnp.int32, (QB, QB), 1)

    def keep_lane(v, h):
        return jnp.where(low_lane if h == 0 else jnp.logical_not(low_lane), v, jnp.zeros_like(v))

    def scores_t(kp, qm, qb):
        kv = (qb + 1) * QB
        s = dot_t(kp[:kv], qm)
        kb = KB[0:kv, :]
        s = s + jnp.concatenate([kb] * (QB // 128), axis=1)
        last = jnp.where(diag, s[kv - QB :], MASKED)
        if qb == 0:
            return last
        return jnp.concatenate([s[: kv - QB], last], axis=0)

    def send_cot():
        return line_send(lambda i: CS.at[i], lambda i: GF.at[pl.ds(mo(z * T, 16), T), :])

    between = {
        (0, 3): (w_out.hop, w_fc2.push),
        (1, 0): (w_fc.hop, w_proj.push),
        (1, 2): (w_out.forward,),
        (1, 3): (w_fc.forward, w_fc2.hop, w_proj2.push),
        (2, 0): (w_out.relay, w_proj.hop),
        (2, 2): (w_fc.relay,),
        (2, 3): (w_fc2.forward,),
    }

    def attend(p, c):
        lanes = pl.ds(mo(p * 128, 128), 128)
        kp, vp = QKV[1, :, lanes], QKV[2, :, lanes]
        vt = vp.T
        for qb in range(NQ):
            for (step, at_qb), work in between.items():
                if at_qb == qb:

                    @pl.when(p == step)
                    def _():
                        for do in work:
                            do()

            kv = (qb + 1) * QB
            qp = QKV[0, qb * QB : kv, lanes]
            parts = []
            for h in range(2):
                s = scores_t(kp, keep_lane(qp, h), qb)
                top = jnp.max(s, axis=0, keepdims=True)
                e = jnp.exp(s - top)
                total = jnp.sum(e, axis=0, keepdims=True)
                LSE[pl.ds(2 * p + h, 1), qb * QB : kv] = top + jnp.log(total)
                parts.append(dot(vt[:, :kv], e.astype(BF)) / total)
            CTX[qb * QB : kv, lanes] = jnp.where(low_row, parts[0], parts[1]).T.astype(BF)
        return c

    lax.fori_loop(0, HC // 128, attend, 0)
    w_proj2.hop()
    cot_sem = send_cot()
    sent = len(pending)

    def split_other(n, product):
        base = new_recv(2)
        PS[n] = product(pl.ds(mo(other, 16), 2 * T)).astype(BF).reshape(2, T, D)
        for s in range(2):
            send(lambda s=s: PS.at[n, s], lambda s=s: PR.at[n, s], base + s, mate)
        return base

    def split_own(product):
        ACC[...] = product(pl.ds(mo(own, 16), 2 * T)).reshape(2, T, D)

    def split_sum(n, product):
        base = split_other(n, product)
        split_own(product)
        return base

    def split_wait(n, base, s):
        arrive(lambda: PR.at[n, s], base + s)

    w_out.ready()
    ex = split_sum(0, lambda rows: dot(CTX[rows, :], WO[...]))
    w_proj.forward()
    a2_sem = new_recv(2)
    for s in range(2):
        split_wait(0, ex, s)

        def second_norm(i, c):
            rows = rows_of(0, i, RB)
            h = XR[s, rows, :].astype(F32) + ACC[s, rows, :] + PR[0, s, rows, :].astype(F32) + b_out
            H[s, rows, :] = h
            scaled, _ = norm_stats(h)
            A2[rows_of(own + s * T, i, RB), :] = (scaled * ln2_g + ln2_b).astype(BF)
            return c

        lax.fori_loop(0, T // RB, second_norm, 0)
        mine = lambda s=s: A2.at[pl.ds(mo(own + s * T, 16), T), :]
        send(mine, mine, a2_sem + s, mate)

    VF[...] = jnp.concatenate([MISC[0, 2 * k, 0:1, :], MISC[0, 2 * k + 1, 0:1, :]], axis=1)

    def hidden(base, start, width):
        rows = pl.ds(mo(base, 16), 2 * T)

        def body(i, c):
            cs = pl.ds(mo(i * FC + start, 128), width)
            u = dot(A2[rows, :], WF[:, :, cs].reshape(D, width)) + VF[:, cs]
            t = jnp.tanh(GELU_C * (u + GELU_A * u * u * u))
            M[rows, cs] = (0.5 * u * (1.0 + t)).astype(BF)
            SL[rows, cs] = (
                0.5 * (1.0 + t) + 0.5 * u * (1.0 - t * t) * GELU_C * (1.0 + 3.0 * GELU_A * u * u)
            ).astype(BF)
            return c

        lax.fori_loop(0, 2, body, 0)

    w_fc.ready()
    hidden(own, 0, first)
    w_fc2.relay()
    for s in range(2):
        arrive(lambda: A2.at[pl.ds(mo(other + s * T, 16), T), :], a2_sem + s)
    hidden(other, 0, first)
    w_proj2.forward()
    w_proj.relay()
    w_fc2.ready()
    hidden(own, first, FC - first)
    w_proj2.relay()
    hidden(other, first, FC - first)
    gf_sem = new_recv(2)
    for s in range(2):
        line_wait(lambda i: GF.at[pl.ds(mo(own + i * T, 16), T), :], cot_sem, s)

        def mask_rows(i, c):
            rows = rows_of(own + s * T, i, RB)
            place = (lax.broadcasted_iota(jnp.int32, (RB, 1), 0) + (own + s * T + i * RB)).astype(F32)
            g = jnp.where(place < length, GF[rows, :].astype(F32), 0.0)
            GF[rows, :] = g.astype(BF)
            V8[V_BPROJ] += fold8(g)
            return c

        lax.fori_loop(0, T // RB, mask_rows, 0)
        mine = lambda s=s: GF.at[pl.ds(mo(own + s * T, 16), T), :]
        send(mine, mine, gf_sem + s, mate)

    w_proj.ready()
    w_proj2.ready()
    mlp_rows = lambda rows: dot(M[rows, :], WP[...])
    mlp_ex = split_other(1, mlp_rows)
    for s in range(2):
        arrive(lambda: GF.at[pl.ds(mo(other + s * T, 16), T), :], gf_sem + s)

    bit = (lax.rem(dq, 2), dq // 2)

    def wide_factors(count, width):
        return [jnp.concatenate([FAC[dq ^ j, 0:1, :]] * (width // 128), axis=1) for j in range(count)]

    class Part:
        def __init__(self, plane, S, B, U, Z, E, slab, piece, place):
            self.S, self.B, self.U, self.Z, self.E = S, B, U, Z, E
            self.slab, self.piece, self.place = slab, piece, place
            self.pair, self.zsem, self.end = new_recv(1), new_recv(2), new_recv(4)
            self.setup(*plane)

        def pass_on(self):
            send(lambda: self.slab(1 - zs), lambda: self.B, self.pair, at(d, k, z ^ 1))

        def middle(self):
            arrive(lambda: self.B, self.pair)
            self.U[...] = (self.slab(zs)[...].astype(F32) + self.B[...].astype(F32)).astype(BF)
            for r in range(2):
                mine = (far == 0) & (r == k)
                piece = lambda r=r: self.piece(r)
                send(piece, lambda: self.Z.at[far], self.zsem + far, at(d, r, target), jnp.logical_not(mine))
                local(piece, lambda: self.Z.at[far], self.zsem + far, mine)

        def finish(self):
            arrive(lambda: self.Z.at[0], self.zsem, is_far)
            arrive_local(lambda: self.Z.at[0], self.zsem, is_near)
            arrive(lambda: self.Z.at[1], self.zsem + 1)
            self.E[...] = (self.Z[0].astype(F32) + self.Z[1].astype(F32)).astype(BF)
            for j in (1, 2, 3):
                send(lambda: self.E, lambda: self.place(dq), self.end + j, quad[j - 1])
            local(lambda: self.E, lambda: self.place(dq), self.end)

        def done(self):
            arrive_local(lambda: self.place(dq), self.end)
            for j in (1, 2, 3):
                arrive(lambda: self.place(dq ^ j), self.end + j)

    class DirectPart(Part):
        def setup(self, G, R):
            self.G, self.R, self.raw = G, R, new_recv(6)

        def quarter(self, q):
            return self.G.at[:, q // 2, lax.rem(q, 2)]

        def spread(self, a):
            for j in (1, 2, 3):
                send(
                    lambda j=j: self.G.at[a, (dq ^ j) // 2, lax.rem(dq ^ j, 2)],
                    lambda j=j: self.R.at[j - 1, a],
                    self.raw + 2 * j - 2 + a,
                    quad[j - 1],
                )

        def reduce(self):
            for j in (1, 2, 3):
                for a in range(2):
                    arrive(lambda: self.R.at[j - 1, a], self.raw + 2 * j - 2 + a)
            G, (_, n, width) = self.quarter(dq), self.S.shape
            factors, steps = wide_factors(QUAD, width), n // 16

            def add(i, c):
                a, rows = i // steps, pl.ds(mo(lax.rem(i, steps) * 16, 16), 16)
                v = G[a, rows, :].astype(F32) * factors[0]
                for j in (1, 2, 3):
                    v = v + self.R[j - 1, a, rows, :].astype(F32) * factors[j]
                self.S[a, rows, :] = v.astype(BF)
                return c

            lax.fori_loop(0, 2 * steps, add, 0)
            self.pass_on()

    class CrossPart(Part):
        def setup(self, G, X, O, Y):
            self.G, self.X, self.O, self.Y = G, X, O, Y
            self.raw, self.cross = new_recv(2), new_recv(2)

        def spread(self, cond=True):
            send(lambda: self.G.at[0, :, 1 - bit[0]], lambda: self.X.at[0], self.raw, quad[0], cond)
            send(lambda: self.G.at[1, 1 - bit[1]], lambda: self.X.at[1], self.raw + 1, quad[1], cond)

        def scale(self):
            _, n, width = self.S.shape
            factors = wide_factors(3, width)
            for a in range(2):
                arrive(lambda: self.X.at[a], self.raw + a)

                def add(i, c, a=a):
                    rows = pl.ds(mo(i * 16, 16), 16)
                    for b, to in ((bit[1 - a], self.S), (1 - bit[1 - a], self.O)):
                        mine = self.G[0, b, bit[0], rows, :] if a == 0 else self.G[1, bit[1], b, rows, :]
                        v = mine.astype(F32) * factors[0] + self.X[a, b, rows, :].astype(F32) * factors[1 + a]
                        to[a, rows, :] = v.astype(BF)
                    return c

                lax.fori_loop(0, n // 16, add, 0)
                send(lambda a=a: self.O.at[a], lambda a=a: self.Y.at[a], self.cross + a, quad[1 - a])

        def reduce(self):
            for a in range(2):
                arrive(lambda: self.Y.at[a], self.cross + a)
            self.S[...] = (self.S[...].astype(F32) + self.Y[...].astype(F32)).astype(BF)
            self.pass_on()

    g_proj = DirectPart(
        (GWP, RP), SPW, BP, UP, ZP, EP,
        lambda cs: SPW.at[cs],
        lambda r: UP.at[:, cols(r)],
        lambda q: gp_out.at[pl.ds(mo(q * p192, 16), p192), :],
    )
    g_out = CrossPart(
        (GWO, XO, OO, YO), SOW, BO, UO, ZO, EO,
        lambda cs: SOW.at[cs],
        lambda r: UO.at[:, cols(r)],
        lambda q: go_out.at[pl.ds(mo(q * o48, 16), o48), :],
    )

    def fc_grad(plane, S, B, U, Z, E, start, n):
        return CrossPart(
            plane, S, B, U, Z, E,
            lambda cs: S.at[:, :, pl.ds(mo(cs * FC, 128), FC)],
            lambda r: U.at[r],
            lambda q: gf_out.at[pl.ds(mo(start + q * n, 16), n), :],
        )

    g_fc2 = fc_grad((GWF, XF, OF, YF), SFW, BF1, UF, ZF, EF, 0, 128 // QUAD)
    g_fc = fc_grad((GWF2, XF2, OF2, YF2), SFW2, BF2, UF2, ZF2, EF2, 128, (FR - 128) // QUAD)

    def qkv_grad(i):
        return CrossPart(
            [v.at[i] for v in (GWQ, XQ, OQ, YQ)],
            *(v.at[i] for v in (SQW, BQ, UQ, ZQ, EQ)),
            lambda cs: SQW.at[i, cs],
            lambda r: UQ.at[i, :, cols(r)],
            lambda q: gq_out.at[i, pl.ds(mo(q * q48, 16), q48), :],
        )

    g_qkv = [qkv_grad(i) for i in range(3)]

    def grad_proj(i, c):
        cs = pl.ds(mo(i * (FC // 2), 128), FC // 2)
        g = t_dot(M[:, cs], GF[...])
        SQ[...] += fold8(g * g)
        GWP[i // 2, lax.rem(i, 2)] = g.astype(BF).reshape(2, p192, D)
        return c

    for a in range(2):
        lax.fori_loop(2 * a, 2 * a + 2, grad_proj, 0)
        g_proj.spread(a)

    NB = 512
    NN = FH // NB

    def grad_hidden(i, c):
        rows = pl.ds(mo(i // NN * 2 * T, 16), 2 * T)
        cs = pl.ds(mo(lax.rem(i, NN) * NB, 128), NB)
        g = dot_t(GF[rows, :], WP[cs, :]) * SL[rows, cs].astype(F32)
        low = g.astype(BF)
        SL[rows, cs] = low
        VF[:, cs] = jnp.where(i < NN, 0.0, VF[:, cs]) + jnp.sum(low.astype(F32), axis=0, keepdims=True)
        return c

    lax.fori_loop(0, 2 * NN, grad_hidden, 0)
    ex = split_sum(2, lambda rows: dot_t(SL[rows, :], WF[...].reshape(D, FH)))

    ga_sem = new_recv(2)
    for s in range(2):
        split_wait(2, ex, s)

        def second_back(i, c):
            rows = rows_of(0, i, RB)
            full = rows_of(own + s * T, i, RB)
            up = ACC[s, rows, :] + PR[2, s, rows, :].astype(F32)
            scaled, inverse = norm_stats(H[s, rows, :])
            through = up * ln2_g
            V8[V_LN2G] += fold8(up * scaled)
            V8[V_LN2B] += fold8(up)
            g = GF[full, :].astype(F32) + inverse * (
                through
                - jnp.mean(through, axis=-1, keepdims=True)
                - scaled * jnp.mean(through * scaled, axis=-1, keepdims=True)
            )
            V8[V_BOUT] += fold8(g)
            HG[s, rows, :] = g
            GA[full, :] = g.astype(BF)
            return c

        lax.fori_loop(0, T // RB, second_back, 0)
        mine = lambda s=s: GA.at[pl.ds(mo(own + s * T, 16), T), :]
        send(mine, mine, ga_sem + s, mate)
    split_own(mlp_rows)
    flush(sent)
    LO, GI = CS, XS
    for s in range(2):
        split_wait(1, mlp_ex, s)

        def output_rows(i, c):
            rows = rows_of(0, i, RB)
            LO[s, rows, :] = (H[s, rows, :] + ACC[s, rows, :] + PR[1, s, rows, :].astype(F32) + b_proj).astype(BF)
            return c

        lax.fori_loop(0, T // RB, output_rows, 0)
    lo_sem = line_send(lambda i: LO.at[i], lambda i: lo_out.at[i])

    for s in range(2):
        arrive(lambda: GA.at[pl.ds(mo(other + s * T, 16), T), :], ga_sem + s)

    GCTX[...] = dot_t(GA[...], WO[...]).astype(BF)
    g = t_dot(CTX[...], GA[...])
    SQ[...] += fold8(g * g)
    GWO[...] = g.astype(BF).reshape(2, 2, 2, o48, D)
    g_out.spread()

    def grad_fc(G, start, n):
        g = t_dot(jnp.concatenate([A2[:, start : start + n], A2[:, FR + start : FR + start + n]], axis=1), SL[...])
        q = fold8(g * g)
        SQ[...] += q[:, :D] + q[:, D:]
        G[...] = g.astype(BF).reshape(2, 2, 2, n // QUAD, FH)

    grad_fc(GWF2, 128, FR - 128)
    g_fc.spread()

    def attend_back(p):
        lanes = pl.ds(mo(p * 128, 128), 128)
        kp, vp = QKV[1, :, lanes], QKV[2, :, lanes]
        kt = kp.T
        DK[...] = jnp.zeros_like(DK)
        DV[...] = jnp.zeros_like(DV)
        for qb in range(NQ):
            kv = (qb + 1) * QB
            qp = QKV[0, qb * QB : kv, lanes]
            do = GCTX[qb * QB : kv, lanes]
            dqt = []
            for h in range(2):
                qm, dm = keep_lane(qp, h), keep_lane(do, h)
                pt = jnp.exp(scores_t(kp, qm, qb) - LSE[pl.ds(2 * p + h, 1), qb * QB : kv])
                gp = dot_t(vp[:kv], dm)
                both = pt * gp
                gs = (both - pt * jnp.sum(both, axis=0, keepdims=True)).astype(BF)
                DV[0:kv, :] += dot(pt.astype(BF), dm)
                DK[0:kv, :] += dot(gs, qm)
                dqt.append(dot(kt[:, :kv], gs))
            GQKV[0, qb * QB : kv, lanes] = (
                jnp.where(low_row, dqt[0], dqt[1]).T * (HEAD_DIM**-0.5)
            ).astype(BF)
        GQKV[1, :, lanes] = DK[...].astype(BF)
        GQKV[2, :, lanes] = DV[...].astype(BF)

    def attend_back_step(p, c):
        attend_back(p)
        return c

    lax.fori_loop(0, HC // 128, attend_back_step, 0)

    def grad_norm_in(rows):
        return dot(GQKV[0, rows, :], WQ[0]) + dot(GQKV[1, rows, :], WQ[1]) + dot(GQKV[2, rows, :], WQ[2])

    ex = split_sum(3, grad_norm_in)
    grad_fc(GWF, 0, 128)
    g_fc2.spread(k == 0)
    for s in range(2):
        split_wait(3, ex, s)

        def first_back(i, c):
            rows = rows_of(0, i, RB)
            up = ACC[s, rows, :] + PR[3, s, rows, :].astype(F32)
            scaled, inverse = norm_stats(XR[s, rows, :].astype(F32))
            through = up * ln1_g
            V8[V_LN1G] += fold8(up * scaled)
            V8[V_LN1B] += fold8(up)
            g = HG[s, rows, :] + inverse * (
                through
                - jnp.mean(through, axis=-1, keepdims=True)
                - scaled * jnp.mean(through * scaled, axis=-1, keepdims=True)
            )
            GI[s, rows, :] = g.astype(BF)
            return c

        lax.fori_loop(0, T // RB, first_back, 0)

    batches = [pl.ds(0, T // 2), pl.ds(T // 2, T // 4), pl.ds(3 * T // 4, T // 4)]
    send_gi = lambda b: line_send(lambda i: GI.at[i, batches[b]], lambda i: gi_out.at[i, batches[b]])
    gi_sems = [send_gi(0)]

    def grad_qkv(i, c):
        g = t_dot(GQKV[i], A1[...])
        SQ[...] += fold8(g * g)
        GWQ[i] = g.astype(BF).reshape(2, 2, 2, q48, D)
        return c

    lax.fori_loop(0, 3, grad_qkv, 0)
    VK[k] = jnp.zeros(VK.shape[1:], F32)
    for i in range(6):
        VK[k, i : i + 1, :] = jnp.sum(V8[i], axis=0, keepdims=True)
    VK[k, V_BQV : V_BQV + 1, :] = jnp.concatenate(
        [jnp.sum(GQKV[i].astype(F32), axis=0, keepdims=True) for i in (0, 2)], axis=1
    )
    VK[k, V_BFC : V_BFC + 1, :] = VF[:, :D]
    VK[k, V_BFC + 1 : V_BFC + 2, :] = VF[:, D:]
    VK[k, V_SQ : V_SQ + 1, :] = jnp.sum(SQ[...], axis=0, keepdims=True)
    vk_sem = new_recv(1)
    send(lambda: VK.at[k], lambda: VK.at[k], vk_sem, mate)
    arrive(lambda: VK.at[1 - k], vk_sem)
    va, vb = VK[0], VK[1]
    pack = jnp.concatenate([va[0:6] + vb[0:6], va[6:9], vb[6:9]], axis=0)
    squares = jnp.sum(jnp.sum(pack * pack, axis=0, keepdims=True) + va[9:10] + vb[9:10], axis=1, keepdims=True)
    norm = jnp.sqrt(squares)
    factor = CLIP_BOUND / jnp.maximum(norm, CLIP_BOUND)
    FAC[dq] = jnp.broadcast_to(factor, (8, 128))
    fac_sem, vp_sem = new_recv(3), new_recv(3)
    for j in (1, 2, 3):
        for dev in (quad[j - 1], quad_mates[j - 1]):
            send(lambda: FAC.at[dq], lambda: FAC.at[dq], fac_sem + j - 1, dev, k == 1)
    VP[dq] = jnp.concatenate([pack, jnp.zeros((4, D), F32)], axis=0)
    for j in (1, 2, 3):
        arrive(lambda: FAC.at[dq ^ j], fac_sem + j - 1)

    order = [g_proj, g_out, g_fc, g_fc2, *g_qkv]
    g_proj.reduce()
    g_out.scale()
    g_fc.scale()
    g_fc2.spread(k == 1)
    for part in g_qkv:
        part.spread()
    for j in (1, 2, 3):
        send(lambda: VP.at[dq], lambda: VP.at[dq], vp_sem + j - 1, quad[j - 1])
    g_out.reduce()
    g_fc.reduce()
    g_proj.middle()
    g_out.middle()
    g_fc.middle()
    gi_sems.append(send_gi(1))
    for part in (g_fc2, *g_qkv):
        part.scale()
    g_proj.finish()
    g_fc2.reduce()
    for j in (1, 2, 3):
        arrive(lambda: VP.at[dq ^ j], vp_sem + j - 1)
    total = jnp.zeros((12, D), F32)
    for q in range(QUAD):
        total = total + VP[q, 0:12, :] * FAC[q, 0:1, 0:1]
    VZ[z] = jnp.concatenate([total, jnp.broadcast_to(norm, (4, D))], axis=0)
    vz_sem = new_recv(3)
    for j in (1, 2, 3):
        send(lambda: VZ.at[z], lambda: VZ.at[z], vz_sem + j - 1, at(d, k, z ^ j))
    for part in g_qkv:
        part.reduce()
    g_out.finish()
    g_fc.finish()
    g_fc2.middle()
    for part in g_qkv:
        part.middle()
    gi_sems.append(send_gi(2))
    g_fc2.finish()
    for part in g_qkv:
        part.finish()

    for j in (1, 2, 3):
        arrive(lambda: VZ.at[z ^ j], vz_sem + j - 1)
    total = VZ[0] + VZ[1] + VZ[2] + VZ[3]
    vec_out[0:6, :] = total[0:6]
    V8[0, 0:6, :] = total[6:12]
    vec_out[6:7, :] = V8[0, pl.ds(V_BFC - V_BQV + 3 * zk + zs, 1), :]
    pair = V8[0, pl.ds(3 * zk, 1), :]
    spare = jnp.zeros((1, D - QR), F32)
    for i in range(2):
        a, b = pair[:, i * HC : i * HC + QR], pair[:, i * HC + QR : (i + 1) * HC]
        vec_out[7 + i : 8 + i, :] = jnp.concatenate([jnp.where(zs == 0, a, b), spare], axis=1)
    first_place = lax.broadcasted_iota(jnp.int32, (1, D), 1) == 0
    vec_out[9:10, :] = jnp.where(
        first_place, VZ[2 * k, V_NORM : V_NORM + 1, :], VZ[2 * k + 1, V_NORM : V_NORM + 1, :]
    )
    vec_out[10:12, :] = jnp.zeros((2, D), F32)

    for part in order:
        part.done()
    for i in range(2):
        line_wait(lambda i: lo_out.at[i], lo_sem, i)
        for b in range(3):
            line_wait(lambda i: gi_out.at[i, batches[b]], gi_sems[b], i)
    flush(len(pending))


def widen(*refs):
    low, vec_in, wide, lines, b_qv, norms = refs[:6], refs[6], refs[7:13], refs[13:20], refs[20], refs[21]
    before, after, vec, rows, sems, line_sems = refs[22:28], refs[28:34], refs[34], refs[35:42], refs[42], refs[43]
    parts = []
    for i, v in enumerate(low):
        parts += [(i, (e,)) for e in range(2)] if i < 2 else [(i, (...,))]

    def load(n, i, at):
        return pltpu.make_async_copy(low[i].at[at], before[i].at[at], sems.at[2 * n])

    def store(n, i, at):
        return pltpu.make_async_copy(after[i].at[at], wide[i].at[at], sems.at[2 * n + 1])

    def store_line(i):
        return pltpu.make_async_copy(rows[i], lines[i], line_sems.at[i])

    load_vec = pltpu.make_async_copy(vec_in, vec, line_sems.at[7])
    for n, (i, at) in enumerate(parts):
        load(n, i, at).start()
    load_vec.start()
    for n, (i, at) in enumerate(parts):
        load(n, i, at).wait()
        after[i][at] = before[i][at].astype(F32)
        store(n, i, at).start()
    load_vec.wait()
    for i in range(7):
        rows[i][...] = vec[i, :]
        store_line(i).start()
    b_qv[...] = vec[7:9, : b_qv.shape[1]]
    norms[...] = vec[9, :2]
    for n, (i, at) in enumerate(parts):
        store(n, i, at).wait()
    for i in range(7):
        store_line(i).wait()


def shards(
    layer_in, w_qkv, b_qv, w_out, b_out, ln1_g, ln1_b, ln2_g, ln2_b, w_fc, b_fc, w_proj, b_proj, lengths, cotangent
):
    E, T, D = layer_in.shape
    n_col, n_row = lax.axis_size("col"), lax.axis_size("row")
    assert lax.axis_size("dp") == QUAD and n_col == 4 and n_row % 2 == 0
    pairs = n_row // 2
    r = lax.axis_index("row")
    core = lax.rem(r, 2)
    half_rows = w_fc.shape[0] * pairs

    def halves(w, axis):
        if pairs == 1:
            return w
        whole = lax.all_gather(w, "row", axis=axis, tiled=True)
        return lax.dynamic_slice_in_dim(whole, core * half_rows, half_rows, axis)

    w_qkv, w_out, w_fc, w_proj = halves(w_qkv, 0), halves(w_out, 1), halves(w_fc, 0), halves(w_proj, 1)
    L = T * n_col
    HQ = w_qkv.shape[2]
    HC = HQ * n_col // 2
    FQ = w_fc.shape[1]
    FH = FQ * n_col // 2
    DH = w_fc.shape[0]
    wq_t = jnp.transpose(w_qkv, (1, 2, 0))
    q48, o48, p192 = HQ // QUAD, HQ // QUAD, FQ // QUAD
    fa, fb = 128 // QUAD, (DH - 128) // QUAD

    anyspec = pl.BlockSpec(memory_space=pl.ANY)
    vm = pl.BlockSpec(memory_space=pltpu.VMEM)
    V = pltpu.VMEM
    outs = pl.pallas_call(
        kernel,
        name="layer",
        out_shape=(
            jax.ShapeDtypeStruct((E, T, D), BF),
            jax.ShapeDtypeStruct((E, T, D), BF),
            jax.ShapeDtypeStruct((3, HQ, DH), BF),
            jax.ShapeDtypeStruct((HQ, DH), BF),
            jax.ShapeDtypeStruct((DH, FQ), BF),
            jax.ShapeDtypeStruct((FQ, DH), BF),
            jax.ShapeDtypeStruct((12, D), F32),
        ),
        in_specs=[anyspec] * 6 + [vm, vm, pl.BlockSpec(memory_space=pltpu.SMEM)] + [vm] * 6,
        out_specs=(anyspec,) * 6 + (vm,),
        scratch_shapes=[
            V((2, T, D), BF),
            V((2, T // 2, D), BF),
            V((2, T, D), BF),
            V((8, D), F32),
            V((2, T, D), BF),
            V((2, T, D), F32),
            V((2, T, D), F32),
            V((L, D), BF),
            V((3, HC, D), BF),
            V((HC, D), BF),
            V((2, DH, FH), BF),
            V((FH, D), BF),
            V((2, n_col, 8, D), F32),
            V((3, L, HC), BF),
            V((L, HC), BF),
            V((8, L), F32),
            V((L, 128), F32),
            V((2, T, D), F32),
            V((4, 2, T, D), BF),
            V((4, 2, T, D), BF),
            V((L, D), BF),
            V((L, FH), BF),
            V((L, FH), BF),
            V((L, D), BF),
            V((L, D), BF),
            V((L, HC), BF),
            V((3, L, HC), BF),
            V((L, 128), F32),
            V((L, 128), F32),
            V((6, 8, D), F32),
            V((8, D), F32),
            V((1, FH), F32),
            V((2, 16, D), F32),
            V((QUAD, 8, 128), F32),
            V((QUAD, 16, D), F32),
            V((n_col, 16, D), F32),
            V((3, 2, 2, 2, q48, D), BF),
            V((2, 2, 2, o48, D), BF),
            V((2, 2, 2, fa, FH), BF),
            V((2, 2, 2, fb, FH), BF),
            V((2, 2, 2, p192, D), BF),
            V((3, 2, p192, D), BF),
            *[
                V(shape, BF)
                for shape in ((3, 2, 2, q48, D), (2, 2, o48, D), (2, 2, fa, FH), (2, 2, fb, FH))
            ],
            *[
                V(shape, BF)
                for _ in "OY"
                for shape in ((3, 2, q48, D), (2, o48, D), (2, fa, FH), (2, fb, FH))
            ],
            V((3, 2, q48, D), BF),
            V((2, o48, D), BF),
            V((2, fa, FH), BF),
            V((2, fb, FH), BF),
            V((2, p192, D), BF),
            *[
                V(shape, BF)
                for _ in "BU"
                for shape in ((3, q48, D), (o48, D), (2, fa, FQ), (2, fb, FQ), (p192, D))
            ],
            V((3, 2, q48, DH), BF),
            V((2, o48, DH), BF),
            V((2, fa, FQ), BF),
            V((2, fb, FQ), BF),
            V((2, p192, DH), BF),
            V((3, q48, DH), BF),
            V((o48, DH), BF),
            V((fa, FQ), BF),
            V((fb, FQ), BF),
            V((p192, DH), BF),
            pltpu.SemaphoreType.DMA((264,)),
            pltpu.SemaphoreType.DMA((264,)),
        ],
        compiler_params=pltpu.CompilerParams(
            collective_id=0, has_side_effects=True, vmem_limit_bytes=63 * 2**20
        ),
    )(
        layer_in, cotangent, wq_t, w_out, w_fc, w_proj, b_fc, b_qv, lengths,
        b_out, ln1_g, ln1_b, ln2_g, ln2_b, b_proj,
    )
    low, vec = outs[:6], outs[6]
    line = jax.ShapeDtypeStruct((D,), F32)
    outs = pl.pallas_call(
        widen,
        name="widen",
        out_shape=(
            *(jax.ShapeDtypeStruct(v.shape, F32) for v in low),
            *(line,) * 7,
            jax.ShapeDtypeStruct((2, HQ), F32),
            jax.ShapeDtypeStruct((2,), F32),
        ),
        in_specs=[anyspec] * 7,
        out_specs=(anyspec,) * 13 + (vm,) * 2,
        scratch_shapes=[
            *(V(v.shape, BF) for v in low),
            *(V(v.shape, F32) for v in (*low, vec)),
            *[V((D,), F32)] * 7,
            pltpu.SemaphoreType.DMA((16,)),
            pltpu.SemaphoreType.DMA((8,)),
        ],
        compiler_params=pltpu.CompilerParams(vmem_limit_bytes=63 * 2**20),
    )(*low, vec)
    lo, gi, gq, go, gf, gp = outs[:6]
    vec, norms = outs[6:14], outs[14]
    gq = jnp.transpose(gq, (2, 0, 1))
    if pairs > 1:
        groups = [[2 * p + q for p in range(pairs)] for q in range(2)]
        cores = [[2 * p, 2 * p + 1] for p in range(pairs)]
        gq, go, gf, gp, *vec = (
            lax.psum(v, "row", axis_index_groups=groups) for v in (gq, go, gf, gp, *vec)
        )

        def share(v, axis):
            whole = lax.all_gather(v, "row", axis=axis, tiled=True, axis_index_groups=cores)
            part = whole.shape[axis] // n_row
            return lax.dynamic_slice_in_dim(whole, r * part, part, axis)

        gq, go, gf, gp = share(gq, 0), share(go, 1), share(gf, 0), share(gp, 1)
    gb_out, g1, b1, g2, b2, gb_proj, gb_fc, gb_qv = vec
    return (lo, gi, norms, gq, gb_qv, go, gb_out, g1, b1, g2, b2, gf, gb_fc, gp, gb_proj)


def solution(mesh):
    in_specs = (
        P(("dp", "row"), "col", None),
        P("row", None, "col"),
        P(None, "col"),
        P("col", "row"),
        P(),
        P(),
        P(),
        P(),
        P(),
        P("row", "col"),
        P("col"),
        P("col", "row"),
        P(),
        P(("dp", "row")),
        P(("dp", "row"), "col", None),
    )
    out_specs = (
        P(("dp", "row"), "col", None),
        P(("dp", "row"), "col", None),
        P(("dp", "row")),
        P("row", None, "col"),
        P(None, "col"),
        P("col", "row"),
        P(),
        P(),
        P(),
        P(),
        P(),
        P("row", "col"),
        P("col"),
        P("col", "row"),
        P(),
    )
    return jax.shard_map(shards, mesh=mesh, in_specs=in_specs, out_specs=out_specs, check_vma=False)
```

```python
import functools

import jax
import jax.numpy as jnp
from jax import lax
from jax.experimental import pallas as pl
from jax.experimental.pallas import tpu as pltpu
from jax.sharding import PartitionSpec as P

MESH = pl.DeviceIdType.MESH
EPSILON = 1e-05
CLIP_BOUND = 1.0
GELU_C = 0.7978845608028654
GELU_A = 0.044715
MASKED = -1e30
HEAD_DIM = 64
QUAD = 4
BF = jnp.bfloat16
F32 = jnp.float32

V_BOUT, V_LN1G, V_LN1B, V_LN2G, V_LN2B, V_BPROJ, V_BQV, V_BFC, V_SQ = 0, 1, 2, 3, 4, 5, 6, 7, 9
V_NORM = 12


def dot(a, b):
    return lax.dot_general(a, b, (((1,), (0,)), ((), ())), preferred_element_type=F32)


def dot_t(a, b):
    return lax.dot_general(a, b, (((1,), (1,)), ((), ())), preferred_element_type=F32)


def t_dot(a, b):
    return lax.dot_general(a, b, (((0,), (0,)), ((), ())), preferred_element_type=F32)


def fold8(v):
    return jnp.sum(v.reshape(v.shape[0] // 8, 8, v.shape[1]), axis=0)


def norm_stats(v):
    center = v - jnp.mean(v, axis=-1, keepdims=True)
    inverse = lax.rsqrt(jnp.mean(center * center, axis=-1, keepdims=True) + EPSILON)
    return center * inverse, inverse


def kernel(
    x_in, cot_in, wq_in, wo_in, wf_in, wp_in, bfc_in, bqv_in, len_in, b_out, ln1_g, ln1_b, ln2_g, ln2_b, b_proj,
    lo_out, gi_out, gq_out, go_out, gf_out, gp_out, vec_out,
    XS, XH, CS, misc_in, XR, H, HG, A1, WQ, WO, WF, WP, MISC, QKV, CTX, LSE, KB, ACC,
    PS, PR, A2, M, SL, GF, GA, GCTX, GQKV, DK, DV,
    V8, SQ, VF, VK, FAC, VP, VZ,
    GWQ, GWO, GWF, GWF2, GWP, RP, XQ, XO, XF, XF2, OQ, OO, OF, OF2, YQ, YO, YF, YF2, SQW, SOW, SFW, SFW2, SPW, BQ, BO, BF1, BF2, BP, UQ, UO, UF, UF2, UP, ZQ, ZO, ZF, ZF2, ZP, EQ, EO, EF, EF2, EP,
    ss, rs,
):
    d, row, z = lax.axis_index("dp"), lax.axis_index("row"), lax.axis_index("col")
    k = lax.rem(row, 2)
    dq = d

    def at(plane, core, place):
        return (plane, row - k + core, place)

    zk, zs = z // 2, lax.rem(z, 2)
    L, D = A1.shape
    T = XR.shape[1]
    HC = CTX.shape[1]
    FH = M.shape[1]
    QR, OR_, FR, PR_ = wq_in.shape[1], wo_in.shape[0], wf_in.shape[0], wp_in.shape[0]
    DH = wo_in.shape[1]
    own, other = k * 2 * T, (1 - k) * 2 * T

    def mo(v, n):
        return pl.multiple_of(v, n)

    def when(cond, f):
        if cond is True:
            f()
        else:
            pl.when(cond)(f)

    n_send = [0]
    n_recv = [0]
    pending = []

    def new_send():
        n_send[0] += 1
        assert n_send[0] <= ss.shape[0]
        return n_send[0] - 1

    def new_recv(n):
        n_recv[0] += n
        assert n_recv[0] <= rs.shape[0]
        return n_recv[0] - n

    def send(src, dst, rsem, dev, cond=True):
        sem = new_send()

        def make():
            return pltpu.make_async_remote_copy(
                src(),
                dst(),
                ss.at[sem],
                rs.at[rsem() if callable(rsem) else rsem],
                device_id=dev() if callable(dev) else dev,
                device_id_type=MESH,
            )

        when(cond, lambda: make().start())
        pending.append((cond, make))

    def flush(count):
        for cond, make in pending[:count]:
            when(cond, lambda: make().wait_send())
        del pending[:count]

    def local(src, dst, rsem, cond=True):
        when(cond, lambda: pltpu.make_async_copy(src(), dst(), rs.at[rsem]).start())

    def arrive(dst, rsem, cond=True):
        def f():
            pltpu.make_async_remote_copy(
                dst(), dst(), ss.at[0], rs.at[rsem], device_id=at(d, k, z), device_id_type=MESH
            ).wait_recv()

        when(cond, f)

    def arrive_local(dst, rsem, cond=True):
        when(cond, lambda: pltpu.make_async_copy(dst(), dst(), rs.at[rsem]).wait())

    mate = at(d, 1 - k, z)
    quad = [at(d ^ j, k, z) for j in (1, 2, 3)]

    barrier = pltpu.get_barrier_semaphore()
    line = [at(d, k, z ^ j) for j in (1, 2, 3)] + [at(d, 1 - k, z ^ j) for j in (0, 1, 2, 3)]
    quad_mates = [at(d ^ j, 1 - k, z) for j in (1, 2, 3)]
    for dev in quad + quad_mates + line:
        pl.semaphore_signal(barrier, inc=1, device_id=dev, device_id_type=MESH)
    pl.semaphore_wait(barrier, len(quad) + len(quad_mates) + len(line))

    def line_send(src, dst):
        base = new_recv(2)
        for i in range(2):
            mine = (zk == k) & (2 * k + i == z)
            send(lambda i=i: src(i), lambda: dst(zs), base + zs, at(d, zk, 2 * k + i), jnp.logical_not(mine))
            local(lambda i=i: src(i), lambda: dst(zs), base + zs, mine)
        return base

    def line_wait(dst, base, i):
        mine = (zk == k) & (2 * k + i == z)
        arrive(lambda: dst(i), base + i, jnp.logical_not(mine))
        arrive_local(lambda: dst(i), base + i, mine)

    far = lax.rem(k + zk, 2)
    target = z ^ (2 * far)
    is_near, is_far = far == 0, far == 1
    zo = 1 - zs

    class Weight:
        def __init__(self, src, src_quarter, piece, full, slab):
            self.src, self.src_quarter, self.piece, self.full, self.slab = src, src_quarter, piece, full, slab
            self.zsem, self.xsem = new_recv(4), new_recv(8)

        def push(self):
            sem = lambda: self.zsem + zs * 2 + k
            for j in (2, 1):
                send(self.src_quarter, lambda: self.piece(zs, k, dq), sem, lambda j=j: at(d, zk, z ^ j))
            send(self.src, lambda: self.full(zs, k), sem, mate, is_far)
            local(self.src, lambda: self.full(zs, k), self.zsem + zs * 2 + k, is_near)

        def spread(self, cs, cond):
            mine = lambda: self.slab(cs, dq)
            for j in (1, 2):
                send(mine, mine, lambda j=j: self.xsem + cs * 4 + j - 1, quad[j - 1], cond)

        def hop(self):
            for r in range(2):
                arrive(lambda: self.piece(zo, r, dq), self.zsem + zo * 2 + r, is_near)
                arrive(lambda: self.piece(zs, r, dq), self.zsem + zs * 2 + r, is_far)
                mine = lambda r=r: self.piece(zs, r, dq)
                send(mine, mine, lambda r=r: self.zsem + zs * 2 + r, lambda: at(d, k, z ^ 1), is_far)
            self.spread(zo, is_near)
            self.spread(zs, is_far)

        def forward(self):
            for r in range(2):
                arrive(lambda: self.piece(zo, r, dq), self.zsem + zo * 2 + r, is_far)
            self.spread(zo, is_far)

        def relay(self):
            for cs, cond in ((zs, is_far), (zo, True)):
                for j in (1, 2):
                    arrive(lambda: self.slab(cs, dq ^ j), self.xsem + cs * 4 + j - 1, cond)
                    half = lambda cs=cs, j=j: self.piece(cs, j - 1, dq ^ j)
                    send(half, half, lambda cs=cs, j=j: self.xsem + cs * 4 + 1 + j, quad[2 - j], cond)

        def ready(self):
            for r in range(2):
                arrive(lambda: self.full(zs, r), self.zsem + zs * 2 + r, is_near & (k != r))
                arrive_local(lambda: self.full(zs, r), self.zsem + zs * 2 + r, is_near & (k == r))
            for cs, cond in ((zs, is_far), (zo, True)):
                for j in (1, 2):
                    arrive(lambda: self.piece(cs, j - 1, dq ^ 3), self.xsem + cs * 4 + 1 + j, cond)

    q48, o48, f96, p192 = QR // QUAD, OR_ // QUAD, FR // QUAD, PR_ // QUAD

    def cols(r):
        return pl.ds(mo(r * DH, 128), DH)

    w_qkv = Weight(
        lambda: wq_in,
        lambda: wq_in.at[:, pl.ds(mo(dq * q48, 16), q48), :],
        lambda cs, r, q: WQ.at[:, pl.ds(mo(cs * QR + q * q48, 16), q48), cols(r)],
        lambda cs, r: WQ.at[:, pl.ds(mo(cs * QR, 16), QR), cols(r)],
        lambda cs, q: WQ.at[:, pl.ds(mo(cs * QR + q * q48, 16), q48), :],
    )
    w_out = Weight(
        lambda: wo_in,
        lambda: wo_in.at[pl.ds(mo(dq * o48, 16), o48), :],
        lambda cs, r, q: WO.at[pl.ds(mo(cs * OR_ + q * o48, 16), o48), cols(r)],
        lambda cs, r: WO.at[pl.ds(mo(cs * OR_, 16), OR_), cols(r)],
        lambda cs, q: WO.at[pl.ds(mo(cs * OR_ + q * o48, 16), o48), :],
    )
    FC = wf_in.shape[1]

    def fc_part(at0, n):
        return Weight(
            lambda: wf_in.at[:, pl.ds(at0, n)],
            lambda: wf_in.at[pl.ds(mo(dq * f96, 16), f96), pl.ds(at0, n)],
            lambda cs, r, q: WF.at[r, pl.ds(mo(q * f96, 16), f96), pl.ds(mo(cs * FC + at0, 128), n)],
            lambda cs, r: WF.at[r, :, pl.ds(mo(cs * FC + at0, 128), n)],
            lambda cs, q: WF.at[:, pl.ds(mo(q * f96, 16), f96), pl.ds(mo(cs * FC + at0, 128), n)],
        )

    def proj_part(at0, n):
        n4 = n // QUAD
        return Weight(
            lambda: wp_in.at[pl.ds(at0, n), :],
            lambda: wp_in.at[pl.ds(mo(at0 + dq * n4, 16), n4), :],
            lambda cs, r, q: WP.at[pl.ds(mo(cs * PR_ + at0 + q * n4, 16), n4), cols(r)],
            lambda cs, r: WP.at[pl.ds(mo(cs * PR_ + at0, 16), n), cols(r)],
            lambda cs, q: WP.at[pl.ds(mo(cs * PR_ + at0 + q * n4, 16), n4), :],
        )

    first = FC // 3
    w_fc, w_fc2 = fc_part(0, first), fc_part(first, FC - first)
    w_proj, w_proj2 = proj_part(0, first), proj_part(first, FC - first)

    stage = new_recv(2)
    pltpu.make_async_copy(x_in, H, rs.at[stage]).start()
    pltpu.make_async_copy(cot_in, ACC, rs.at[stage + 1]).start()
    bq, bv = bqv_in[0:1, :], bqv_in[1:2, :]
    gap = jnp.zeros_like(bq)
    misc_in[...] = jnp.concatenate(
        [
            bfc_in[...].reshape(1, D),
            jnp.where(zs == 0, jnp.concatenate([bq, gap, bv, gap], axis=1), jnp.concatenate([gap, bq, gap, bv], axis=1)),
            jnp.full((1, D), len_in[0].astype(F32)),
            jnp.full((1, D), len_in[1].astype(F32)),
            jnp.zeros((4, D), F32),
        ],
        axis=0,
    )
    misc_sem = new_recv(8)
    for dev in line:
        send(lambda: misc_in, lambda: MISC.at[k, z], misc_sem + k * 4 + z, dev)
    local(lambda: misc_in, lambda: MISC.at[k, z], misc_sem + k * 4 + z)
    w_qkv.push()
    pltpu.make_async_copy(x_in, H, rs.at[stage]).wait()
    XS[...] = H[...].astype(BF)
    half_rows = T // 2
    xh_sem, x_sem = new_recv(1), new_recv(4)
    part_of = lambda core: pl.ds(mo(core * half_rows, 16), half_rows)
    send(lambda: XS.at[:, part_of(1 - k)], lambda: XH, xh_sem, mate)
    for i in range(2):
        mine = is_near & (zs == i)
        src, dst = lambda i=i: XS.at[i, part_of(k)], lambda: XR.at[zs, part_of(k)]
        send(src, dst, x_sem + zs * 2 + k, at(d, zk, 2 * k + i), jnp.logical_not(mine))
        local(src, dst, x_sem + zs * 2 + k, mine)
    pltpu.make_async_copy(cot_in, ACC, rs.at[stage + 1]).wait()
    CS[...] = ACC[...].astype(BF)

    V8[...] = jnp.zeros_like(V8)
    SQ[...] = jnp.zeros_like(SQ)

    b_out, ln1_g, ln1_b, ln2_g, ln2_b, b_proj = (
        v[...].reshape(1, D) for v in (b_out, ln1_g, ln1_b, ln2_g, ln2_b, b_proj)
    )

    w_qkv.hop()
    arrive(lambda: XH, xh_sem)
    for i in range(2):
        send(lambda i=i: XH.at[i], dst, x_sem + zs * 2 + k, at(d, zk, 2 * (1 - k) + i))
    w_qkv.forward()
    w_qkv.relay()

    RB = 256
    a1_sem = new_recv(2)

    def rows_of(base, i, n):
        return pl.ds(mo(base + i * n, 16), n)

    for s in range(2):
        for core in range(2):
            here = is_near & (zs == s) & (k == core)
            arrive(lambda: XR.at[s, part_of(core)], x_sem + s * 2 + core, jnp.logical_not(here))
            arrive_local(lambda: XR.at[s, part_of(core)], x_sem + s * 2 + core, here)

        def first_norm(i, c):
            scaled, _ = norm_stats(XR[s, rows_of(0, i, RB), :].astype(F32))
            A1[rows_of(own + s * T, i, RB), :] = (scaled * ln1_g + ln1_b).astype(BF)
            return c

        lax.fori_loop(0, T // RB, first_norm, 0)
        mine = lambda s=s: A1.at[pl.ds(mo(own + s * T, 16), T), :]
        send(mine, mine, a1_sem + s, mate)

    for r in range(2):
        for c in range(4):
            here = (k == r) & (z == c)
            arrive(lambda: MISC.at[r, c], misc_sem + r * 4 + c, jnp.logical_not(here))
            arrive_local(lambda: MISC.at[r, c], misc_sem + r * 4 + c, here)
    pair_misc = MISC[0, 2 * k] + MISC[0, 2 * k + 1]
    bias_q, bias_v = pair_misc[1:2, :HC], pair_misc[1:2, HC:]
    length = MISC[zk, 0, pl.ds(2 + zs, 1), :][:, 0:1]

    w_qkv.ready()

    def project(base):
        rows = pl.ds(mo(base, 16), 2 * T)
        a = A1[rows, :]
        QKV[0, rows, :] = ((dot_t(a, WQ[0]) + bias_q).astype(BF).astype(F32) * (HEAD_DIM**-0.5)).astype(BF)
        QKV[1, rows, :] = dot_t(a, WQ[1]).astype(BF)
        QKV[2, rows, :] = (dot_t(a, WQ[2]) + bias_v).astype(BF)

    project(own)
    for s in range(2):
        arrive(lambda: A1.at[pl.ds(mo(other + s * T, 16), T), :], a1_sem + s)
    w_out.push()
    w_fc.push()
    project(other)

    key_place = lax.broadcasted_iota(jnp.int32, (L, 128), 0).astype(F32)
    KB[...] = jnp.where(key_place < length, 0.0, MASKED)

    QB = T
    NQ = L // QB
    low_lane = lax.broadcasted_iota(jnp.int32, (1, 128), 1) < HEAD_DIM
    low_row = lax.broadcasted_iota(jnp.int32, (128, 1), 0) < HEAD_DIM
    diag = lax.broadcasted_iota(jnp.int32, (QB, QB), 0) <= lax.broadcasted_iota(jnp.int32, (QB, QB), 1)

    def keep_lane(v, h):
        return jnp.where(low_lane if h == 0 else jnp.logical_not(low_lane), v, jnp.zeros_like(v))

    def scores_t(kp, qm, qb):
        kv = (qb + 1) * QB
        s = dot_t(kp[:kv], qm)
        kb = KB[0:kv, :]
        s = s + jnp.concatenate([kb] * (QB // 128), axis=1)
        last = jnp.where(diag, s[kv - QB :], MASKED)
        if qb == 0:
            return last
        return jnp.concatenate([s[: kv - QB], last], axis=0)

    def send_cot():
        return line_send(lambda i: CS.at[i], lambda i: GF.at[pl.ds(mo(z * T, 16), T), :])

    between = {
        (0, 3): (w_out.hop, w_fc2.push),
        (1, 0): (w_fc.hop, w_proj.push),
        (1, 2): (w_out.forward,),
        (1, 3): (w_fc.forward, w_fc2.hop, w_proj2.push),
        (2, 0): (w_out.relay, w_proj.hop),
        (2, 2): (w_fc.relay,),
        (2, 3): (w_fc2.forward,),
    }

    def attend(p, c):
        lanes = pl.ds(mo(p * 128, 128), 128)
        kp, vp = QKV[1, :, lanes], QKV[2, :, lanes]
        vt = vp.T
        for qb in range(NQ):
            for (step, at_qb), work in between.items():
                if at_qb == qb:

                    @pl.when(p == step)
                    def _():
                        for do in work:
                            do()

            kv = (qb + 1) * QB
            qp = QKV[0, qb * QB : kv, lanes]
            parts = []
            for h in range(2):
                s = scores_t(kp, keep_lane(qp, h), qb)
                top = jnp.max(s, axis=0, keepdims=True)
                e = jnp.exp(s - top)
                total = jnp.sum(e, axis=0, keepdims=True)
                LSE[pl.ds(2 * p + h, 1), qb * QB : kv] = top + jnp.log(total)
                parts.append(dot(vt[:, :kv], e.astype(BF)) / total)
            CTX[qb * QB : kv, lanes] = jnp.where(low_row, parts[0], parts[1]).T.astype(BF)
        return c

    lax.fori_loop(0, HC // 128, attend, 0)
    w_proj2.hop()
    cot_sem = send_cot()
    sent = len(pending)

    def split_other(n, product):
        base = new_recv(2)
        PS[n] = product(pl.ds(mo(other, 16), 2 * T)).astype(BF).reshape(2, T, D)
        for s in range(2):
            send(lambda s=s: PS.at[n, s], lambda s=s: PR.at[n, s], base + s, mate)
        return base

    def split_own(product):
        ACC[...] = product(pl.ds(mo(own, 16), 2 * T)).reshape(2, T, D)

    def split_sum(n, product):
        base = split_other(n, product)
        split_own(product)
        return base

    def split_wait(n, base, s):
        arrive(lambda: PR.at[n, s], base + s)

    w_out.ready()
    ex = split_sum(0, lambda rows: dot(CTX[rows, :], WO[...]))
    w_proj.forward()
    a2_sem = new_recv(2)
    for s in range(2):
        split_wait(0, ex, s)

        def second_norm(i, c):
            rows = rows_of(0, i, RB)
            h = XR[s, rows, :].astype(F32) + ACC[s, rows, :] + PR[0, s, rows, :].astype(F32) + b_out
            H[s, rows, :] = h
            scaled, _ = norm_stats(h)
            A2[rows_of(own + s * T, i, RB), :] = (scaled * ln2_g + ln2_b).astype(BF)
            return c

        lax.fori_loop(0, T // RB, second_norm, 0)
        mine = lambda s=s: A2.at[pl.ds(mo(own + s * T, 16), T), :]
        send(mine, mine, a2_sem + s, mate)

    VF[...] = jnp.concatenate([MISC[0, 2 * k, 0:1, :], MISC[0, 2 * k + 1, 0:1, :]], axis=1)

    def hidden(base, start, width):
        rows = pl.ds(mo(base, 16), 2 * T)

        def body(i, c):
            cs = pl.ds(mo(i * FC + start, 128), width)
            u = dot(A2[rows, :], WF[:, :, cs].reshape(D, width)) + VF[:, cs]
            t = jnp.tanh(GELU_C * (u + GELU_A * u * u * u))
            M[rows, cs] = (0.5 * u * (1.0 + t)).astype(BF)
            SL[rows, cs] = (
                0.5 * (1.0 + t) + 0.5 * u * (1.0 - t * t) * GELU_C * (1.0 + 3.0 * GELU_A * u * u)
            ).astype(BF)
            return c

        lax.fori_loop(0, 2, body, 0)

    w_fc.ready()
    hidden(own, 0, first)
    w_fc2.relay()
    for s in range(2):
        arrive(lambda: A2.at[pl.ds(mo(other + s * T, 16), T), :], a2_sem + s)
    hidden(other, 0, first)
    w_proj2.forward()
    w_proj.relay()
    w_fc2.ready()
    hidden(own, first, FC - first)
    w_proj2.relay()
    hidden(other, first, FC - first)
    gf_sem = new_recv(2)
    for s in range(2):
        line_wait(lambda i: GF.at[pl.ds(mo(own + i * T, 16), T), :], cot_sem, s)

        def mask_rows(i, c):
            rows = rows_of(own + s * T, i, RB)
            place = (lax.broadcasted_iota(jnp.int32, (RB, 1), 0) + (own + s * T + i * RB)).astype(F32)
            g = jnp.where(place < length, GF[rows, :].astype(F32), 0.0)
            GF[rows, :] = g.astype(BF)
            V8[V_BPROJ] += fold8(g)
            return c

        lax.fori_loop(0, T // RB, mask_rows, 0)
        mine = lambda s=s: GF.at[pl.ds(mo(own + s * T, 16), T), :]
        send(mine, mine, gf_sem + s, mate)

    w_proj.ready()
    w_proj2.ready()
    mlp_rows = lambda rows: dot(M[rows, :], WP[...])
    mlp_ex = split_other(1, mlp_rows)
    for s in range(2):
        arrive(lambda: GF.at[pl.ds(mo(other + s * T, 16), T), :], gf_sem + s)

    bit = (lax.rem(dq, 2), dq // 2)

    def wide_factors(count, width):
        return [jnp.concatenate([FAC[dq ^ j, 0:1, :]] * (width // 128), axis=1) for j in range(count)]

    class Part:
        def __init__(self, plane, S, B, U, Z, E, slab, piece, place):
            self.S, self.B, self.U, self.Z, self.E = S, B, U, Z, E
            self.slab, self.piece, self.place = slab, piece, place
            self.pair, self.zsem, self.end = new_recv(1), new_recv(2), new_recv(4)
            self.setup(*plane)

        def pass_on(self):
            send(lambda: self.slab(1 - zs), lambda: self.B, self.pair, at(d, k, z ^ 1))

        def middle(self):
            arrive(lambda: self.B, self.pair)
            self.U[...] = (self.slab(zs)[...].astype(F32) + self.B[...].astype(F32)).astype(BF)
            for r in range(2):
                mine = (far == 0) & (r == k)
                piece = lambda r=r: self.piece(r)
                send(piece, lambda: self.Z.at[far], self.zsem + far, at(d, r, target), jnp.logical_not(mine))
                local(piece, lambda: self.Z.at[far], self.zsem + far, mine)

        def finish(self):
            arrive(lambda: self.Z.at[0], self.zsem, is_far)
            arrive_local(lambda: self.Z.at[0], self.zsem, is_near)
            arrive(lambda: self.Z.at[1], self.zsem + 1)
            self.E[...] = (self.Z[0].astype(F32) + self.Z[1].astype(F32)).astype(BF)
            for j in (1, 2, 3):
                send(lambda: self.E, lambda: self.place(dq), self.end + j, quad[j - 1])
            local(lambda: self.E, lambda: self.place(dq), self.end)

        def done(self):
            arrive_local(lambda: self.place(dq), self.end)
            for j in (1, 2, 3):
                arrive(lambda: self.place(dq ^ j), self.end + j)

    class DirectPart(Part):
        def setup(self, G, R):
            self.G, self.R, self.raw = G, R, new_recv(6)

        def quarter(self, q):
            return self.G.at[:, q // 2, lax.rem(q, 2)]

        def spread(self, a):
            for j in (1, 2, 3):
                send(
                    lambda j=j: self.G.at[a, (dq ^ j) // 2, lax.rem(dq ^ j, 2)],
                    lambda j=j: self.R.at[j - 1, a],
                    self.raw + 2 * j - 2 + a,
                    quad[j - 1],
                )

        def reduce(self):
            for j in (1, 2, 3):
                for a in range(2):
                    arrive(lambda: self.R.at[j - 1, a], self.raw + 2 * j - 2 + a)
            G, (_, n, width) = self.quarter(dq), self.S.shape
            factors, steps = wide_factors(QUAD, width), n // 16

            def add(i, c):
                a, rows = i // steps, pl.ds(mo(lax.rem(i, steps) * 16, 16), 16)
                v = G[a, rows, :].astype(F32) * factors[0]
                for j in (1, 2, 3):
                    v = v + self.R[j - 1, a, rows, :].astype(F32) * factors[j]
                self.S[a, rows, :] = v.astype(BF)
                return c

            lax.fori_loop(0, 2 * steps, add, 0)
            self.pass_on()

    class CrossPart(Part):
        def setup(self, G, X, O, Y):
            self.G, self.X, self.O, self.Y = G, X, O, Y
            self.raw, self.cross = new_recv(2), new_recv(2)

        def spread(self, cond=True):
            send(lambda: self.G.at[0, :, 1 - bit[0]], lambda: self.X.at[0], self.raw, quad[0], cond)
            send(lambda: self.G.at[1, 1 - bit[1]], lambda: self.X.at[1], self.raw + 1, quad[1], cond)

        def scale(self):
            _, n, width = self.S.shape
            factors = wide_factors(3, width)
            for a in range(2):
                arrive(lambda: self.X.at[a], self.raw + a)

                def add(i, c, a=a):
                    rows = pl.ds(mo(i * 16, 16), 16)
                    for b, to in ((bit[1 - a], self.S), (1 - bit[1 - a], self.O)):
                        mine = self.G[0, b, bit[0], rows, :] if a == 0 else self.G[1, bit[1], b, rows, :]
                        v = mine.astype(F32) * factors[0] + self.X[a, b, rows, :].astype(F32) * factors[1 + a]
                        to[a, rows, :] = v.astype(BF)
                    return c

                lax.fori_loop(0, n // 16, add, 0)
                send(lambda a=a: self.O.at[a], lambda a=a: self.Y.at[a], self.cross + a, quad[1 - a])

        def reduce(self):
            for a in range(2):
                arrive(lambda: self.Y.at[a], self.cross + a)
            self.S[...] = (self.S[...].astype(F32) + self.Y[...].astype(F32)).astype(BF)
            self.pass_on()

    g_proj = DirectPart(
        (GWP, RP), SPW, BP, UP, ZP, EP,
        lambda cs: SPW.at[cs],
        lambda r: UP.at[:, cols(r)],
        lambda q: gp_out.at[pl.ds(mo(q * p192, 16), p192), :],
    )
    g_out = CrossPart(
        (GWO, XO, OO, YO), SOW, BO, UO, ZO, EO,
        lambda cs: SOW.at[cs],
        lambda r: UO.at[:, cols(r)],
        lambda q: go_out.at[pl.ds(mo(q * o48, 16), o48), :],
    )

    def fc_grad(plane, S, B, U, Z, E, start, n):
        return CrossPart(
            plane, S, B, U, Z, E,
            lambda cs: S.at[:, :, pl.ds(mo(cs * FC, 128), FC)],
            lambda r: U.at[r],
            lambda q: gf_out.at[pl.ds(mo(start + q * n, 16), n), :],
        )

    g_fc2 = fc_grad((GWF, XF, OF, YF), SFW, BF1, UF, ZF, EF, 0, 128 // QUAD)
    g_fc = fc_grad((GWF2, XF2, OF2, YF2), SFW2, BF2, UF2, ZF2, EF2, 128, (FR - 128) // QUAD)

    def qkv_grad(i):
        return CrossPart(
            [v.at[i] for v in (GWQ, XQ, OQ, YQ)],
            *(v.at[i] for v in (SQW, BQ, UQ, ZQ, EQ)),
            lambda cs: SQW.at[i, cs],
            lambda r: UQ.at[i, :, cols(r)],
            lambda q: gq_out.at[i, pl.ds(mo(q * q48, 16), q48), :],
        )

    g_qkv = [qkv_grad(i) for i in range(3)]

    def grad_proj(i, c):
        cs = pl.ds(mo(i * (FC // 2), 128), FC // 2)
        g = t_dot(M[:, cs], GF[...])
        SQ[...] += fold8(g * g)
        GWP[i // 2, lax.rem(i, 2)] = g.astype(BF).reshape(2, p192, D)
        return c

    for a in range(2):
        lax.fori_loop(2 * a, 2 * a + 2, grad_proj, 0)
        g_proj.spread(a)

    NB = 512
    NN = FH // NB

    def grad_hidden(i, c):
        rows = pl.ds(mo(i // NN * 2 * T, 16), 2 * T)
        cs = pl.ds(mo(lax.rem(i, NN) * NB, 128), NB)
        g = dot_t(GF[rows, :], WP[cs, :]) * SL[rows, cs].astype(F32)
        low = g.astype(BF)
        SL[rows, cs] = low
        VF[:, cs] = jnp.where(i < NN, 0.0, VF[:, cs]) + jnp.sum(low.astype(F32), axis=0, keepdims=True)
        return c

    lax.fori_loop(0, 2 * NN, grad_hidden, 0)
    ex = split_sum(2, lambda rows: dot_t(SL[rows, :], WF[...].reshape(D, FH)))

    ga_sem = new_recv(2)
    for s in range(2):
        split_wait(2, ex, s)

        def second_back(i, c):
            rows = rows_of(0, i, RB)
            full = rows_of(own + s * T, i, RB)
            up = ACC[s, rows, :] + PR[2, s, rows, :].astype(F32)
            scaled, inverse = norm_stats(H[s, rows, :])
            through = up * ln2_g
            V8[V_LN2G] += fold8(up * scaled)
            V8[V_LN2B] += fold8(up)
            g = GF[full, :].astype(F32) + inverse * (
                through
                - jnp.mean(through, axis=-1, keepdims=True)
                - scaled * jnp.mean(through * scaled, axis=-1, keepdims=True)
            )
            V8[V_BOUT] += fold8(g)
            HG[s, rows, :] = g
            GA[full, :] = g.astype(BF)
            return c

        lax.fori_loop(0, T // RB, second_back, 0)
        mine = lambda s=s: GA.at[pl.ds(mo(own + s * T, 16), T), :]
        send(mine, mine, ga_sem + s, mate)
    split_own(mlp_rows)
    flush(sent)
    LO, GI = CS, XS
    for s in range(2):
        split_wait(1, mlp_ex, s)

        def output_rows(i, c):
            rows = rows_of(0, i, RB)
            LO[s, rows, :] = (H[s, rows, :] + ACC[s, rows, :] + PR[1, s, rows, :].astype(F32) + b_proj).astype(BF)
            return c

        lax.fori_loop(0, T // RB, output_rows, 0)
    lo_sem = line_send(lambda i: LO.at[i], lambda i: lo_out.at[i])

    for s in range(2):
        arrive(lambda: GA.at[pl.ds(mo(other + s * T, 16), T), :], ga_sem + s)

    GCTX[...] = dot_t(GA[...], WO[...]).astype(BF)
    g = t_dot(CTX[...], GA[...])
    SQ[...] += fold8(g * g)
    GWO[...] = g.astype(BF).reshape(2, 2, 2, o48, D)
    g_out.spread()

    def grad_fc(G, start, n):
        g = t_dot(jnp.concatenate([A2[:, start : start + n], A2[:, FR + start : FR + start + n]], axis=1), SL[...])
        q = fold8(g * g)
        SQ[...] += q[:, :D] + q[:, D:]
        G[...] = g.astype(BF).reshape(2, 2, 2, n // QUAD, FH)

    grad_fc(GWF2, 128, FR - 128)
    g_fc.spread()

    def attend_back(p):
        lanes = pl.ds(mo(p * 128, 128), 128)
        kp, vp = QKV[1, :, lanes], QKV[2, :, lanes]
        kt = kp.T
        DK[...] = jnp.zeros_like(DK)
        DV[...] = jnp.zeros_like(DV)
        for qb in range(NQ):
            kv = (qb + 1) * QB
            qp = QKV[0, qb * QB : kv, lanes]
            do = GCTX[qb * QB : kv, lanes]
            dqt = []
            for h in range(2):
                qm, dm = keep_lane(qp, h), keep_lane(do, h)
                pt = jnp.exp(scores_t(kp, qm, qb) - LSE[pl.ds(2 * p + h, 1), qb * QB : kv])
                gp = dot_t(vp[:kv], dm)
                both = pt * gp
                gs = (both - pt * jnp.sum(both, axis=0, keepdims=True)).astype(BF)
                DV[0:kv, :] += dot(pt.astype(BF), dm)
                DK[0:kv, :] += dot(gs, qm)
                dqt.append(dot(kt[:, :kv], gs))
            GQKV[0, qb * QB : kv, lanes] = (
                jnp.where(low_row, dqt[0], dqt[1]).T * (HEAD_DIM**-0.5)
            ).astype(BF)
        GQKV[1, :, lanes] = DK[...].astype(BF)
        GQKV[2, :, lanes] = DV[...].astype(BF)

    def attend_back_step(p, c):
        attend_back(p)
        return c

    lax.fori_loop(0, HC // 128, attend_back_step, 0)

    def grad_norm_in(rows):
        return dot(GQKV[0, rows, :], WQ[0]) + dot(GQKV[1, rows, :], WQ[1]) + dot(GQKV[2, rows, :], WQ[2])

    ex = split_sum(3, grad_norm_in)
    grad_fc(GWF, 0, 128)
    g_fc2.spread(k == 0)
    for s in range(2):
        split_wait(3, ex, s)

        def first_back(i, c):
            rows = rows_of(0, i, RB)
            up = ACC[s, rows, :] + PR[3, s, rows, :].astype(F32)
            scaled, inverse = norm_stats(XR[s, rows, :].astype(F32))
            through = up * ln1_g
            V8[V_LN1G] += fold8(up * scaled)
            V8[V_LN1B] += fold8(up)
            g = HG[s, rows, :] + inverse * (
                through
                - jnp.mean(through, axis=-1, keepdims=True)
                - scaled * jnp.mean(through * scaled, axis=-1, keepdims=True)
            )
            GI[s, rows, :] = g.astype(BF)
            return c

        lax.fori_loop(0, T // RB, first_back, 0)

    batches = [pl.ds(0, T // 2), pl.ds(T // 2, T // 4), pl.ds(3 * T // 4, T // 4)]
    send_gi = lambda b: line_send(lambda i: GI.at[i, batches[b]], lambda i: gi_out.at[i, batches[b]])
    gi_sems = [send_gi(0)]

    def grad_qkv(i, c):
        g = t_dot(GQKV[i], A1[...])
        SQ[...] += fold8(g * g)
        GWQ[i] = g.astype(BF).reshape(2, 2, 2, q48, D)
        return c

    lax.fori_loop(0, 3, grad_qkv, 0)
    VK[k] = jnp.zeros(VK.shape[1:], F32)
    for i in range(6):
        VK[k, i : i + 1, :] = jnp.sum(V8[i], axis=0, keepdims=True)
    VK[k, V_BQV : V_BQV + 1, :] = jnp.concatenate(
        [jnp.sum(GQKV[i].astype(F32), axis=0, keepdims=True) for i in (0, 2)], axis=1
    )
    VK[k, V_BFC : V_BFC + 1, :] = VF[:, :D]
    VK[k, V_BFC + 1 : V_BFC + 2, :] = VF[:, D:]
    VK[k, V_SQ : V_SQ + 1, :] = jnp.sum(SQ[...], axis=0, keepdims=True)
    vk_sem = new_recv(1)
    send(lambda: VK.at[k], lambda: VK.at[k], vk_sem, mate)
    arrive(lambda: VK.at[1 - k], vk_sem)
    va, vb = VK[0], VK[1]
    pack = jnp.concatenate([va[0:6] + vb[0:6], va[6:9], vb[6:9]], axis=0)
    squares = jnp.sum(jnp.sum(pack * pack, axis=0, keepdims=True) + va[9:10] + vb[9:10], axis=1, keepdims=True)
    norm = jnp.sqrt(squares)
    factor = CLIP_BOUND / jnp.maximum(norm, CLIP_BOUND)
    FAC[dq] = jnp.broadcast_to(factor, (8, 128))
    fac_sem, vp_sem = new_recv(3), new_recv(3)
    for j in (1, 2, 3):
        for dev in (quad[j - 1], quad_mates[j - 1]):
            send(lambda: FAC.at[dq], lambda: FAC.at[dq], fac_sem + j - 1, dev, k == 1)
    VP[dq] = jnp.concatenate([pack, jnp.zeros((4, D), F32)], axis=0)
    for j in (1, 2, 3):
        arrive(lambda: FAC.at[dq ^ j], fac_sem + j - 1)

    order = [g_proj, g_out, g_fc, g_fc2, *g_qkv]
    g_proj.reduce()
    g_out.scale()
    g_fc.scale()
    g_fc2.spread(k == 1)
    for part in g_qkv:
        part.spread()
    for j in (1, 2, 3):
        send(lambda: VP.at[dq], lambda: VP.at[dq], vp_sem + j - 1, quad[j - 1])
    g_out.reduce()
    g_fc.reduce()
    g_proj.middle()
    g_out.middle()
    g_fc.middle()
    gi_sems.append(send_gi(1))
    for part in (g_fc2, *g_qkv):
        part.scale()
    g_proj.finish()
    g_fc2.reduce()
    for j in (1, 2, 3):
        arrive(lambda: VP.at[dq ^ j], vp_sem + j - 1)
    total = jnp.zeros((12, D), F32)
    for q in range(QUAD):
        total = total + VP[q, 0:12, :] * FAC[q, 0:1, 0:1]
    VZ[z] = jnp.concatenate([total, jnp.broadcast_to(norm, (4, D))], axis=0)
    vz_sem = new_recv(3)
    for j in (1, 2, 3):
        send(lambda: VZ.at[z], lambda: VZ.at[z], vz_sem + j - 1, at(d, k, z ^ j))
    for part in g_qkv:
        part.reduce()
    g_out.finish()
    g_fc.finish()
    g_fc2.middle()
    for part in g_qkv:
        part.middle()
    gi_sems.append(send_gi(2))
    g_fc2.finish()
    for part in g_qkv:
        part.finish()

    for j in (1, 2, 3):
        arrive(lambda: VZ.at[z ^ j], vz_sem + j - 1)
    total = VZ[0] + VZ[1] + VZ[2] + VZ[3]
    vec_out[0:6, :] = total[0:6]
    V8[0, 0:6, :] = total[6:12]
    vec_out[6:7, :] = V8[0, pl.ds(V_BFC - V_BQV + 3 * zk + zs, 1), :]
    pair = V8[0, pl.ds(3 * zk, 1), :]
    spare = jnp.zeros((1, D - QR), F32)
    for i in range(2):
        a, b = pair[:, i * HC : i * HC + QR], pair[:, i * HC + QR : (i + 1) * HC]
        vec_out[7 + i : 8 + i, :] = jnp.concatenate([jnp.where(zs == 0, a, b), spare], axis=1)
    first_place = lax.broadcasted_iota(jnp.int32, (1, D), 1) == 0
    vec_out[9:10, :] = jnp.where(
        first_place, VZ[2 * k, V_NORM : V_NORM + 1, :], VZ[2 * k + 1, V_NORM : V_NORM + 1, :]
    )
    vec_out[10:12, :] = jnp.zeros((2, D), F32)

    for part in order:
        part.done()
    for i in range(2):
        line_wait(lambda i: lo_out.at[i], lo_sem, i)
        for b in range(3):
            line_wait(lambda i: gi_out.at[i, batches[b]], gi_sems[b], i)
    flush(len(pending))


def widen(*refs):
    low, vec_in, wide, lines, b_qv, norms = refs[:6], refs[6], refs[7:13], refs[13:20], refs[20], refs[21]
    before, after, vec, rows, sems, line_sems = refs[22:28], refs[28:34], refs[34], refs[35:42], refs[42], refs[43]
    parts = []
    for i, v in enumerate(low):
        parts += [(i, (e,)) for e in range(2)] if i < 2 else [(i, (...,))]

    def load(n, i, at):
        return pltpu.make_async_copy(low[i].at[at], before[i].at[at], sems.at[2 * n])

    def store(n, i, at):
        return pltpu.make_async_copy(after[i].at[at], wide[i].at[at], sems.at[2 * n + 1])

    def store_line(i):
        return pltpu.make_async_copy(rows[i], lines[i], line_sems.at[i])

    load_vec = pltpu.make_async_copy(vec_in, vec, line_sems.at[7])
    for n, (i, at) in enumerate(parts):
        load(n, i, at).start()
    load_vec.start()
    for n, (i, at) in enumerate(parts):
        load(n, i, at).wait()
        after[i][at] = before[i][at].astype(F32)
        store(n, i, at).start()
    load_vec.wait()
    for i in range(7):
        rows[i][...] = vec[i, :]
        store_line(i).start()
    b_qv[...] = vec[7:9, : b_qv.shape[1]]
    norms[...] = vec[9, :2]
    for n, (i, at) in enumerate(parts):
        store(n, i, at).wait()
    for i in range(7):
        store_line(i).wait()


def shards(
    layer_in, w_qkv, b_qv, w_out, b_out, ln1_g, ln1_b, ln2_g, ln2_b, w_fc, b_fc, w_proj, b_proj, lengths, cotangent
):
    E, T, D = layer_in.shape
    n_col, n_row = lax.axis_size("col"), lax.axis_size("row")
    assert lax.axis_size("dp") == QUAD and n_col == 4 and n_row % 2 == 0
    pairs = n_row // 2
    r = lax.axis_index("row")
    core = lax.rem(r, 2)
    half_rows = w_fc.shape[0] * pairs

    def halves(w, axis):
        if pairs == 1:
            return w
        whole = lax.all_gather(w, "row", axis=axis, tiled=True)
        return lax.dynamic_slice_in_dim(whole, core * half_rows, half_rows, axis)

    w_qkv, w_out, w_fc, w_proj = halves(w_qkv, 0), halves(w_out, 1), halves(w_fc, 0), halves(w_proj, 1)
    L = T * n_col
    HQ = w_qkv.shape[2]
    HC = HQ * n_col // 2
    FQ = w_fc.shape[1]
    FH = FQ * n_col // 2
    DH = w_fc.shape[0]
    wq_t = jnp.transpose(w_qkv, (1, 2, 0))
    q48, o48, p192 = HQ // QUAD, HQ // QUAD, FQ // QUAD
    fa, fb = 128 // QUAD, (DH - 128) // QUAD

    anyspec = pl.BlockSpec(memory_space=pl.ANY)
    vm = pl.BlockSpec(memory_space=pltpu.VMEM)
    V = pltpu.VMEM
    outs = pl.pallas_call(
        kernel,
        name="layer",
        out_shape=(
            jax.ShapeDtypeStruct((E, T, D), BF),
            jax.ShapeDtypeStruct((E, T, D), BF),
            jax.ShapeDtypeStruct((3, HQ, DH), BF),
            jax.ShapeDtypeStruct((HQ, DH), BF),
            jax.ShapeDtypeStruct((DH, FQ), BF),
            jax.ShapeDtypeStruct((FQ, DH), BF),
            jax.ShapeDtypeStruct((12, D), F32),
        ),
        in_specs=[anyspec] * 6 + [vm, vm, pl.BlockSpec(memory_space=pltpu.SMEM)] + [vm] * 6,
        out_specs=(anyspec,) * 6 + (vm,),
        scratch_shapes=[
            V((2, T, D), BF),
            V((2, T // 2, D), BF),
            V((2, T, D), BF),
            V((8, D), F32),
            V((2, T, D), BF),
            V((2, T, D), F32),
            V((2, T, D), F32),
            V((L, D), BF),
            V((3, HC, D), BF),
            V((HC, D), BF),
            V((2, DH, FH), BF),
            V((FH, D), BF),
            V((2, n_col, 8, D), F32),
            V((3, L, HC), BF),
            V((L, HC), BF),
            V((8, L), F32),
            V((L, 128), F32),
            V((2, T, D), F32),
            V((4, 2, T, D), BF),
            V((4, 2, T, D), BF),
            V((L, D), BF),
            V((L, FH), BF),
            V((L, FH), BF),
            V((L, D), BF),
            V((L, D), BF),
            V((L, HC), BF),
            V((3, L, HC), BF),
            V((L, 128), F32),
            V((L, 128), F32),
            V((6, 8, D), F32),
            V((8, D), F32),
            V((1, FH), F32),
            V((2, 16, D), F32),
            V((QUAD, 8, 128), F32),
            V((QUAD, 16, D), F32),
            V((n_col, 16, D), F32),
            V((3, 2, 2, 2, q48, D), BF),
            V((2, 2, 2, o48, D), BF),
            V((2, 2, 2, fa, FH), BF),
            V((2, 2, 2, fb, FH), BF),
            V((2, 2, 2, p192, D), BF),
            V((3, 2, p192, D), BF),
            *[
                V(shape, BF)
                for shape in ((3, 2, 2, q48, D), (2, 2, o48, D), (2, 2, fa, FH), (2, 2, fb, FH))
            ],
            *[
                V(shape, BF)
                for _ in "OY"
                for shape in ((3, 2, q48, D), (2, o48, D), (2, fa, FH), (2, fb, FH))
            ],
            V((3, 2, q48, D), BF),
            V((2, o48, D), BF),
            V((2, fa, FH), BF),
            V((2, fb, FH), BF),
            V((2, p192, D), BF),
            *[
                V(shape, BF)
                for _ in "BU"
                for shape in ((3, q48, D), (o48, D), (2, fa, FQ), (2, fb, FQ), (p192, D))
            ],
            V((3, 2, q48, DH), BF),
            V((2, o48, DH), BF),
            V((2, fa, FQ), BF),
            V((2, fb, FQ), BF),
            V((2, p192, DH), BF),
            V((3, q48, DH), BF),
            V((o48, DH), BF),
            V((fa, FQ), BF),
            V((fb, FQ), BF),
            V((p192, DH), BF),
            pltpu.SemaphoreType.DMA((264,)),
            pltpu.SemaphoreType.DMA((264,)),
        ],
        compiler_params=pltpu.CompilerParams(
            collective_id=0, has_side_effects=True, vmem_limit_bytes=63 * 2**20
        ),
    )(
        layer_in, cotangent, wq_t, w_out, w_fc, w_proj, b_fc, b_qv, lengths,
        b_out, ln1_g, ln1_b, ln2_g, ln2_b, b_proj,
    )
    low, vec = outs[:6], outs[6]
    line = jax.ShapeDtypeStruct((D,), F32)
    outs = pl.pallas_call(
        widen,
        name="widen",
        out_shape=(
            *(jax.ShapeDtypeStruct(v.shape, F32) for v in low),
            *(line,) * 7,
            jax.ShapeDtypeStruct((2, HQ), F32),
            jax.ShapeDtypeStruct((2,), F32),
        ),
        in_specs=[anyspec] * 7,
        out_specs=(anyspec,) * 13 + (vm,) * 2,
        scratch_shapes=[
            *(V(v.shape, BF) for v in low),
            *(V(v.shape, F32) for v in (*low, vec)),
            *[V((D,), F32)] * 7,
            pltpu.SemaphoreType.DMA((16,)),
            pltpu.SemaphoreType.DMA((8,)),
        ],
        compiler_params=pltpu.CompilerParams(vmem_limit_bytes=63 * 2**20),
    )(*low, vec)
    lo, gi, gq, go, gf, gp = outs[:6]
    vec, norms = outs[6:14], outs[14]
    gq = jnp.transpose(gq, (2, 0, 1))
    if pairs > 1:
        groups = [[2 * p + q for p in range(pairs)] for q in range(2)]
        cores = [[2 * p, 2 * p + 1] for p in range(pairs)]
        gq, go, gf, gp, *vec = (
            lax.psum(v, "row", axis_index_groups=groups) for v in (gq, go, gf, gp, *vec)
        )

        def share(v, axis):
            whole = lax.all_gather(v, "row", axis=axis, tiled=True, axis_index_groups=cores)
            part = whole.shape[axis] // n_row
            return lax.dynamic_slice_in_dim(whole, r * part, part, axis)

        gq, go, gf, gp = share(gq, 0), share(go, 1), share(gf, 0), share(gp, 1)
    gb_out, g1, b1, g2, b2, gb_proj, gb_fc, gb_qv = vec
    return (lo, gi, norms, gq, gb_qv, go, gb_out, g1, b1, g2, b2, gf, gb_fc, gp, gb_proj)


def solution(mesh):
    in_specs = (
        P(("dp", "row"), "col", None),
        P("row", None, "col"),
        P(None, "col"),
        P("col", "row"),
        P(),
        P(),
        P(),
        P(),
        P(),
        P("row", "col"),
        P("col"),
        P("col", "row"),
        P(),
        P(("dp", "row")),
        P(("dp", "row"), "col", None),
    )
    out_specs = (
        P(("dp", "row"), "col", None),
        P(("dp", "row"), "col", None),
        P(("dp", "row")),
        P("row", None, "col"),
        P(None, "col"),
        P("col", "row"),
        P(),
        P(),
        P(),
        P(),
        P(),
        P("row", "col"),
        P("col"),
        P("col", "row"),
        P(),
    )
    return jax.shard_map(shards, mesh=mesh, in_specs=in_specs, out_specs=out_specs, check_vma=False)
```
